32 devices in a mesh: seq: 8 (over z, x), shard: 4 (over y, core).
Axes of the slice: x: 2, y: 2, z: 4, core: 2. Of those that a mesh axis runs over, the one named last changes fastest.
Arguments:
- tokens: bfloat16 [4, 2048, 2048], P('shard', 'seq'), may hold values from -6 to 6
- gain_one: float32 [2048], P('shard'), may hold values from 0.5 to 1.5
- in_weight: float32 [2048, 8192], P('shard'), may hold values from -0.125 to 0.125
- conv_weight: float32 [4, 4096], P(None, 'shard'), may hold values from -3 to 3
- conv_bias: float32 [4096], P('shard'), may hold values from -3 to 3
- x_weight: float32 [4096, 160], P('shard'), may hold values from -0.09375 to 0.09375
- dt_weight: float32 [128, 4096], P(None, 'shard'), may hold values from -0.5 to 0.5
- dt_bias: float32 [4096], P('shard'), may hold values from -6 to -3
- a_log: float32 [4096, 16], P('shard'), may hold values from -6.5 to 1
- skip_gain: float32 [4096], P('shard'), may hold values from 0.5 to 1.5
- out_weight: float32 [2048, 4096], P('shard'), may hold values from -0.09375 to 0.09375
- gain_two: float32 [2048], P('shard'), may hold values from 0.5 to 1.5
- ffn_in: float32 [2048, 16384], P('shard'), may hold values from -0.125 to 0.125
- ffn_down: float32 [2048, 8192], P('shard'), may hold values from -0.0625 to 0.0625
- cotangent: bfloat16 [4, 2048, 2048], P('shard', 'seq'), may hold values from -6 to 6
Outputs:
- output: bfloat16 [4, 2048, 2048], P('shard', 'seq')
- input_grad: bfloat16 [4, 2048, 2048], P('shard', 'seq')
- gain_one_grad: float32 [2048], P(('seq', 'shard'))
- in_weight_grad: float32 [2048, 8192], P(('seq', 'shard'))
- conv_weight_grad: float32 [4, 4096], P(None, ('seq', 'shard'))
- conv_bias_grad: float32 [4096], P(('seq', 'shard'))
- x_weight_grad: float32 [4096, 160], P(('seq', 'shard'))
- dt_weight_grad: float32 [128, 4096], P(None, ('seq', 'shard'))
- dt_bias_grad: float32 [4096], P(('seq', 'shard'))
- a_log_grad: float32 [4096, 16], P(('seq', 'shard'))
- skip_gain_grad: float32 [4096], P(('seq', 'shard'))
- out_weight_grad: float32 [2048, 4096], P(('seq', 'shard'))
- gain_two_grad: float32 [2048], P(('seq', 'shard'))
- ffn_in_grad: float32 [2048, 16384], P(('seq', 'shard'))
- ffn_down_grad: float32 [2048, 8192], P(('seq', 'shard'))
The draws below stay inside these ranges and needn't reach their ends.
All inputs are finite; a program needn't handle non-finite values.
Results may differ from the reference program's by a relative error of at most 0.012.
The reference program's roundings to bfloat16 on the way count: a program that leaves them out, or rounds other values in their place, can miss the bound.
Values may be sent and summed in bfloat16 or wider, within the bound.
No kernel may reach another device: no remote copies, remote signals or barrier semaphores. Data moves between devices by JAX's collectives and lax.ppermute only.
A program may use at most 960 MiB of HBM per device.

```python
import math
import jax
import jax.numpy as jnp
from jax import lax

D = 2048
E = 4096
N = 16
K = 4
R = 128
FF = 8192
SEQS = 4
LENGTH = 2048


def draw_a_log(key, part):
    key = jax.random.fold_in(key, 7)
    return jax.random.uniform(key, (E, N), jnp.float32, -5.5, 1.0)


def with_spikes(entries, own_key, source, target, shards_of, factor):
    def block_of(position):
        return (jnp.arange(entries.shape[position]) // (entries.shape[position] // shards_of)).reshape((-1,) + (1,) * (entries.ndim - 1 - position))

    one_side = jax.random.permutation(own_key, shards_of)[block_of(target)]
    second = (block_of(target) + shards_of // 2) % shards_of
    return jnp.where((block_of(source) == one_side) | (block_of(source) == second), factor * entries, entries)


def levels(rng, extent, cuts, low, largest):
    level, own = 1.0, jax.random.fold_in(rng, 6)
    for axis_at, parts in cuts:
        heights = jnp.exp(jax.random.uniform(jax.random.fold_in(own, axis_at), (parts,), jnp.float32, low / len(cuts), largest / len(cuts)))
        level = level * jnp.repeat(heights, extent[axis_at] // parts).reshape([-1 if axis == axis_at else 1 for axis in range(len(extent))])
    return level


def noise(key, extent, deviation, limit, cuts=(), dtype=jnp.bfloat16):
    loudness = levels(key, extent, cuts, -0.22, 0.18) if cuts else 1.0
    values = jax.random.normal(key, extent, jnp.float32) * deviation * loudness
    return jnp.minimum(jnp.maximum(values, -limit), limit).astype(dtype)


def noise_with(own_key, extent, width, most, cuts, heavy, dtype=jnp.bfloat16):
    values = width * jax.random.normal(own_key, extent, jnp.float32)
    if cuts:
        values = values * levels(own_key, extent, cuts, -0.22, 0.18)
    return jnp.clip(with_spikes(values, jax.random.fold_in(own_key, 3), *heavy), -most, most).astype(dtype)


def setup_inputs(seed: int = 0) -> dict:
    streams_of = jax.random.split(jax.random.key(seed), 16)
    return {
        "tokens": noise_with(streams_of[0], (SEQS, LENGTH, D), 1.0, 6.0, ((0, 4), (1, 8)), (1, 2, 8, 2.0)),
        "gain_one": jnp.clip(1.0 + 0.1 * jax.random.normal(streams_of[1], (D,), jnp.float32), 0.5, 1.5),
        "in_weight": noise(streams_of[2], (D, 2 * E), D ** -0.5, 0.125, ((0, 4),), jnp.float32),
        "conv_weight": noise(streams_of[3], (K, E), K ** -0.5, 3.0, ((1, 4),), jnp.float32),
        "conv_bias": noise(streams_of[4], (E,), 0.5, 3.0, ((0, 4),), jnp.float32),
        "x_weight": noise(streams_of[5], (E, R + 2 * N), E ** -0.5, 0.09375, ((0, 4),), jnp.float32),
        "dt_weight": noise(streams_of[6], (R, E), R ** -0.5, 0.5, ((1, 4),), jnp.float32),
        "dt_bias": jnp.clip(-6.0 + 3.0 * jax.random.uniform(streams_of[7], (E,), jnp.float32) ** levels(streams_of[7], (E,), ((0, 4),), -0.2, 0.2), -6.0, -3.0),
        "a_log": draw_a_log(jax.random.fold_in(streams_of[15], 71), 0),
        "skip_gain": jnp.clip(0.5 + 1.0 * jax.random.uniform(streams_of[9], (E,), jnp.float32) ** levels(streams_of[9], (E,), ((0, 4),), -0.2, 0.2), 0.5, 1.5),
        "out_weight": noise(streams_of[10], (D, E), E ** -0.5, 0.09375, ((0, 4),), jnp.float32),
        "gain_two": jnp.clip(1.0 + 0.1 * jax.random.normal(streams_of[11], (D,), jnp.float32), 0.5, 1.5),
        "ffn_in": noise(streams_of[12], (D, 2 * FF), D ** -0.5, 0.125, ((0, 4),), jnp.float32),
        "ffn_down": noise(streams_of[13], (D, FF), FF ** -0.5, 0.0625, ((0, 4),), jnp.float32),
        "cotangent": noise_with(streams_of[14], (SEQS, LENGTH, D), 1.0, 6.0, ((0, 4), (1, 8)), (1, 2, 8, 2.0)),
    }


epsilon = 1e-05

@jax.custom_vjp
def low(v):
    return lax.optimization_barrier(v.astype(jnp.bfloat16)).astype(jnp.float32)

@jax.custom_vjp
def low_back(v):
    return v

def low_keep(v):
    return (low(v), None)

def low_pass(kept, grad):
    return (grad,)

def back_keep(v):
    return (v, None)

def back_low(kept, grad):
    return (low(grad),)
low.defvjp(low_keep, low_pass)
low_back.defvjp(back_keep, back_low)

def matmul(left, right):
    return jnp.dot(left, right, precision=lax.Precision.HIGHEST, preferred_element_type=jnp.float32)

def rms_scale(values, gain):
    return values * lax.rsqrt(lax.optimization_barrier(jnp.mean(values * values, axis=-1, keepdims=True)) + epsilon) * gain

def conv_causal(conv_in, weight, bias):
    length = conv_in.shape[0]
    padded = jnp.concatenate([jnp.zeros((K - 1, conv_in.shape[1]), jnp.float32), conv_in], axis=0)
    total = bias + jnp.zeros_like(conv_in)
    for offset in range(K):
        total = total + weight[offset] * padded[offset:offset + length]
    return total

def selective_scan(rates, signal, b_rows, c_rows, a_matrix):
    length = rates.shape[0]
    span = math.gcd(length, 256)

    def block_run(a_values, state, pieces):

        def token_step(carry, row):
            rate_row, signal_row, b_row, c_row = row
            carry = jnp.exp(rate_row[:, None] * a_values) * carry + (rate_row * signal_row)[:, None] * b_row[None, :]
            return (carry, lax.optimization_barrier(jnp.sum(carry * c_row[None, :], axis=1)))
        return lax.scan(token_step, state, pieces)
    checked = jax.checkpoint(block_run)

    def outer_step(state, pieces):
        return checked(a_matrix, state, pieces)
    pieces = tuple((value.reshape(length // span, span, value.shape[1]) for value in (rates, signal, b_rows, c_rows)))
    _, outputs = lax.scan(outer_step, jnp.zeros(a_matrix.shape, jnp.float32), pieces)
    return outputs.reshape(length, rates.shape[1])

def forward(inputs, gain_one, in_weight, conv_weight, conv_bias, x_weight, dt_weight, dt_bias, a_log, skip_gain, out_weight, gain_two, ffn_in, ffn_down):
    normed = low(rms_scale(inputs, low(gain_one)))
    projected = low_back(matmul(normed, low(in_weight)))
    conv_in = low(projected[:, :E])
    gate_mix = projected[:, E:]
    conv_out = conv_causal(conv_in, low(conv_weight), low(conv_bias))
    signal = low(jax.nn.silu(conv_out))
    selection = low_back(matmul(signal, low(x_weight)))
    rank_part = low(selection[:, :R])
    b_rows = selection[:, R:R + N]
    c_rows = selection[:, R + N:]
    pre_rate = low_back(matmul(rank_part, low(dt_weight)))
    rates = jax.nn.softplus(pre_rate + low(dt_bias))
    a_matrix = -jnp.exp(low(a_log))
    scanned = selective_scan(rates, signal, b_rows, c_rows, a_matrix) + low(skip_gain) * signal
    gated = low(scanned * jax.nn.silu(gate_mix))
    middle = inputs + low_back(matmul(gated, low(out_weight).T))
    normed_two = low(rms_scale(middle, low(gain_two)))
    hidden = low_back(matmul(normed_two, low(ffn_in)))
    activated = low(jax.nn.silu(hidden[:, :FF]) * hidden[:, FF:])
    return middle + low_back(matmul(activated, low(ffn_down).T))

def reference(tokens, gain_one, in_weight, conv_weight, conv_bias, x_weight, dt_weight, dt_bias, a_log, skip_gain, out_weight, gain_two, ffn_in, ffn_down, cotangent):
    params = (gain_one, in_weight, conv_weight, conv_bias, x_weight, dt_weight, dt_bias, a_log, skip_gain, out_weight, gain_two, ffn_in, ffn_down)

    def one_sequence(totals, paired):
        sequence, upstream = paired
        result, pullback = jax.vjp(forward, sequence.astype(jnp.float32), *params)
        gradients = pullback(upstream.astype(jnp.float32))
        totals = tuple((summed + grad for summed, grad in zip(totals, gradients[1:])))
        return (totals, (result.astype(jnp.bfloat16), gradients[0].astype(jnp.bfloat16)))
    zeroes = tuple((jnp.zeros_like(weight) for weight in params))
    totals, (outputs, input_grads) = lax.scan(one_sequence, zeroes, (tokens, cotangent))
    return (outputs, input_grads, totals[0], totals[1], totals[2], totals[3], totals[4], totals[5], totals[6], totals[7], totals[8], totals[9], totals[10], totals[11], totals[12])
```

```python
import functools
import math

import jax
import jax.numpy as jnp
from jax import lax
from jax.experimental import pallas as pl
from jax.experimental.pallas import tpu as pltpu
from jax.sharding import PartitionSpec as P

D = 2048
E = 4096
N = 16
K = 4
R = 128
FF = 8192

LANES = 128
GROUP = 8

epsilon = 1e-05
log2_e = math.log2(math.e)
ln_2 = math.log(2.0)


def silu_slope(value):
    sigma = jax.nn.sigmoid(value)
    return sigma * (1.0 + value * (1.0 - sigma))


def dot_last(left, right):
    return lax.dot_general(
        left, right, (((1,), (1,)), ((), ())), preferred_element_type=jnp.float32
    )


def dot_first(left, right):
    return lax.dot_general(
        left, right, (((0,), (0,)), ((), ())), preferred_element_type=jnp.float32
    )


def dot_plain(left, right):
    return jnp.dot(left, right, preferred_element_type=jnp.float32)


def wide(value):
    return value.astype(jnp.float32)


def low(value):
    return value.astype(jnp.bfloat16)


def rounded(value):
    return lax.reduce_precision(value, 8, 7).astype(jnp.bfloat16)


def exchange(value, axis, mask):
    return lax.ppermute(value, axis, [(i, i ^ mask) for i in range(lax.axis_size(axis))])


def passed_along(value, axis, by):
    peers = lax.axis_size(axis)
    pairs = [(i, i + by) for i in range(peers) if 0 <= i + by < peers]
    return lax.ppermute(value, axis, pairs)


def masks_of(axis):
    size = lax.axis_size(axis)
    return [1 << bit for bit in range(size.bit_length() - 1)]


def gather_rows(value):
    parts = {0: value}
    for mask in reversed(masks_of("shard")):
        held = sorted(parts)
        got = exchange(jnp.concatenate([parts[k] for k in held], axis=0), "shard", mask)
        for place, k in enumerate(held):
            parts[k ^ mask] = got[place * value.shape[0] : (place + 1) * value.shape[0]]
    return jnp.concatenate([parts[k] for k in sorted(parts)], axis=0)


def scatter_rows(value, sent_type=jnp.bfloat16):
    shards = lax.axis_size("shard")
    rows = value.shape[0] // shards
    parts = {k: value[k * rows : (k + 1) * rows] for k in range(shards)}
    for mask in masks_of("shard"):
        sent = [k for k in sorted(parts) if k & mask]
        block = jnp.concatenate([parts[k] for k in sent], axis=0)
        if mask > 1:
            block = block.astype(sent_type)
        got = exchange(block, "shard", mask)
        for place, k in enumerate(sent):
            parts[k ^ mask] = parts[k ^ mask] + wide(got[place * rows : (place + 1) * rows])
            del parts[k]
    return parts[0]


def sum_columns(value):
    shards = lax.axis_size("shard")
    features = value.shape[0]
    for mask in masks_of("shard"):
        got = exchange(value, "shard", mask).reshape(features, shards // (2 * mask), 2, -1)
        value = value + jnp.concatenate([got[:, :, 1:], got[:, :, :1]], axis=2).reshape(
            value.shape
        )
    return value


def own_columns(weight, groups):
    shards, mine = lax.axis_size("shard"), lax.axis_index("shard")
    side = lax.axis_index("seq") & 1
    rows, width = weight.shape
    columns = width // (groups * shards)
    split = low(weight).reshape(rows, groups, shards, columns)

    def part(target):
        piece = lax.dynamic_index_in_dim(split, target, 2, keepdims=False)
        return piece.reshape(rows, groups * columns)

    whole = jnp.tile(part(mine), (shards, 1))
    half = rows // 2
    for k in range(1, shards):
        piece = part(mine ^ k)
        at = (mine ^ k) * rows
        if k == 1:
            whole = lax.dynamic_update_slice(whole, exchange(piece, "shard", k), (at, 0))
            continue
        sent = lax.dynamic_slice_in_dim(piece, side * half, half, axis=0)
        got = exchange(sent, "shard", k)
        other = exchange(got, "seq", 1)
        whole = lax.dynamic_update_slice(whole, got, (at + side * half, 0))
        whole = lax.dynamic_update_slice(whole, other, (at + (1 - side) * half, 0))
    return whole


def halve(value, bit, sent_type):
    mine = (lax.axis_index("seq") >> bit) & 1
    shaped = value.reshape((value.shape[0] // 2, 2) + value.shape[1:])
    sent = lax.dynamic_index_in_dim(shaped, 1 - mine, 1, keepdims=False).astype(sent_type)
    kept = lax.dynamic_index_in_dim(shaped, mine, 1, keepdims=False)
    return kept + wide(exchange(sent, "seq", 1 << bit))


def weight_grad(left, right):
    peers = lax.axis_size("seq")
    side = lax.axis_index("seq") & 1
    rows = left.shape[1] // peers
    split = left.reshape(left.shape[0], peers // 2, 2, rows)

    def half(which):
        piece = lax.dynamic_index_in_dim(split, which, 2, keepdims=False)
        return piece.reshape(left.shape[0], left.shape[1] // 2)

    sent = low(dot_first(half(1 - side), right))
    got = exchange(sent, "seq", 1)
    total = dot_first(half(side), right) + wide(got)
    total = total.reshape(peers // 2, rows, right.shape[1])
    for mask in masks_of("seq")[1:]:
        total = halve(total, mask.bit_length() - 1, jnp.bfloat16)
    return total.reshape(rows, right.shape[1])


def rows_of_columns(block, groups):
    shards, mine = lax.axis_size("shard"), lax.axis_index("shard")
    rows = block.shape[0] // shards
    columns = block.shape[1] // groups
    split = block.reshape(shards, rows, groups, 1, columns)

    def part(target):
        return lax.dynamic_index_in_dim(split, target, 0, keepdims=False)

    whole = jnp.broadcast_to(part(mine), (rows, groups, shards, columns))
    for k in range(1, shards):
        got = exchange(part(mine ^ k), "shard", k)
        whole = lax.dynamic_update_slice(whole, got, (0, 0, mine ^ k, 0))
    return whole.reshape(rows, groups * shards * columns)


def small_grads(value):
    peers, shards = lax.axis_size("seq"), lax.axis_size("shard")
    rows = value.shape[0] // peers
    total = value.reshape(peers, rows, value.shape[1])
    for mask in masks_of("seq"):
        total = halve(total, mask.bit_length() - 1, jnp.float32)
    total = total.reshape(rows, value.shape[1])
    pairs = [(s * shards + h, h * peers + s) for s in range(peers) for h in range(shards)]
    return lax.ppermute(total, ("seq", "shard"), pairs)


def gain_grad(value):
    peers, shards = lax.axis_size("seq"), lax.axis_size("shard")
    mine = lax.axis_index("seq") * shards + lax.axis_index("shard")
    value = value.reshape(peers * shards, -1)
    for axis, shift in (("seq", shards.bit_length() - 1), ("shard", 0)):
        for mask in masks_of(axis):
            bit = (mine >> (shift + mask.bit_length() - 1)) & 1
            inner = shards if axis == "seq" else 1
            shaped = value.reshape(value.shape[0] // (2 * inner), 2, inner, -1)
            sent = lax.dynamic_index_in_dim(shaped, 1 - bit, 1, keepdims=False)
            kept = lax.dynamic_index_in_dim(shaped, bit, 1, keepdims=False)
            total = kept + exchange(sent, axis, mask)
            value = total.reshape(value.shape[0] // 2, -1)
    return value.reshape(-1)


def spread(source, target, length):
    for c in range(source.shape[-1] // LANES):
        target[pl.ds(c * length, length), :] = wide(source[0, :, c * LANES : (c + 1) * LANES])


def collect(source, target, length):
    for c in range(target.shape[-1] // LANES):
        target[0, :, c * LANES : (c + 1) * LANES] = source[pl.ds(c * length, length), :]


def token_rows(ref, token, blocks, length):
    return ref[pl.ds(token, blocks, stride=length), :]


def sum_blocks(values):
    blocks = values[0].shape[0]
    if blocks != GROUP:
        return jnp.concatenate([jnp.sum(v, axis=0, keepdims=True) for v in values], axis=0)
    row = lax.broadcasted_iota(jnp.int32, (GROUP, LANES), 0)
    upper = row < 4
    level = [
        jnp.where(upper, values[j], values[j + 4])
        + pltpu.roll(jnp.where(upper, values[j + 4], values[j]), 4, 0)
        for j in range(4)
    ]
    for step in (2, 1):
        first = (row & step) == 0
        level = [
            jnp.where(
                first,
                level[j] + pltpu.roll(level[j], GROUP - step, 0),
                level[j + step] + pltpu.roll(level[j + step], step, 0),
            )
            for j in range(step)
        ]
    return level[0]


def end_kernel(length, blocks, rows_ref, rate_ref, signal_ref, a_ref, state_ref, total_ref, rate, signal):
    spread(rate_ref, rate, length)
    spread(signal_ref, signal, length)
    state_ref[...] = jnp.zeros_like(state_ref)

    def group(i, total):
        start = i * GROUP
        rates = [token_rows(rate, start + j, blocks, length) for j in range(GROUP)]
        drives = [
            rates[j] * token_rows(signal, start + j, blocks, length) for j in range(GROUP)
        ]
        for n in range(N):
            state, a = state_ref[0, n], a_ref[n]
            for j in range(GROUP):
                state = jnp.exp2(rates[j] * a) * state + drives[j] * rows_ref[0, 0, n * length + start + j]
            state_ref[0, n] = state
        for j in range(GROUP):
            total = total + rates[j]
        return total

    total_ref[0, 0] = lax.fori_loop(
        0, length // GROUP, group, jnp.zeros((blocks, LANES), jnp.float32)
    )


def scan_kernel(
    length, blocks, rows_ref, rate_ref, signal_ref, a_ref, in_ref, out_ref, state_ref, rate, signal, out
):
    spread(rate_ref, rate, length)
    spread(signal_ref, signal, length)
    state_ref[...] = in_ref[0]

    def group(i, carry):
        start = i * GROUP
        rates = [token_rows(rate, start + j, blocks, length) for j in range(GROUP)]
        drives = [
            rates[j] * token_rows(signal, start + j, blocks, length) for j in range(GROUP)
        ]
        outs = [None] * GROUP
        for n in range(N):
            state, a = state_ref[n], a_ref[n]
            for j in range(GROUP):
                state = jnp.exp2(rates[j] * a) * state + drives[j] * rows_ref[0, 0, n * length + start + j]
                term = state * rows_ref[0, 0, (N + n) * length + start + j]
                outs[j] = term if outs[j] is None else outs[j] + term
            state_ref[n] = state
        for j in range(GROUP):
            out[pl.ds(start + j, blocks, stride=length), :] = outs[j]
        return carry

    lax.fori_loop(0, length // GROUP, group, 0)
    collect(out, out_ref, length)


def seed_kernel(length, blocks, rows_ref, rate_ref, up_ref, a_ref, seed_ref, rate, up):
    spread(rate_ref, rate, length)
    spread(up_ref, up, length)
    seed_ref[...] = jnp.zeros_like(seed_ref)

    def group(i, carry):
        start = length - GROUP - i * GROUP
        rates = [token_rows(rate, start + j, blocks, length) for j in range(GROUP)]
        ups = [token_rows(up, start + j, blocks, length) for j in range(GROUP)]
        for n in range(N):
            back, a = seed_ref[0, n], a_ref[n]
            for j in reversed(range(GROUP)):
                back = jnp.exp2(rates[j] * a) * (
                    back + ups[j] * rows_ref[0, 0, (N + n) * length + start + j]
                )
            seed_ref[0, n] = back
        return carry

    lax.fori_loop(0, length // GROUP, group, 0)


def grad_kernel(
    length,
    blocks,
    rows_ref,
    rate_ref,
    signal_ref,
    up_ref,
    a_ref,
    in_ref,
    back_ref,
    rate_grad_ref,
    signal_grad_ref,
    rows_grad_ref,
    a_grad_ref,
    states,
    back_state,
    rate,
    signal,
    up,
    rate_grad,
    signal_grad,
):
    spread(rate_ref, rate, length)
    spread(signal_ref, signal, length)
    spread(up_ref, up, length)
    for n in range(N):
        states[n, 0] = in_ref[0, n]
    back_state[...] = back_ref[0]

    @pl.when(pl.program_id(0) == 0)
    def _():
        a_grad_ref[...] = jnp.zeros_like(a_grad_ref)

    def forward(i, carry):
        start = i * GROUP
        rates = [token_rows(rate, start + j, blocks, length) for j in range(GROUP)]
        drives = [
            rates[j] * token_rows(signal, start + j, blocks, length) for j in range(GROUP)
        ]
        for n in range(N):
            state, a = states[n, start], a_ref[n]
            for j in range(GROUP):
                state = jnp.exp2(rates[j] * a) * state + drives[j] * rows_ref[0, 0, n * length + start + j]
                states[n, start + j + 1] = state
        return carry

    lax.fori_loop(0, length // GROUP, forward, 0)

    def backward(i, carry):
        start = length - GROUP - i * GROUP
        rates = [token_rows(rate, start + j, blocks, length) for j in range(GROUP)]
        signals = [token_rows(signal, start + j, blocks, length) for j in range(GROUP)]
        ups = [token_rows(up, start + j, blocks, length) for j in range(GROUP)]
        through = [None] * GROUP
        slope = [None] * GROUP
        for n in range(N):
            back, a = back_state[n], a_ref[n]
            a_sum = None
            to_b = [None] * GROUP
            to_c = [None] * GROUP
            for j in reversed(range(GROUP)):
                b = rows_ref[0, 0, n * length + start + j]
                c = rows_ref[0, 0, (N + n) * length + start + j]
                here = back + ups[j] * c
                back = jnp.exp2(rates[j] * a) * here
                moved = back * states[n, start + j]
                a_term = moved * rates[j]
                a_sum = a_term if a_sum is None else a_sum + a_term
                b_term, a_slope = here * b, moved * a
                through[j] = b_term if through[j] is None else through[j] + b_term
                slope[j] = a_slope if slope[j] is None else slope[j] + a_slope
                to_b[j] = here * (rates[j] * signals[j])
                to_c[j] = ups[j] * states[n, start + j + 1]
            back_state[n] = back
            a_grad_ref[n] = a_grad_ref[n] + a_sum
            at = pl.ds(pl.multiple_of(start, GROUP), GROUP)
            rows_grad_ref[0, n, at, :] = sum_blocks(to_b)
            rows_grad_ref[0, N + n, at, :] = sum_blocks(to_c)
        for j in range(GROUP):
            rows = pl.ds(start + j, blocks, stride=length)
            rate_grad[rows, :] = through[j] * signals[j] + slope[j] * ln_2
            signal_grad[rows, :] = through[j] * rates[j]
        return carry

    lax.fori_loop(0, length // GROUP, backward, 0)
    collect(rate_grad, rate_grad_ref, length)
    collect(signal_grad, signal_grad_ref, length)


def scan_call(kernel, name, sequences, length, channels, inputs, outputs, scratch):
    blocks = channels // LANES
    kinds = {
        "rows": ((1, 1, 2 * N * length), lambda s: (s, 0, 0)),
        "tokens": ((1, length, channels), lambda s: (s, 0, 0)),
        "states": ((1, N, blocks, LANES), lambda s: (s, 0, 0, 0)),
        "total": ((1, 1, blocks, LANES), lambda s: (s, 0, 0, 0)),
        "fixed": ((N, blocks, LANES), lambda s: (0, 0, 0)),
        "rows_grad": ((1, 2 * N, length, LANES), lambda s: (s, 0, 0, 0)),
    }
    counts = {"fixed": None}

    def spec(kind):
        shape, index = kinds[kind]
        if kind == "rows":
            return pl.BlockSpec(shape, index, memory_space=pltpu.SMEM)
        return pl.BlockSpec(shape, index)

    def whole(kind):
        shape = kinds[kind][0]
        if kind != "fixed":
            shape = (sequences,) + shape[1:]
        return jax.ShapeDtypeStruct(shape, jnp.float32)

    def space(kind):
        if kind == "tokens":
            return pltpu.VMEM((blocks * length, LANES), jnp.float32)
        if kind == "history":
            return pltpu.VMEM((N, length + 1, blocks, LANES), jnp.float32)
        return pltpu.VMEM((N, blocks, LANES), jnp.float32)

    elements = sequences * length * channels
    return pl.pallas_call(
        functools.partial(kernel, length, blocks),
        name=name,
        grid=(sequences,),
        in_specs=[spec(kind) for kind, _ in inputs],
        out_specs=[spec(kind) for kind in outputs],
        out_shape=[whole(kind) for kind in outputs],
        scratch_shapes=[space(kind) for kind in scratch],
        compiler_params=pltpu.CompilerParams(vmem_limit_bytes=56 * 1024 * 1024),
        cost_estimate=pl.CostEstimate(
            flops=elements * N * 8 * len(inputs),
            bytes_accessed=elements * 4 * (len(inputs) + len(outputs)),
            transcendentals=elements * N,
        ),
    )(*[value for _, value in inputs])


def chained(total, state, a_scaled, direction):
    def join(first, second):
        return (
            first[0] + second[0],
            jnp.exp2(second[0] * a_scaled) * first[1] + second[1],
        )

    def moved(pair, by):
        packed = jnp.concatenate(pair, axis=1)
        got = passed_along(packed, "seq", direction * by)
        return (got[:, :1], got[:, 1:])

    pair = moved((total, state), 1)
    for mask in masks_of("seq"):
        pair = join(moved(pair, mask), pair)
    return pair[1]


def local(
    tokens,
    gain_one,
    in_weight,
    conv_weight,
    conv_bias,
    x_weight,
    dt_weight,
    dt_bias,
    a_log,
    skip_gain,
    out_weight,
    gain_two,
    ffn_in,
    ffn_down,
    cotangent,
):
    shards = lax.axis_size("shard")
    held, length, _ = tokens.shape
    sequences = held * shards
    own_rows = held * length
    row_count = sequences * length
    channels = conv_bias.shape[0]
    blocks = channels // LANES

    def by_sequence(value):
        return value.reshape(sequences, length, value.shape[-1])

    gains = lax.all_gather(rounded(jnp.stack([gain_one, gain_two])), "shard", axis=1, tiled=True)
    gain_norm, gain_second = wide(gains[0]), wide(gains[1])
    tokens_own = tokens.reshape(own_rows, D)
    up_own = cotangent.reshape(own_rows, D)
    tokens_all = gather_rows(tokens_own)
    weight_in = own_columns(in_weight, 2)
    weight_out = own_columns(out_weight, 1)
    up_all = gather_rows(up_own)
    weight_ffn = own_columns(ffn_in, 2)
    weight_down = own_columns(ffn_down, 1)

    conv_taps = wide(rounded(conv_weight))
    bias_conv = wide(rounded(conv_bias))
    weight_x = rounded(x_weight)
    weight_dt = rounded(dt_weight)
    bias_dt = wide(rounded(dt_bias))
    weight_skip = wide(rounded(skip_gain))
    a_matrix = -jnp.exp(wide(rounded(a_log)))
    a_scaled = (a_matrix * log2_e).T.reshape(N, blocks, LANES)

    inputs_all = wide(tokens_all)
    scale_all = lax.rsqrt(jnp.mean(inputs_all * inputs_all, axis=1, keepdims=True) + epsilon)
    normed = rounded(inputs_all * scale_all * gain_norm)
    projected = dot_plain(normed, weight_in)
    conv_in = by_sequence(rounded(projected[:, :channels]))
    gate_mix = projected[:, channels:]
    borrowed = passed_along(conv_in[:, length - (K - 1) :], "seq", 1)
    padded = wide(jnp.concatenate([borrowed, conv_in], axis=1))
    conv_out = bias_conv + jnp.zeros((sequences, length, channels), jnp.float32)
    for offset in range(K):
        conv_out = conv_out + conv_taps[offset] * padded[:, offset : offset + length]
    conv_out = conv_out.reshape(row_count, channels)
    signal = rounded(jax.nn.silu(conv_out))
    signal_wide = wide(signal)
    selection = sum_columns(
        lax.dot_general(
            weight_x, signal, (((0,), (1,)), ((), ())), preferred_element_type=jnp.float32
        )
    )
    rank_part = rounded(selection[:R])
    rows = jnp.swapaxes(selection[R:].reshape(2 * N, sequences, length), 0, 1).reshape(
        sequences, 1, 2 * N * length
    )
    pre_rate = dot_first(rank_part, weight_dt) + bias_dt
    rates = by_sequence(jax.nn.softplus(pre_rate))
    signals = by_sequence(signal)
    sizes = (sequences, length, channels)
    end_state, total_rate = scan_call(
        end_kernel,
        "scan_end",
        *sizes,
        [("rows", rows), ("tokens", rates), ("tokens", signals), ("fixed", a_scaled)],
        ["states", "total"],
        ["tokens", "tokens"],
    )
    incoming = chained(total_rate, end_state, a_scaled, 1)
    (scan_out,) = scan_call(
        scan_kernel,
        "scan_out",
        *sizes,
        [
            ("rows", rows),
            ("tokens", rates),
            ("tokens", signals),
            ("fixed", a_scaled),
            ("states", incoming),
        ],
        ["tokens"],
        ["fixed", "tokens", "tokens", "tokens"],
    )
    scanned = scan_out.reshape(row_count, channels) + weight_skip * signal_wide
    gate_act = jax.nn.silu(gate_mix)
    gated = rounded(scanned * gate_act)
    inputs = wide(tokens_own)
    middle = inputs + scatter_rows(dot_last(gated, weight_out), jnp.float32)

    scale_two = lax.rsqrt(jnp.mean(middle * middle, axis=1, keepdims=True) + epsilon)
    normed_two = gather_rows(rounded(middle * scale_two * gain_second))
    hidden = dot_plain(normed_two, weight_ffn)
    half_width = weight_ffn.shape[1] // 2
    gate_part = hidden[:, :half_width]
    up_part = hidden[:, half_width:]
    gate_silu = jax.nn.silu(gate_part)
    activated = rounded(gate_silu * up_part)
    act_grad = dot_plain(up_all, weight_down)
    hidden_grad = rounded(
        jnp.concatenate(
            [act_grad * up_part * silu_slope(gate_part), act_grad * gate_silu], axis=1
        )
    )
    normed_two_grad = scatter_rows(dot_last(hidden_grad, weight_ffn))
    result = middle + scatter_rows(dot_last(activated, weight_down))
    output = rounded(result).reshape(tokens.shape)
    ffn_down_result = rows_of_columns(weight_grad(up_all, activated), 1)
    ffn_in_result = rows_of_columns(weight_grad(normed_two, hidden_grad), 2)
    gain_two_grad = gain_grad(jnp.sum(normed_two_grad * middle * scale_two, axis=0))
    scaled_two = normed_two_grad * gain_second
    middle_grad = (
        wide(up_own)
        + scale_two * scaled_two
        - middle
        * (scale_two * scale_two * scale_two)
        * jnp.mean(scaled_two * middle, axis=1, keepdims=True)
    )
    mixed_grad = gather_rows(rounded(middle_grad))

    gated_grad = dot_plain(mixed_grad, weight_out)
    scan_grad = gated_grad * gate_act
    gate_grad = rounded(gated_grad * scanned * silu_slope(gate_mix))
    skip_grad = jnp.sum(scan_grad * signal_wide, axis=0)
    ups = by_sequence(scan_grad)
    (seed,) = scan_call(
        seed_kernel,
        "scan_seed",
        *sizes,
        [("rows", rows), ("tokens", rates), ("tokens", ups), ("fixed", a_scaled)],
        ["states"],
        ["tokens", "tokens"],
    )
    returning = chained(total_rate, seed, a_scaled, -1)
    out_result = rows_of_columns(weight_grad(mixed_grad, gated), 1)
    in_gate_result = weight_grad(normed, gate_grad)
    rate_grad, scan_signal_grad, rows_grad, a_grad = scan_call(
        grad_kernel,
        "scan_grad",
        *sizes,
        [
            ("rows", rows),
            ("tokens", rates),
            ("tokens", signals),
            ("tokens", ups),
            ("fixed", a_scaled),
            ("states", incoming),
            ("states", returning),
        ],
        ["tokens", "tokens", "rows_grad", "fixed"],
        ["history", "fixed", "tokens", "tokens", "tokens", "tokens", "tokens"],
    )
    rate_grad = rate_grad.reshape(row_count, channels)
    pre_grad = rate_grad * jax.nn.sigmoid(pre_rate)
    pre_grad_low = rounded(pre_grad)
    rank_grad = dot_last(weight_dt, pre_grad_low)
    rows_grad = jnp.swapaxes(jnp.sum(rows_grad, axis=3), 0, 1).reshape(2 * N, row_count)
    selection_grad = rounded(sum_columns(jnp.concatenate([rank_grad, rows_grad], axis=0)))
    signal_grad = (
        scan_grad * weight_skip
        + scan_signal_grad.reshape(row_count, channels)
        + lax.dot_general(
            selection_grad, weight_x, (((0,), (1,)), ((), ())), preferred_element_type=jnp.float32
        )
    )
    conv_grad = (signal_grad * silu_slope(conv_out)).reshape(sequences, length, channels)
    padded_grad = jnp.zeros((sequences, length + K - 1, channels), jnp.float32)
    for offset in range(K):
        padded_grad = padded_grad + jnp.pad(
            conv_taps[offset] * conv_grad, ((0, 0), (offset, K - 1 - offset), (0, 0))
        )
    returned = wide(passed_along(rounded(padded_grad[:, : K - 1]), "seq", -1))
    conv_in_grad = rounded(
        padded_grad[:, K - 1 :] + jnp.pad(returned, ((0, 0), (length - (K - 1), 0), (0, 0)))
    ).reshape(row_count, channels)
    in_conv_result = weight_grad(normed, conv_in_grad)
    normed_grad_part = dot_last(conv_in_grad, weight_in[:, :channels]) + dot_last(
        gate_grad, weight_in[:, channels:]
    )
    gain_one_grad = gain_grad(jnp.sum(normed_grad_part * inputs_all * scale_all, axis=0))
    normed_grad = scatter_rows(normed_grad_part)
    scale_one = scale_all[:own_rows]
    scaled_one = normed_grad * gain_norm
    input_grad = (
        middle_grad
        + scale_one * scaled_one
        - inputs
        * (scale_one * scale_one * scale_one)
        * jnp.mean(scaled_one * inputs, axis=1, keepdims=True)
    )

    conv_weight_grad = jnp.stack(
        [
            jnp.sum(conv_grad * padded[:, offset : offset + length], axis=(0, 1))
            for offset in range(K)
        ],
        axis=1,
    )
    column_sums = jnp.stack(
        [jnp.sum(conv_grad, axis=(0, 1)), jnp.sum(pre_grad, axis=0), skip_grad], axis=1
    )
    a_log_grad = a_grad.reshape(N, channels).T * a_matrix
    dt_weight_grad = lax.dot_general(
        pre_grad_low, rank_part, (((0,), (1,)), ((), ())), preferred_element_type=jnp.float32
    )
    x_weight_grad = lax.dot_general(
        signal, selection_grad, (((0,), (1,)), ((), ())), preferred_element_type=jnp.float32
    )
    small = small_grads(
        jnp.concatenate(
            [dt_weight_grad, x_weight_grad, a_log_grad, conv_weight_grad, column_sums], axis=1
        )
    )
    at = R + R + 2 * N
    in_result = rows_of_columns(jnp.concatenate([in_conv_result, in_gate_result], axis=1), 2)
    return (
        output,
        rounded(input_grad).reshape(tokens.shape),
        gain_one_grad,
        in_result,
        small[:, at + N : at + N + K].T,
        small[:, at + N + K],
        small[:, R:at],
        small[:, :R].T,
        small[:, at + N + K + 1],
        small[:, at : at + N],
        small[:, at + N + K + 2],
        out_result,
        gain_two_grad,
        ffn_in_result,
        ffn_down_result,
    )


def solution(mesh):
    in_specs = (
        P("shard", "seq", None),
        P("shard"),
        P("shard", None),
        P(None, "shard"),
        P("shard"),
        P("shard", None),
        P(None, "shard"),
        P("shard"),
        P("shard", None),
        P("shard"),
        P("shard", None),
        P("shard"),
        P("shard", None),
        P("shard", None),
        P("shard", "seq", None),
    )
    out_specs = (
        P("shard", "seq", None),
        P("shard", "seq", None),
        P(("seq", "shard")),
        P(("seq", "shard"), None),
        P(None, ("seq", "shard")),
        P(("seq", "shard")),
        P(("seq", "shard"), None),
        P(None, ("seq", "shard")),
        P(("seq", "shard")),
        P(("seq", "shard"), None),
        P(("seq", "shard")),
        P(("seq", "shard"), None),
        P(("seq", "shard")),
        P(("seq", "shard"), None),
        P(("seq", "shard"), None),
    )
    return jax.shard_map(local, mesh=mesh, in_specs=in_specs, out_specs=out_specs, check_vma=False)
```

```python
import functools
import math

import jax
import jax.numpy as jnp
from jax import lax
from jax.experimental import pallas as pl
from jax.experimental.pallas import tpu as pltpu
from jax.sharding import PartitionSpec as P

D = 2048
E = 4096
N = 16
K = 4
R = 128
FF = 8192

LANES = 128
GROUP = 8

epsilon = 1e-05
log2_e = math.log2(math.e)
ln_2 = math.log(2.0)


def silu_slope(value):
    sigma = jax.nn.sigmoid(value)
    return sigma * (1.0 + value * (1.0 - sigma))


def dot_last(left, right):
    return lax.dot_general(
        left, right, (((1,), (1,)), ((), ())), preferred_element_type=jnp.float32
    )


def dot_first(left, right):
    return lax.dot_general(
        left, right, (((0,), (0,)), ((), ())), preferred_element_type=jnp.float32
    )


def dot_plain(left, right):
    return jnp.dot(left, right, preferred_element_type=jnp.float32)


def wide(value):
    return value.astype(jnp.float32)


def low(value):
    return value.astype(jnp.bfloat16)


def rounded(value):
    return lax.reduce_precision(value, 8, 7).astype(jnp.bfloat16)


def exchange(value, axis, mask):
    return lax.ppermute(value, axis, [(i, i ^ mask) for i in range(lax.axis_size(axis))])


def passed_along(value, axis, by):
    peers = lax.axis_size(axis)
    pairs = [(i, i + by) for i in range(peers) if 0 <= i + by < peers]
    return lax.ppermute(value, axis, pairs)


def masks_of(axis):
    size = lax.axis_size(axis)
    return [1 << bit for bit in range(size.bit_length() - 1)]


def gather_rows(value):
    parts = {0: value}
    for mask in reversed(masks_of("shard")):
        held = sorted(parts)
        got = exchange(jnp.concatenate([parts[k] for k in held], axis=0), "shard", mask)
        for place, k in enumerate(held):
            parts[k ^ mask] = got[place * value.shape[0] : (place + 1) * value.shape[0]]
    return jnp.concatenate([parts[k] for k in sorted(parts)], axis=0)


def scatter_rows(make, sent_type=jnp.bfloat16):
    shards = lax.axis_size("shard")
    parts = {}
    for pair in reversed(range(0, shards, 2)):
        value = make(pair, pair + 2)
        rows = value.shape[0] // 2
        parts[pair] = value[:rows] + exchange(value[rows:], "shard", 1)
    for mask in masks_of("shard")[1:]:
        sent = [k for k in sorted(parts) if k & mask]
        block = jnp.concatenate([parts[k] for k in sent], axis=0).astype(sent_type)
        got = exchange(block, "shard", mask)
        for place, k in enumerate(sent):
            parts[k ^ mask] = parts[k ^ mask] + wide(got[place * rows : (place + 1) * rows])
            del parts[k]
    return parts[0]


def sum_columns(value):
    shards = lax.axis_size("shard")
    count = value.shape[1] // shards
    for mask in masks_of("shard"):
        got = exchange(value, "shard", mask)
        order = [k ^ mask for k in range(shards)]
        value = value + jnp.concatenate(
            [got[:, k * count : (k + 1) * count] for k in order], axis=1
        )
    return value


def tied(values, after):
    return lax.optimization_barrier((values, after))[0]


def assemble_kernel(plan, count, at_ref, *refs):
    pieces, outs, sems = refs[:count], refs[count:-1], refs[-1]
    copies = []
    for place, (piece, part, target, row, col, shape) in enumerate(plan):
        first = pl.multiple_of(at_ref[row], 16) if row is not None else 0
        left = pl.multiple_of(at_ref[col], LANES) if col is not None else 0
        copy = pltpu.make_async_copy(
            pieces[piece].at[:, pl.ds(part * shape[1], shape[1])],
            outs[target].at[pl.ds(first, shape[0]), pl.ds(left, shape[1])],
            sems.at[place],
        )
        copy.start()
        copies.append(copy)
    for copy in copies:
        copy.wait()


def assemble(pieces, plan, offsets, shapes):
    moved = sum(piece.size * piece.dtype.itemsize for piece in pieces)
    return pl.pallas_call(
        functools.partial(assemble_kernel, plan, len(pieces)),
        name="assemble",
        in_specs=[pl.BlockSpec(memory_space=pltpu.SMEM)]
        + [pl.BlockSpec(memory_space=pltpu.VMEM)] * len(pieces),
        out_specs=[pl.BlockSpec(memory_space=pl.ANY)] * len(shapes),
        out_shape=[jax.ShapeDtypeStruct(shape, pieces[0].dtype) for shape in shapes],
        scratch_shapes=[pltpu.SemaphoreType.DMA((len(plan),))],
        compiler_params=pltpu.CompilerParams(vmem_limit_bytes=48 * 1024 * 1024),
        cost_estimate=pl.CostEstimate(flops=0, bytes_accessed=2 * moved, transcendentals=0),
    )(jnp.stack(offsets).astype(jnp.int32), *pieces)


def recut(weight, groups, chosen, after=None):
    shards, mine = lax.axis_size("shard"), lax.axis_index("shard")
    side = lax.axis_index("seq") & 1
    rows, width = weight.shape
    columns = width // (groups * shards)
    half = rows // 2

    def part(target, first, count):
        return jnp.concatenate(
            [
                low(
                    lax.dynamic_slice(
                        weight, (first, (group * shards + target) * columns), (count, columns)
                    )
                )
                for group in chosen
            ],
            axis=1,
        )

    sent = [part(mine ^ 1, 0, rows)]
    sent += [part(mine ^ k, side * half, half) for k in range(2, shards)]
    if after is not None:
        sent = tied(sent, after)
    got = [exchange(piece, "shard", k + 1) for k, piece in enumerate(sent)]
    return part(mine, 0, rows), got


def second_half(got, after=None):
    far = got[1:] if after is None else tied(got[1:], after)
    return [exchange(piece, "seq", 1) for piece in far]


def recut_end(own, got, other, groups):
    shards, mine = lax.axis_size("shard"), lax.axis_index("shard")
    side = lax.axis_index("seq") & 1
    rows, width = own.shape
    half, columns = rows // 2, width // groups
    pieces = [own] + got + other
    offsets = [mine * rows, (mine ^ 1) * rows]
    offsets += [(mine ^ k) * rows + side * half for k in range(2, shards)]
    offsets += [(mine ^ k) * rows + (1 - side) * half for k in range(2, shards)]
    plan = [
        (place, group, group, place, None, (piece.shape[0], columns))
        for place, piece in enumerate(pieces)
        for group in range(groups)
    ]
    return assemble(pieces, plan, offsets, [(shards * rows, columns)] * groups)


def with_bit(blocks, bit):
    return [b for b in range(blocks) if not b >> bit & 1]


def halve(value, left, bit, sent_type):
    mine = (lax.axis_index("seq") >> bit) & 1
    inner = 1 << sorted(left).index(bit)
    blocks, rows, columns = value.shape
    shaped = value.reshape(blocks // (2 * inner), 2, inner * rows, columns)
    sent = lax.dynamic_index_in_dim(shaped, 1 - mine, 1, keepdims=False).astype(sent_type)
    kept = lax.dynamic_index_in_dim(shaped, mine, 1, keepdims=False)
    left.remove(bit)
    return sent, kept


class WeightGrad:
    def __init__(self, left, right, bits):
        self.left, self.right, self.bits = left, right, list(bits)
        self.remaining = list(bits)
        self.total = None

    def half(self, which, bit):
        peers = lax.axis_size("seq")
        rows = self.left.shape[1] // peers
        pieces = [
            lax.dynamic_slice_in_dim(self.left, (b + (which << bit)) * rows, rows, axis=1)
            for b in with_bit(peers, bit)
        ]
        return jnp.concatenate(pieces, axis=1)

    def ready(self, after=None):
        self.bit = self.bits.pop(0)
        if self.total is None:
            if after is not None:
                self.left, self.right = tied((self.left, self.right), after)
            mine = (lax.axis_index("seq") >> self.bit) & 1
            self.sent = low(dot_first(self.half(1 - mine, self.bit), self.right))
            self.kept_left = self.half(mine, self.bit)
            self.remaining.remove(self.bit)
        else:
            if after is not None:
                self.total = tied(self.total, after)
            self.sent, self.kept = halve(self.total, self.remaining, self.bit, jnp.bfloat16)
        return self

    def send(self, after=None):
        if after is not None:
            self.sent = tied(self.sent, after)
        self.got = exchange(self.sent, "seq", 1 << self.bit)
        return self

    def add(self, after=None):
        if after is not None:
            self.got = tied(self.got, after)
        rows = self.left.shape[1] // lax.axis_size("seq")
        columns = self.right.shape[1]
        if self.total is None:
            self.total = dot_first(self.kept_left, self.right) + wide(self.got)
            self.total = self.total.reshape(-1, rows, columns)
        else:
            self.total = (self.kept + wide(self.got).reshape(self.kept.shape)).reshape(
                -1, rows, columns
            )
        return self

    def step(self):
        return self.ready().send().add()

    def end(self):
        while self.bits:
            self.step()
        return self.total.reshape(self.total.shape[1:])


def rows_of_columns(blocks):
    shards, mine = lax.axis_size("shard"), lax.axis_index("shard")
    groups = len(blocks)
    rows = blocks[0].shape[0] // shards
    columns = blocks[0].shape[1]

    def part(target):
        return jnp.concatenate(
            [lax.dynamic_slice_in_dim(block, target * rows, rows, axis=0) for block in blocks],
            axis=1,
        )

    pieces = [part(mine)] + [exchange(part(mine ^ k), "shard", k) for k in range(1, shards)]
    offsets = [
        (group * shards + (mine ^ k)) * columns for k in range(shards) for group in range(groups)
    ]
    plan = [
        (k, group, 0, None, k * groups + group, (rows, columns))
        for k in range(shards)
        for group in range(groups)
    ]
    return assemble(pieces, plan, offsets, [(rows, groups * shards * columns)])[0]


def small_grads(value, gains):
    peers, shards = lax.axis_size("seq"), lax.axis_size("shard")
    rows = value.shape[0] // peers
    width = value.shape[1]
    packed = jnp.transpose(gains.reshape(2, peers, shards, -1), (1, 0, 3, 2))
    value = jnp.concatenate([value, packed.reshape(value.shape[0], shards)], axis=1)
    total = value.reshape(peers, rows, width + shards)
    left = [mask.bit_length() - 1 for mask in masks_of("seq")]
    for bit in list(left):
        sent, kept = halve(total, left, bit, jnp.float32)
        total = (kept + exchange(sent, "seq", 1 << bit)).reshape(-1, rows, width + shards)
    total = total.reshape(rows, width + shards)
    gain_sum = total[:, width:]
    for mask in masks_of("shard"):
        gain_sum = gain_sum + exchange(gain_sum, "shard", mask)
    gain_sum = lax.dynamic_index_in_dim(gain_sum, lax.axis_index("shard"), 1, keepdims=False)
    pairs = [(s * shards + h, h * peers + s) for s in range(peers) for h in range(shards)]
    return lax.ppermute(total[:, :width], ("seq", "shard"), pairs), gain_sum.reshape(2, -1)


def spread(source, target, length):
    for c in range(source.shape[-1] // LANES):
        target[pl.ds(c * length, length), :] = wide(source[0, :, c * LANES : (c + 1) * LANES])


def collect(source, target, length):
    for c in range(target.shape[-1] // LANES):
        target[0, :, c * LANES : (c + 1) * LANES] = source[pl.ds(c * length, length), :]


def token_rows(ref, token, blocks, length):
    return ref[pl.ds(token, blocks, stride=length), :]


def sum_blocks(values):
    blocks = values[0].shape[0]
    if blocks != GROUP:
        return jnp.concatenate([jnp.sum(v, axis=0, keepdims=True) for v in values], axis=0)
    row = lax.broadcasted_iota(jnp.int32, (GROUP, LANES), 0)
    upper = row < 4
    level = [
        jnp.where(upper, values[j], values[j + 4])
        + pltpu.roll(jnp.where(upper, values[j + 4], values[j]), 4, 0)
        for j in range(4)
    ]
    for step in (2, 1):
        first = (row & step) == 0
        level = [
            jnp.where(
                first,
                level[j] + pltpu.roll(level[j], GROUP - step, 0),
                level[j + step] + pltpu.roll(level[j + step], step, 0),
            )
            for j in range(step)
        ]
    return level[0]


def end_kernel(length, blocks, rows_ref, rate_ref, signal_ref, a_ref, state_ref, total_ref, rate, signal):
    spread(rate_ref, rate, length)
    spread(signal_ref, signal, length)
    state_ref[...] = jnp.zeros_like(state_ref)

    def group(i, total):
        start = i * GROUP
        rates = [token_rows(rate, start + j, blocks, length) for j in range(GROUP)]
        drives = [
            rates[j] * token_rows(signal, start + j, blocks, length) for j in range(GROUP)
        ]
        for n in range(N):
            state, a = state_ref[0, n], a_ref[n]
            for j in range(GROUP):
                state = jnp.exp2(rates[j] * a) * state + drives[j] * rows_ref[0, 0, n * length + start + j]
            state_ref[0, n] = state
        for j in range(GROUP):
            total = total + rates[j]
        return total

    total_ref[0, 0] = lax.fori_loop(
        0, length // GROUP, group, jnp.zeros((blocks, LANES), jnp.float32)
    )


def scan_kernel(
    length, blocks, rows_ref, rate_ref, signal_ref, a_ref, in_ref, out_ref, state_ref, rate, signal, out
):
    spread(rate_ref, rate, length)
    spread(signal_ref, signal, length)
    state_ref[...] = in_ref[0]

    def group(i, carry):
        start = i * GROUP
        rates = [token_rows(rate, start + j, blocks, length) for j in range(GROUP)]
        drives = [
            rates[j] * token_rows(signal, start + j, blocks, length) for j in range(GROUP)
        ]
        outs = [None] * GROUP
        for n in range(N):
            state, a = state_ref[n], a_ref[n]
            for j in range(GROUP):
                state = jnp.exp2(rates[j] * a) * state + drives[j] * rows_ref[0, 0, n * length + start + j]
                term = state * rows_ref[0, 0, (N + n) * length + start + j]
                outs[j] = term if outs[j] is None else outs[j] + term
            state_ref[n] = state
        for j in range(GROUP):
            out[pl.ds(start + j, blocks, stride=length), :] = outs[j]
        return carry

    lax.fori_loop(0, length // GROUP, group, 0)
    collect(out, out_ref, length)


def seed_kernel(length, blocks, rows_ref, rate_ref, up_ref, a_ref, seed_ref, rate, up):
    spread(rate_ref, rate, length)
    spread(up_ref, up, length)
    seed_ref[...] = jnp.zeros_like(seed_ref)

    def group(i, carry):
        start = length - GROUP - i * GROUP
        rates = [token_rows(rate, start + j, blocks, length) for j in range(GROUP)]
        ups = [token_rows(up, start + j, blocks, length) for j in range(GROUP)]
        for n in range(N):
            back, a = seed_ref[0, n], a_ref[n]
            for j in reversed(range(GROUP)):
                back = jnp.exp2(rates[j] * a) * (
                    back + ups[j] * rows_ref[0, 0, (N + n) * length + start + j]
                )
            seed_ref[0, n] = back
        return carry

    lax.fori_loop(0, length // GROUP, group, 0)


def grad_kernel(
    length,
    blocks,
    rows_ref,
    rate_ref,
    signal_ref,
    up_ref,
    a_ref,
    in_ref,
    back_ref,
    rate_grad_ref,
    signal_grad_ref,
    rows_grad_ref,
    a_grad_ref,
    states,
    back_state,
    rate,
    signal,
    up,
    rate_grad,
    signal_grad,
):
    spread(rate_ref, rate, length)
    spread(signal_ref, signal, length)
    spread(up_ref, up, length)
    for n in range(N):
        states[n, 0] = in_ref[0, n]
    back_state[...] = back_ref[0]

    @pl.when(pl.program_id(0) == 0)
    def _():
        a_grad_ref[...] = jnp.zeros_like(a_grad_ref)

    def forward(i, carry):
        start = i * GROUP
        rates = [token_rows(rate, start + j, blocks, length) for j in range(GROUP)]
        drives = [
            rates[j] * token_rows(signal, start + j, blocks, length) for j in range(GROUP)
        ]
        for n in range(N):
            state, a = states[n, start], a_ref[n]
            for j in range(GROUP):
                state = jnp.exp2(rates[j] * a) * state + drives[j] * rows_ref[0, 0, n * length + start + j]
                states[n, start + j + 1] = state
        return carry

    lax.fori_loop(0, length // GROUP, forward, 0)

    def backward(i, carry):
        start = length - GROUP - i * GROUP
        rates = [token_rows(rate, start + j, blocks, length) for j in range(GROUP)]
        signals = [token_rows(signal, start + j, blocks, length) for j in range(GROUP)]
        ups = [token_rows(up, start + j, blocks, length) for j in range(GROUP)]
        through = [None] * GROUP
        slope = [None] * GROUP
        for n in range(N):
            back, a = back_state[n], a_ref[n]
            a_sum = None
            to_b = [None] * GROUP
            to_c = [None] * GROUP
            for j in reversed(range(GROUP)):
                b = rows_ref[0, 0, n * length + start + j]
                c = rows_ref[0, 0, (N + n) * length + start + j]
                here = back + ups[j] * c
                back = jnp.exp2(rates[j] * a) * here
                moved = back * states[n, start + j]
                a_term = moved * rates[j]
                a_sum = a_term if a_sum is None else a_sum + a_term
                b_term, a_slope = here * b, moved * a
                through[j] = b_term if through[j] is None else through[j] + b_term
                slope[j] = a_slope if slope[j] is None else slope[j] + a_slope
                to_b[j] = here * (rates[j] * signals[j])
                to_c[j] = ups[j] * states[n, start + j + 1]
            back_state[n] = back
            a_grad_ref[n] = a_grad_ref[n] + a_sum
            at = pl.ds(pl.multiple_of(start, GROUP), GROUP)
            rows_grad_ref[0, n, at, :] = sum_blocks(to_b)
            rows_grad_ref[0, N + n, at, :] = sum_blocks(to_c)
        for j in range(GROUP):
            rows = pl.ds(start + j, blocks, stride=length)
            rate_grad[rows, :] = through[j] * signals[j] + slope[j] * ln_2
            signal_grad[rows, :] = through[j] * rates[j]
        return carry

    lax.fori_loop(0, length // GROUP, backward, 0)
    collect(rate_grad, rate_grad_ref, length)
    collect(signal_grad, signal_grad_ref, length)


def scan_call(kernel, name, work, sequences, length, channels, inputs, outputs, scratch, after=()):
    blocks = channels // LANES
    kinds = {
        "rows": ((1, 1, 2 * N * length), lambda s: (s, 0, 0)),
        "tokens": ((1, length, channels), lambda s: (s, 0, 0)),
        "states": ((1, N, blocks, LANES), lambda s: (s, 0, 0, 0)),
        "total": ((1, 1, blocks, LANES), lambda s: (s, 0, 0, 0)),
        "fixed": ((N, blocks, LANES), lambda s: (0, 0, 0)),
        "rows_grad": ((1, 2 * N, length, LANES), lambda s: (s, 0, 0, 0)),
    }
    def spec(kind):
        shape, index = kinds[kind]
        if kind == "rows":
            return pl.BlockSpec(shape, index, memory_space=pltpu.SMEM)
        return pl.BlockSpec(shape, index)

    def whole(kind):
        shape = kinds[kind][0]
        if kind != "fixed":
            shape = (sequences,) + shape[1:]
        return jax.ShapeDtypeStruct(shape, jnp.float32)

    def space(kind):
        if kind == "tokens":
            return pltpu.VMEM((blocks * length, LANES), jnp.float32)
        if kind == "history":
            return pltpu.VMEM((N, length + 1, blocks, LANES), jnp.float32)
        return pltpu.VMEM((N, blocks, LANES), jnp.float32)

    values = [value for _, value in inputs]
    values = tied(values, list(after))
    elements = sequences * length * channels
    return pl.pallas_call(
        functools.partial(kernel, length, blocks),
        name=name,
        grid=(sequences,),
        in_specs=[spec(kind) for kind, _ in inputs],
        out_specs=[spec(kind) for kind in outputs],
        out_shape=[whole(kind) for kind in outputs],
        scratch_shapes=[space(kind) for kind in scratch],
        compiler_params=pltpu.CompilerParams(vmem_limit_bytes=56 * 1024 * 1024),
        cost_estimate=pl.CostEstimate(
            flops=elements * N * work,
            bytes_accessed=elements * 4 * (len(inputs) + len(outputs)),
            transcendentals=elements * N,
        ),
    )(*values)


def chained(total, state, a_scaled, direction):
    peers = lax.axis_size("seq")
    second_of_pair = (lax.axis_index("seq") & 1) == (1 if direction == 1 else 0)

    def join(first, second):
        return (
            first[0] + second[0],
            jnp.exp2(second[0] * a_scaled) * first[1] + second[1],
        )

    def split(packed):
        return (packed[:, :1], packed[:, 1:])

    def chosen(flag, yes, no):
        return tuple(jnp.where(flag, a, b) for a, b in zip(yes, no))

    own = (total, state)
    mate = split(exchange(jnp.concatenate(own, axis=1), "seq", 1))
    first = chosen(second_of_pair, mate, own)
    pair = join(first, chosen(second_of_pair, own, mate))
    packed = jnp.concatenate(pair, axis=1)
    before = None
    for by in reversed(range(2, peers, 2)):
        got = split(passed_along(packed, "seq", direction * by))
        before = got if before is None else join(before, got)
    return jnp.where(second_of_pair, join(before, first)[1], before[1]), packed


def local(
    tokens,
    gain_one,
    in_weight,
    conv_weight,
    conv_bias,
    x_weight,
    dt_weight,
    dt_bias,
    a_log,
    skip_gain,
    out_weight,
    gain_two,
    ffn_in,
    ffn_down,
    cotangent,
):
    shards = lax.axis_size("shard")
    held, length, _ = tokens.shape
    sequences = held * shards
    own_rows = held * length
    row_count = sequences * length
    channels = conv_bias.shape[0]
    blocks = channels // LANES

    def by_sequence(value):
        return value.reshape(sequences, length, value.shape[-1])

    tokens_own = tokens.reshape(own_rows, D)
    up_own = cotangent.reshape(own_rows, D)
    gains_own = rounded(jnp.concatenate([gain_one, gain_two])).reshape(1, -1)
    gain_rows = jnp.pad(gains_own, ((0, 15), (0, D - gains_own.shape[1])))
    packed = gather_rows(jnp.concatenate([tokens_own, gain_rows], axis=0)).reshape(
        shards, own_rows + 16, D
    )
    tokens_all = packed[:, :own_rows].reshape(row_count, D)
    gains = packed[:, own_rows, : gains_own.shape[1]].reshape(shards, 2, -1)
    in_turn = [
        lax.dynamic_index_in_dim(gains, lax.axis_index("shard") ^ k, 0, keepdims=False)
        for k in range(shards)
    ]
    gains = wide(jnp.concatenate(in_turn, axis=1))
    gain_norm, gain_second = gains[0], gains[1]

    conv_own, conv_got = recut(in_weight, 2, [0])
    (weight_conv_in,) = recut_end(conv_own, conv_got, second_half(conv_got), 1)
    gate_own, gate_got = recut(in_weight, 2, [1], conv_got)
    out_own, out_got = recut(out_weight, 1, [0], conv_got)
    (weight_gate_in,) = recut_end(gate_own, gate_got, second_half(gate_got), 1)
    (weight_out,) = recut_end(out_own, out_got, second_half(out_got), 1)

    conv_taps = wide(rounded(conv_weight))
    bias_conv = wide(rounded(conv_bias))
    weight_x = rounded(x_weight)
    weight_dt = rounded(dt_weight)
    bias_dt = wide(rounded(dt_bias))
    weight_skip = wide(rounded(skip_gain))
    a_matrix = -jnp.exp(wide(rounded(a_log)))
    a_scaled = (a_matrix * log2_e).T.reshape(N, blocks, LANES)

    inputs_all = wide(tokens_all)
    scale_all = lax.rsqrt(jnp.mean(inputs_all * inputs_all, axis=1, keepdims=True) + epsilon)
    normed = rounded(inputs_all * scale_all * gain_norm)
    conv_in = by_sequence(rounded(dot_plain(normed, weight_conv_in)))
    gate_mix = dot_plain(normed, weight_gate_in)
    borrowed = passed_along(conv_in[:, length - (K - 1) :], "seq", 1)
    padded = wide(jnp.concatenate([borrowed, conv_in], axis=1))
    conv_out = bias_conv + jnp.zeros((sequences, length, channels), jnp.float32)
    for offset in range(K):
        conv_out = conv_out + conv_taps[offset] * padded[:, offset : offset + length]
    conv_out = conv_out.reshape(row_count, channels)
    signal = rounded(jax.nn.silu(conv_out))
    signal_wide = wide(signal)
    selection = sum_columns(
        lax.dot_general(
            weight_x, signal, (((0,), (1,)), ((), ())), preferred_element_type=jnp.float32
        )
    )
    ffn_own, ffn_got = recut(ffn_in, 2, [0, 1], selection)
    down_own, down_got = recut(ffn_down, 1, [0], ffn_got)
    rank_part = rounded(selection[:R])
    rows = jnp.swapaxes(selection[R:].reshape(2 * N, sequences, length), 0, 1).reshape(
        sequences, 1, 2 * N * length
    )
    pre_rate = dot_first(rank_part, weight_dt) + bias_dt
    rates = by_sequence(jax.nn.softplus(pre_rate))
    signals = by_sequence(signal)
    sizes = (sequences, length, channels)
    end_state, total_rate = scan_call(
        end_kernel,
        "scan_end",
        1370,
        *sizes,
        [("rows", rows), ("tokens", rates), ("tokens", signals), ("fixed", a_scaled)],
        ["states", "total"],
        ["tokens", "tokens"],
        out_got,
    )
    incoming, first_round = chained(total_rate, end_state, a_scaled, 1)
    ffn_other = second_half(ffn_got, first_round)
    (scan_out,) = scan_call(
        scan_kernel,
        "scan_out",
        1900,
        *sizes,
        [
            ("rows", rows),
            ("tokens", rates),
            ("tokens", signals),
            ("fixed", a_scaled),
            ("states", incoming),
        ],
        ["tokens"],
        ["fixed", "tokens", "tokens", "tokens"],
        [weight_gate_in, weight_out] + ffn_got + ffn_other[:1],
    )
    scan_out = tied(scan_out, ffn_other[1:])
    weight_gate, weight_up = recut_end(ffn_own, ffn_got, ffn_other, 2)
    scanned = scan_out.reshape(row_count, channels) + weight_skip * signal_wide
    gate_act = jax.nn.silu(gate_mix)
    gated = rounded(scanned * gate_act)
    inputs = wide(tokens_own)

    def mixed_rows(first, last):
        return dot_last(gated[first * own_rows : last * own_rows], weight_out)

    middle = inputs + scatter_rows(mixed_rows, jnp.float32)

    (weight_down,) = recut_end(down_own, down_got, second_half(down_got), 1)
    scale_two = lax.rsqrt(jnp.mean(middle * middle, axis=1, keepdims=True) + epsilon)
    normed_two = gather_rows(rounded(middle * scale_two * gain_second))
    up_all = gather_rows(tied(up_own, normed_two))
    gate_part = dot_plain(normed_two, weight_gate)
    up_part = dot_plain(normed_two, weight_up)
    gate_silu = jax.nn.silu(gate_part)
    activated = rounded(gate_silu * up_part)
    act_grad = dot_plain(up_all, weight_down)
    gate_grad = rounded(act_grad * up_part * silu_slope(gate_part))
    up_grad = rounded(act_grad * gate_silu)

    def normed_two_rows(first, last):
        at = slice(first * own_rows, last * own_rows)
        return dot_last(gate_grad[at], weight_gate) + dot_last(up_grad[at], weight_up)

    x_first = tuple(range(len(masks_of("seq"))))
    down_grad = WeightGrad(up_all, activated, x_first).ready().send()
    normed_two_grad = scatter_rows(normed_two_rows)
    gain_two_grad = jnp.sum(normed_two_grad * middle * scale_two, axis=0)
    scaled_two = normed_two_grad * gain_second
    middle_grad = (
        wide(up_own)
        + scale_two * scaled_two
        - middle
        * (scale_two * scale_two * scale_two)
        * jnp.mean(scaled_two * middle, axis=1, keepdims=True)
    )
    mixed_grad = gather_rows(rounded(middle_grad))

    activated_late = tied(activated, mixed_grad)

    def result_rows(first, last):
        return dot_last(activated_late[first * own_rows : last * own_rows], weight_down)

    result = middle + scatter_rows(result_rows)
    output = rounded(result).reshape(tokens.shape)

    gated_grad = dot_plain(mixed_grad, weight_out)
    scan_grad = gated_grad * gate_act
    gate_mix_grad = rounded(gated_grad * scanned * silu_slope(gate_mix))
    skip_grad = jnp.sum(scan_grad * signal_wide, axis=0)
    ups = by_sequence(scan_grad)
    down_grad.add()
    gate_sum = WeightGrad(normed_two, gate_grad, x_first).ready(down_grad.got).send(ups)
    down_grad.ready().send()
    (seed,) = scan_call(
        seed_kernel,
        "scan_seed",
        1600,
        *sizes,
        [("rows", rows), ("tokens", rates), ("tokens", ups), ("fixed", a_scaled)],
        ["states"],
        ["tokens", "tokens"],
        [down_grad.sent, gate_sum.sent],
    )
    returning, _ = chained(total_rate, seed, a_scaled, -1)
    up_sum = WeightGrad(normed_two, up_grad, x_first).ready(gate_sum.sent).send(returning)
    gate_sum.add().ready().send(returning)
    down_grad.add().ready().send(returning)
    out_sum = WeightGrad(mixed_grad, gated, x_first)
    in_gate_sum = WeightGrad(normed, gate_mix_grad, x_first)
    rate_grad, scan_signal_grad, rows_grad, a_grad = scan_call(
        grad_kernel,
        "scan_grad",
        6300,
        *sizes,
        [
            ("rows", rows),
            ("tokens", rates),
            ("tokens", signals),
            ("tokens", ups),
            ("fixed", a_scaled),
            ("states", incoming),
            ("states", returning),
        ],
        ["tokens", "tokens", "rows_grad", "fixed"],
        ["history", "fixed", "tokens", "tokens", "tokens", "tokens", "tokens"],
        [up_sum.sent, gate_sum.sent, down_grad.sent],
    )
    out_sum.ready(rate_grad).send()
    in_gate_sum.ready(rate_grad).send(out_sum.got)
    rate_grad = rate_grad.reshape(row_count, channels)
    pre_grad = rate_grad * jax.nn.sigmoid(pre_rate)
    pre_grad_low = rounded(pre_grad)
    rank_grad = dot_last(weight_dt, pre_grad_low)
    rows_grad = jnp.swapaxes(jnp.sum(rows_grad, axis=3), 0, 1).reshape(2 * N, row_count)
    selection_grad = rounded(sum_columns(jnp.concatenate([rank_grad, rows_grad], axis=0)))
    signal_grad = (
        scan_grad * weight_skip
        + scan_signal_grad.reshape(row_count, channels)
        + lax.dot_general(
            selection_grad, weight_x, (((0,), (1,)), ((), ())), preferred_element_type=jnp.float32
        )
    )
    conv_grad = (signal_grad * silu_slope(conv_out)).reshape(sequences, length, channels)
    padded_grad = jnp.zeros((sequences, length + K - 1, channels), jnp.float32)
    for offset in range(K):
        padded_grad = padded_grad + jnp.pad(
            conv_taps[offset] * conv_grad, ((0, 0), (offset, K - 1 - offset), (0, 0))
        )
    returned = wide(passed_along(low(padded_grad[:, : K - 1]), "seq", -1))
    conv_in_grad = rounded(
        padded_grad[:, K - 1 :] + jnp.pad(returned, ((0, 0), (length - (K - 1), 0), (0, 0)))
    ).reshape(row_count, channels)
    in_conv_sum = WeightGrad(normed, conv_in_grad, x_first).ready().send()
    normed_grad_parts = {}

    def normed_rows(first, last):
        at = slice(first * own_rows, last * own_rows)
        part = dot_last(conv_in_grad[at], weight_conv_in) + dot_last(
            gate_mix_grad[at], weight_gate_in
        )
        normed_grad_parts[first] = jnp.sum(part * inputs_all[at] * scale_all[at], axis=0)
        return part

    normed_grad = scatter_rows(normed_rows)
    gain_one_grad = sum(normed_grad_parts.values())
    scale_one = scale_all[:own_rows]
    scaled_one = normed_grad * gain_norm
    input_grad = (
        middle_grad
        + scale_one * scaled_one
        - inputs
        * (scale_one * scale_one * scale_one)
        * jnp.mean(scaled_one * inputs, axis=1, keepdims=True)
    )

    conv_weight_grad = jnp.stack(
        [
            jnp.sum(conv_grad * padded[:, offset : offset + length], axis=(0, 1))
            for offset in range(K)
        ],
        axis=1,
    )
    column_sums = jnp.stack(
        [jnp.sum(conv_grad, axis=(0, 1)), jnp.sum(pre_grad, axis=0), skip_grad], axis=1
    )
    a_log_grad = a_grad.reshape(N, channels).T * a_matrix
    dt_weight_grad = lax.dot_general(
        pre_grad_low, rank_part, (((0,), (1,)), ((), ())), preferred_element_type=jnp.float32
    )
    x_weight_grad = lax.dot_general(
        signal, selection_grad, (((0,), (1,)), ((), ())), preferred_element_type=jnp.float32
    )
    small, gain_grads = small_grads(
        jnp.concatenate(
            [dt_weight_grad, x_weight_grad, a_log_grad, conv_weight_grad, column_sums], axis=1
        ),
        jnp.stack([gain_one_grad, gain_two_grad]),
    )
    at = R + R + 2 * N

    down_grad.add(rate_grad)
    ffn_down_result = rows_of_columns([down_grad.end()])
    up_sum.add()
    gate_sum.add()
    ffn_in_result = rows_of_columns([gate_sum.end(), up_sum.end()])
    out_sum.add()
    out_result = rows_of_columns([out_sum.end()])
    in_gate_sum.add()
    in_conv_sum.add()
    in_result = rows_of_columns([in_conv_sum.end(), in_gate_sum.end()])
    return (
        output,
        rounded(input_grad).reshape(tokens.shape),
        gain_grads[0],
        in_result,
        small[:, at + N : at + N + K].T,
        small[:, at + N + K],
        small[:, R:at],
        small[:, :R].T,
        small[:, at + N + K + 1],
        small[:, at : at + N],
        small[:, at + N + K + 2],
        out_result,
        gain_grads[1],
        ffn_in_result,
        ffn_down_result,
    )


def solution(mesh):
    in_specs = (
        P("shard", "seq", None),
        P("shard"),
        P("shard", None),
        P(None, "shard"),
        P("shard"),
        P("shard", None),
        P(None, "shard"),
        P("shard"),
        P("shard", None),
        P("shard"),
        P("shard", None),
        P("shard"),
        P("shard", None),
        P("shard", None),
        P("shard", "seq", None),
    )
    out_specs = (
        P("shard", "seq", None),
        P("shard", "seq", None),
        P(("seq", "shard")),
        P(("seq", "shard"), None),
        P(None, ("seq", "shard")),
        P(("seq", "shard")),
        P(("seq", "shard"), None),
        P(None, ("seq", "shard")),
        P(("seq", "shard")),
        P(("seq", "shard"), None),
        P(("seq", "shard")),
        P(("seq", "shard"), None),
        P(("seq", "shard")),
        P(("seq", "shard"), None),
        P(("seq", "shard"), None),
    )
    return jax.shard_map(local, mesh=mesh, in_specs=in_specs, out_specs=out_specs, check_vma=False)
```

```python
import functools
import math

import jax
import jax.numpy as jnp
from jax import lax
from jax.experimental import pallas as pl
from jax.experimental.pallas import tpu as pltpu
from jax.sharding import PartitionSpec as P

D = 2048
E = 4096
N = 16
K = 4
R = 128
FF = 8192

LANES = 128
GROUP = 8

epsilon = 1e-05
log2_e = math.log2(math.e)
ln_2 = math.log(2.0)


def silu_slope(value):
    sigma = jax.nn.sigmoid(value)
    return sigma * (1.0 + value * (1.0 - sigma))


def dot_last(left, right):
    return lax.dot_general(
        left, right, (((1,), (1,)), ((), ())), preferred_element_type=jnp.float32
    )


def dot_first(left, right):
    return lax.dot_general(
        left, right, (((0,), (0,)), ((), ())), preferred_element_type=jnp.float32
    )


def dot_plain(left, right):
    return jnp.dot(left, right, preferred_element_type=jnp.float32)


def wide(value):
    return value.astype(jnp.float32)


def low(value):
    return value.astype(jnp.bfloat16)


def rounded(value):
    return lax.reduce_precision(value, 8, 7).astype(jnp.bfloat16)


def exchange(value, axis, mask):
    return lax.ppermute(value, axis, [(i, i ^ mask) for i in range(lax.axis_size(axis))])


def passed_along(value, axis, by):
    peers = lax.axis_size(axis)
    pairs = [(i, i + by) for i in range(peers) if 0 <= i + by < peers]
    return lax.ppermute(value, axis, pairs)


def masks_of(axis):
    size = lax.axis_size(axis)
    return [1 << bit for bit in range(size.bit_length() - 1)]


def gather_rows(value, arrived=None):
    parts = {0: value}
    for mask in reversed(masks_of("shard")):
        held = sorted(parts)
        got = exchange(jnp.concatenate([parts[k] for k in held], axis=0), "shard", mask)
        if arrived is not None and mask > 1:
            arrived.append(got)
        for place, k in enumerate(held):
            parts[k ^ mask] = got[place * value.shape[0] : (place + 1) * value.shape[0]]
    return jnp.concatenate([parts[k] for k in sorted(parts)], axis=0)


def exchange_scaled(value, axis, mask):
    largest = jnp.maximum(jnp.max(jnp.abs(value)), 1e-30)
    scale = jnp.broadcast_to(largest, (8, LANES))
    got_scale = exchange(scale, axis, mask)
    got = exchange((value * (1.0 / largest)).astype(jnp.float16), axis, mask)
    return got.astype(jnp.float32) * got_scale[0, 0]


def scatter_rows(make, scaled=False, after=None):
    shards = lax.axis_size("shard")
    parts = {}
    for pair in reversed(range(0, shards, 2)):
        value = make(pair, pair + 2)
        rows = value.shape[0] // 2
        parts[pair] = value[:rows] + exchange(value[rows:], "shard", 1)
    for mask in masks_of("shard")[1:]:
        sent = [k for k in sorted(parts) if k & mask]
        block = jnp.concatenate([parts[k] for k in sent], axis=0)
        if scaled:
            got = exchange_scaled(block, "shard", mask)
        else:
            got = wide(exchange(low(block), "shard", mask))
        if after is not None:
            got = tied(got, after)
        for place, k in enumerate(sent):
            parts[k ^ mask] = parts[k ^ mask] + got[place * rows : (place + 1) * rows]
            del parts[k]
    return parts[0]


def sum_columns(value):
    shards = lax.axis_size("shard")
    count = value.shape[1] // shards
    for mask in masks_of("shard"):
        got = exchange(value, "shard", mask)
        order = [k ^ mask for k in range(shards)]
        value = value + jnp.concatenate(
            [got[:, k * count : (k + 1) * count] for k in order], axis=1
        )
    return value


def tied(values, after):
    return lax.optimization_barrier((values, after))[0]


def assemble_kernel(plan, count, at_ref, *refs):
    pieces, outs = refs[:count], refs[count : -1 - len(plan)]
    held, sems = refs[-1 - len(plan) : -1], refs[-1]
    fetches, stores = [], []
    for place, (piece, part, target, row, col, shape) in enumerate(plan):
        first = pl.multiple_of(at_ref[row], 16) if row is not None else 0
        left = pl.multiple_of(at_ref[col], LANES) if col is not None else 0
        fetch = pltpu.make_async_copy(
            pieces[piece].at[:, pl.ds(part * shape[1], shape[1])], held[place], sems.at[0, place]
        )
        fetch.start()
        fetches.append(fetch)
        stores.append(
            pltpu.make_async_copy(
                held[place],
                outs[target].at[pl.ds(first, shape[0]), pl.ds(left, shape[1])],
                sems.at[1, place],
            )
        )
    for fetch, store in zip(fetches, stores):
        fetch.wait()
        store.start()
    for store in stores:
        store.wait()


def assemble(pieces, plan, offsets, shapes):
    kind = pieces[0].dtype
    moved = sum(shape[0] * shape[1] * kind.itemsize for shape in shapes)
    any_space = pl.BlockSpec(memory_space=pl.ANY)
    return pl.pallas_call(
        functools.partial(assemble_kernel, plan, len(pieces)),
        name="assemble",
        in_specs=[pl.BlockSpec(memory_space=pltpu.SMEM)] + [any_space] * len(pieces),
        out_specs=[any_space] * len(shapes),
        out_shape=[jax.ShapeDtypeStruct(shape, kind) for shape in shapes],
        scratch_shapes=[pltpu.VMEM(entry[5], kind) for entry in plan]
        + [pltpu.SemaphoreType.DMA((2, len(plan)))],
        compiler_params=pltpu.CompilerParams(vmem_limit_bytes=48 * 1024 * 1024),
        cost_estimate=pl.CostEstimate(flops=0, bytes_accessed=2 * moved, transcendentals=0),
    )(jnp.stack(offsets).astype(jnp.int32), *pieces)


def column_part(weight, groups, group, target, first, count):
    columns = weight.shape[1] // (groups * lax.axis_size("shard"))
    at = (first, (group * lax.axis_size("shard") + target) * columns)
    return low(lax.dynamic_slice(weight, at, (count, columns)))


def halves_out(weight, groups, group):
    shards, mine = lax.axis_size("shard"), lax.axis_index("shard")
    rows = weight.shape[0]
    side = (lax.axis_index("seq") & 1) * (rows // 2)
    sent = [column_part(weight, groups, group, mine ^ 1, 0, rows)]
    return sent + [
        column_part(weight, groups, group, mine ^ k, side, rows // 2) for k in range(2, shards)
    ]


def halves_in(weight, groups, group, got, other):
    shards, mine = lax.axis_size("shard"), lax.axis_index("shard")
    rows = weight.shape[0]
    half = rows // 2
    side = (lax.axis_index("seq") & 1) * half
    own = column_part(weight, groups, group, mine, 0, rows)
    pieces = [own] + got + other
    offsets = [mine * rows, (mine ^ 1) * rows]
    offsets += [(mine ^ k) * rows + side for k in range(2, shards)]
    offsets += [(mine ^ k) * rows + half - side for k in range(2, shards)]
    plan = [(place, 0, 0, place, None, piece.shape) for place, piece in enumerate(pieces)]
    return assemble(pieces, plan, offsets, [(shards * rows, own.shape[1])])[0]


def recut(groups, after):
    shards, mine = lax.axis_size("shard"), lax.axis_index("shard")
    peers, range_at = lax.axis_size("seq"), lax.axis_index("seq")
    rows = groups[0][0].shape[0]
    fetched = rows // peers

    def part(target, first, count):
        pieces = [column_part(*group, target, first, count) for group in groups]
        return jnp.concatenate(pieces, axis=1)

    far = [part(mine ^ k, range_at * fetched, fetched) for k in range(2, shards)]
    far = [exchange(piece, "shard", k + 2) for k, piece in enumerate(tied(far, after))]
    near = exchange(part(mine ^ 1, 0, rows), "shard", 1)
    return part(mine, 0, rows), near, far


def gathered(pieces):
    return lax.all_gather(jnp.concatenate(pieces, axis=1), "seq", axis=0, tiled=True)


def recut_end(own, near, far, count, width, first=0):
    shards, mine = lax.axis_size("shard"), lax.axis_index("shard")
    rows = own.shape[0]
    plan, offsets = [], []
    for k in range(shards):
        offsets.append((mine ^ k) * rows)
        for group in range(count):
            part = first + group if k < 2 else (k - 2) * count + group
            plan.append((min(k, 2), part, group, k, None, (rows, width)))
    return assemble([own, near, far], plan, offsets, [(shards * rows, width)] * count)


def with_bit(blocks, bit):
    return [b for b in range(blocks) if not b >> bit & 1]


def halve(value, left, bit, sent_type):
    mine = (lax.axis_index("seq") >> bit) & 1
    inner = 1 << sorted(left).index(bit)
    blocks, rows, columns = value.shape
    shaped = value.reshape(blocks // (2 * inner), 2, inner * rows, columns)
    sent = lax.dynamic_index_in_dim(shaped, 1 - mine, 1, keepdims=False).astype(sent_type)
    kept = lax.dynamic_index_in_dim(shaped, mine, 1, keepdims=False)
    left.remove(bit)
    return sent, kept


def split_columns(left, bit):
    peers = lax.axis_size("seq")
    mine = (lax.axis_index("seq") >> bit) & 1
    rows = left.shape[1] // peers

    def half(which):
        pieces = [
            lax.dynamic_slice_in_dim(left, (b + (which << bit)) * rows, rows, axis=1)
            for b in with_bit(peers, bit)
        ]
        return jnp.concatenate(pieces, axis=1)

    return half(1 - mine), half(mine)


class WeightGrad:
    def __init__(self, halves, right):
        self.halves, self.right = halves, right
        self.remaining = [mask.bit_length() - 1 for mask in masks_of("seq")]
        self.rows = 2 * halves[0].shape[1] // lax.axis_size("seq")
        self.total = None

    def ready(self, after=None):
        bit = self.remaining[0]
        if self.total is None:
            if after is not None:
                self.right = tied(self.right, after)
            self.sent = low(dot_first(self.halves[0], self.right))
            self.remaining.remove(bit)
        else:
            self.sent, self.kept = halve(self.total, self.remaining, bit, jnp.bfloat16)
        self.got = exchange(self.sent, "seq", 1 << bit)
        return self.sent

    def add(self, after=None):
        got = self.got if after is None else tied(self.got, after)
        if self.total is None:
            total = dot_first(self.halves[1], self.right) + wide(got)
        else:
            total = self.kept + wide(got).reshape(self.kept.shape)
        self.total = total.reshape(-1, self.rows, self.right.shape[1])

    def step(self, after=None):
        self.add(after)
        return self.ready()

    def end(self, after=None):
        self.add(after)
        while self.remaining:
            self.ready()
            self.add()
        self.done = self.total.reshape(self.total.shape[1:])
        return self.done


def rows_of_columns(blocks, groups):
    shards, mine = lax.axis_size("shard"), lax.axis_index("shard")
    parts = len(blocks) // groups
    rows = blocks[0].shape[0] // shards
    columns = blocks[0].shape[1]

    def part(target):
        return jnp.concatenate(
            [lax.dynamic_slice_in_dim(block, target * rows, rows, axis=0) for block in blocks],
            axis=1,
        )

    pieces = [part(mine)] + [exchange(part(mine ^ k), "shard", k) for k in range(1, shards)]
    offsets = [
        (group * shards + (mine ^ k)) * columns * parts
        for k in range(shards)
        for group in range(groups)
    ]
    shape = (rows, columns * parts)
    plan = [
        (k, group, 0, None, k * groups + group, shape)
        for k in range(shards)
        for group in range(groups)
    ]
    return assemble(pieces, plan, offsets, [(rows, groups * shards * columns * parts)])[0]


def small_grads(value, gains):
    peers, shards = lax.axis_size("seq"), lax.axis_size("shard")
    rows = value.shape[0] // peers
    width = value.shape[1]
    packed = jnp.transpose(gains.reshape(2, peers, shards, -1), (1, 0, 3, 2))
    value = jnp.concatenate([value, packed.reshape(value.shape[0], shards)], axis=1)
    total = value.reshape(peers, rows, width + shards)
    left = [mask.bit_length() - 1 for mask in masks_of("seq")]
    for bit in list(left):
        sent, kept = halve(total, left, bit, jnp.float32)
        total = (kept + exchange(sent, "seq", 1 << bit)).reshape(-1, rows, width + shards)
    total = total.reshape(rows, width + shards)
    gain_sum = total[:, width:]
    for mask in masks_of("shard"):
        gain_sum = gain_sum + exchange(gain_sum, "shard", mask)
    gain_sum = lax.dynamic_index_in_dim(gain_sum, lax.axis_index("shard"), 1, keepdims=False)
    pairs = [(s * shards + h, h * peers + s) for s in range(peers) for h in range(shards)]
    return lax.ppermute(total[:, :width], ("seq", "shard"), pairs), gain_sum.reshape(2, -1)


def spread(source, target, length):
    for c in range(source.shape[-1] // LANES):
        target[pl.ds(c * length, length), :] = wide(source[0, :, c * LANES : (c + 1) * LANES])


def collect(source, target, length):
    for c in range(target.shape[-1] // LANES):
        target[0, :, c * LANES : (c + 1) * LANES] = source[pl.ds(c * length, length), :]


def token_rows(ref, token, blocks, length):
    return ref[pl.ds(token, blocks, stride=length), :]


def sum_blocks(values):
    blocks = values[0].shape[0]
    if blocks != GROUP:
        return jnp.concatenate([jnp.sum(v, axis=0, keepdims=True) for v in values], axis=0)
    row = lax.broadcasted_iota(jnp.int32, (GROUP, LANES), 0)
    upper = row < 4
    level = [
        jnp.where(upper, values[j], values[j + 4])
        + pltpu.roll(jnp.where(upper, values[j + 4], values[j]), 4, 0)
        for j in range(4)
    ]
    for step in (2, 1):
        first = (row & step) == 0
        level = [
            jnp.where(
                first,
                level[j] + pltpu.roll(level[j], GROUP - step, 0),
                level[j + step] + pltpu.roll(level[j + step], step, 0),
            )
            for j in range(step)
        ]
    return level[0]


def end_kernel(length, blocks, rows_ref, rate_ref, signal_ref, a_ref, state_ref, total_ref, rate, signal):
    spread(rate_ref, rate, length)
    spread(signal_ref, signal, length)
    state_ref[...] = jnp.zeros_like(state_ref)

    def group(i, total):
        start = i * GROUP
        rates = [token_rows(rate, start + j, blocks, length) for j in range(GROUP)]
        drives = [
            rates[j] * token_rows(signal, start + j, blocks, length) for j in range(GROUP)
        ]
        for n in range(N):
            state, a = state_ref[0, n], a_ref[n]
            for j in range(GROUP):
                state = jnp.exp2(rates[j] * a) * state + drives[j] * rows_ref[0, 0, n * length + start + j]
            state_ref[0, n] = state
        for j in range(GROUP):
            total = total + rates[j]
        return total

    total_ref[0, 0] = lax.fori_loop(
        0, length // GROUP, group, jnp.zeros((blocks, LANES), jnp.float32)
    )


def scan_kernel(
    length, blocks, rows_ref, rate_ref, signal_ref, a_ref, in_ref, out_ref, state_ref, rate, signal, out
):
    spread(rate_ref, rate, length)
    spread(signal_ref, signal, length)
    state_ref[...] = in_ref[0]

    def group(i, carry):
        start = i * GROUP
        rates = [token_rows(rate, start + j, blocks, length) for j in range(GROUP)]
        drives = [
            rates[j] * token_rows(signal, start + j, blocks, length) for j in range(GROUP)
        ]
        outs = [None] * GROUP
        for n in range(N):
            state, a = state_ref[n], a_ref[n]
            for j in range(GROUP):
                state = jnp.exp2(rates[j] * a) * state + drives[j] * rows_ref[0, 0, n * length + start + j]
                term = state * rows_ref[0, 0, (N + n) * length + start + j]
                outs[j] = term if outs[j] is None else outs[j] + term
            state_ref[n] = state
        for j in range(GROUP):
            out[pl.ds(start + j, blocks, stride=length), :] = outs[j]
        return carry

    lax.fori_loop(0, length // GROUP, group, 0)
    collect(out, out_ref, length)


def seed_kernel(length, blocks, rows_ref, rate_ref, up_ref, a_ref, seed_ref, rate, up):
    spread(rate_ref, rate, length)
    spread(up_ref, up, length)
    seed_ref[...] = jnp.zeros_like(seed_ref)

    def group(i, carry):
        start = length - GROUP - i * GROUP
        rates = [token_rows(rate, start + j, blocks, length) for j in range(GROUP)]
        ups = [token_rows(up, start + j, blocks, length) for j in range(GROUP)]
        for n in range(N):
            back, a = seed_ref[0, n], a_ref[n]
            for j in reversed(range(GROUP)):
                back = jnp.exp2(rates[j] * a) * (
                    back + ups[j] * rows_ref[0, 0, (N + n) * length + start + j]
                )
            seed_ref[0, n] = back
        return carry

    lax.fori_loop(0, length // GROUP, group, 0)


def grad_kernel(
    length,
    blocks,
    rows_ref,
    rate_ref,
    signal_ref,
    up_ref,
    a_ref,
    in_ref,
    back_ref,
    a_before_ref,
    rate_grad_ref,
    signal_grad_ref,
    rows_grad_ref,
    a_grad_ref,
    states,
    back_state,
    rate,
    signal,
    up,
    rate_grad,
    signal_grad,
):
    spread(rate_ref, rate, length)
    spread(signal_ref, signal, length)
    spread(up_ref, up, length)
    for n in range(N):
        states[n, 0] = in_ref[0, n]
    back_state[...] = back_ref[0]

    @pl.when(pl.program_id(0) == 0)
    def _():
        a_grad_ref[...] = a_before_ref[...]

    def forward(i, carry):
        start = i * GROUP
        rates = [token_rows(rate, start + j, blocks, length) for j in range(GROUP)]
        drives = [
            rates[j] * token_rows(signal, start + j, blocks, length) for j in range(GROUP)
        ]
        for n in range(N):
            state, a = states[n, start], a_ref[n]
            for j in range(GROUP):
                state = jnp.exp2(rates[j] * a) * state + drives[j] * rows_ref[0, 0, n * length + start + j]
                states[n, start + j + 1] = state
        return carry

    lax.fori_loop(0, length // GROUP, forward, 0)

    def backward(i, carry):
        start = length - GROUP - i * GROUP
        rates = [token_rows(rate, start + j, blocks, length) for j in range(GROUP)]
        signals = [token_rows(signal, start + j, blocks, length) for j in range(GROUP)]
        ups = [token_rows(up, start + j, blocks, length) for j in range(GROUP)]
        through = [None] * GROUP
        slope = [None] * GROUP
        for n in range(N):
            back, a = back_state[n], a_ref[n]
            a_sum = None
            to_b = [None] * GROUP
            to_c = [None] * GROUP
            for j in reversed(range(GROUP)):
                b = rows_ref[0, 0, n * length + start + j]
                c = rows_ref[0, 0, (N + n) * length + start + j]
                here = back + ups[j] * c
                back = jnp.exp2(rates[j] * a) * here
                moved = back * states[n, start + j]
                a_term = moved * rates[j]
                a_sum = a_term if a_sum is None else a_sum + a_term
                b_term, a_slope = here * b, moved * a
                through[j] = b_term if through[j] is None else through[j] + b_term
                slope[j] = a_slope if slope[j] is None else slope[j] + a_slope
                to_b[j] = here * (rates[j] * signals[j])
                to_c[j] = ups[j] * states[n, start + j + 1]
            back_state[n] = back
            a_grad_ref[n] = a_grad_ref[n] + a_sum
            at = pl.ds(pl.multiple_of(start, GROUP), GROUP)
            rows_grad_ref[0, n, at, :] = sum_blocks(to_b)
            rows_grad_ref[0, N + n, at, :] = sum_blocks(to_c)
        for j in range(GROUP):
            rows = pl.ds(start + j, blocks, stride=length)
            rate_grad[rows, :] = through[j] * signals[j] + slope[j] * ln_2
            signal_grad[rows, :] = through[j] * rates[j]
        return carry

    lax.fori_loop(0, length // GROUP, backward, 0)
    collect(rate_grad, rate_grad_ref, length)
    collect(signal_grad, signal_grad_ref, length)


def scan_call(kernel, name, sequences, length, channels, inputs, outputs, scratch, after=(), part=(0, 1), before=None):
    blocks = channels // LANES
    count = sequences // part[1]
    at = part[0] * count
    before = [] if before is None else list(before)
    kinds = {
        "rows": ((1, 1, 2 * N * length), lambda s: (at + s, 0, 0)),
        "tokens": ((1, length, channels), lambda s: (at + s, 0, 0)),
        "states": ((1, N, blocks, LANES), lambda s: (at + s, 0, 0, 0)),
        "total": ((1, 1, blocks, LANES), lambda s: (at + s, 0, 0, 0)),
        "fixed": ((N, blocks, LANES), lambda s: (0, 0, 0)),
        "rows_grad": ((1, 2 * N, length, LANES), lambda s: (at + s, 0, 0, 0)),
    }

    def spec(kind):
        shape, index = kinds[kind]
        if kind == "rows":
            return pl.BlockSpec(shape, index, memory_space=pltpu.SMEM)
        return pl.BlockSpec(shape, index)

    def whole(kind):
        shape = kinds[kind][0]
        if kind != "fixed":
            shape = (sequences,) + shape[1:]
        return jax.ShapeDtypeStruct(shape, jnp.float32)

    def space(kind):
        if kind == "tokens":
            return pltpu.VMEM((blocks * length, LANES), jnp.float32)
        if kind == "history":
            return pltpu.VMEM((N, length + 1, blocks, LANES), jnp.float32)
        return pltpu.VMEM((N, blocks, LANES), jnp.float32)

    values = [value for _, value in inputs]
    values = tied(values, list(after))
    def body(*refs):
        kernel(length, blocks, *refs[: len(inputs)], *refs[len(inputs) + len(before) :])

    return pl.pallas_call(
        body,
        name=name,
        grid=(count,),
        in_specs=[spec(kind) for kind, _ in inputs]
        + [pl.BlockSpec(memory_space=pl.ANY)] * len(before),
        input_output_aliases={len(inputs) + i: i for i in range(len(before))},
        out_specs=[spec(kind) for kind in outputs],
        out_shape=[whole(kind) for kind in outputs],
        scratch_shapes=[space(kind) for kind in scratch],
        compiler_params=pltpu.CompilerParams(vmem_limit_bytes=56 * 1024 * 1024),
        cost_estimate=pl.CostEstimate(
            flops=0,
            bytes_accessed=0,
            transcendentals=0,
        ),
    )(*values, *before)


def chained(total, state, a_scaled, direction):
    peers = lax.axis_size("seq")
    second_of_pair = (lax.axis_index("seq") & 1) == (1 if direction == 1 else 0)

    def join(first, second):
        return (
            first[0] + second[0],
            jnp.exp2(second[0] * a_scaled) * first[1] + second[1],
        )

    def split(packed):
        return (packed[:, :1], packed[:, 1:])

    def chosen(flag, yes, no):
        return tuple(jnp.where(flag, a, b) for a, b in zip(yes, no))

    own = (total, state)
    mate = split(exchange(jnp.concatenate(own, axis=1), "seq", 1))
    first = chosen(second_of_pair, mate, own)
    pair = join(first, chosen(second_of_pair, own, mate))
    packed = jnp.concatenate(pair, axis=1)
    before = None
    for by in reversed(range(2, peers, 2)):
        got = split(passed_along(packed, "seq", direction * by))
        before = got if before is None else join(before, got)
    return jnp.where(second_of_pair, join(before, first)[1], before[1]), packed


def local(
    tokens,
    gain_one,
    in_weight,
    conv_weight,
    conv_bias,
    x_weight,
    dt_weight,
    dt_bias,
    a_log,
    skip_gain,
    out_weight,
    gain_two,
    ffn_in,
    ffn_down,
    cotangent,
):
    shards = lax.axis_size("shard")
    held, length, _ = tokens.shape
    sequences = held * shards
    own_rows = held * length
    row_count = sequences * length
    channels = conv_bias.shape[0]
    blocks = channels // LANES

    def by_sequence(value):
        return value.reshape(sequences, length, value.shape[-1])

    tokens_own = tokens.reshape(own_rows, D)
    up_own = cotangent.reshape(own_rows, D)
    gains_own = rounded(jnp.concatenate([gain_one, gain_two])).reshape(1, -1)
    gain_rows = jnp.pad(gains_own, ((0, 15), (0, D - gains_own.shape[1])))
    conv_sent = halves_out(in_weight, 2, 0)
    conv_got = [exchange(piece, "shard", k + 1) for k, piece in enumerate(conv_sent)]
    arrived = []
    packed = jnp.concatenate([tokens_own, gain_rows], axis=0)
    packed = gather_rows(tied(packed, conv_sent), arrived).reshape(shards, own_rows + 16, D)
    tokens_all = packed[:, :own_rows].reshape(row_count, D)
    gains = packed[:, own_rows, : gains_own.shape[1]].reshape(shards, 2, -1)
    in_turn = [
        lax.dynamic_index_in_dim(gains, lax.axis_index("shard") ^ k, 0, keepdims=False)
        for k in range(shards)
    ]
    gains = wide(jnp.concatenate(in_turn, axis=1))
    gain_norm, gain_second = gains[0], gains[1]

    conv_other = [exchange(piece, "seq", 1) for piece in conv_got[1:]]
    groups = [(in_weight, 2, 1), (out_weight, 1, 0)]
    own, near, far = recut(groups + [(ffn_in, 2, 0), (ffn_in, 2, 1)], [arrived, conv_got])
    weight_conv_in = halves_in(in_weight, 2, 0, conv_got, conv_other)
    mixer_far = gathered([piece[:, : 2 * channels] for piece in far])
    ffn_far = gathered([piece[:, 2 * channels :] for piece in far])
    weight_gate_in, weight_out = recut_end(own, near, mixer_far, 2, channels)

    conv_taps = wide(rounded(conv_weight))
    bias_conv = wide(rounded(conv_bias))
    weight_x = rounded(x_weight)
    weight_dt = rounded(dt_weight)
    bias_dt = wide(rounded(dt_bias))
    weight_skip = wide(rounded(skip_gain))
    a_matrix = -jnp.exp(wide(rounded(a_log)))
    a_scaled = (a_matrix * log2_e).T.reshape(N, blocks, LANES)

    inputs_all = wide(tokens_all)
    scale_all = lax.rsqrt(jnp.mean(inputs_all * inputs_all, axis=1, keepdims=True) + epsilon)
    normed = rounded(inputs_all * scale_all * gain_norm)
    conv_in = by_sequence(rounded(dot_plain(normed, weight_conv_in)))
    gate_mix = dot_plain(normed, weight_gate_in)
    borrowed = passed_along(conv_in[:, length - (K - 1) :], "seq", 1)
    padded = wide(jnp.concatenate([borrowed, conv_in], axis=1))
    conv_out = bias_conv + jnp.zeros((sequences, length, channels), jnp.float32)
    for offset in range(K):
        conv_out = conv_out + conv_taps[offset] * padded[:, offset : offset + length]
    conv_out = conv_out.reshape(row_count, channels)
    signal = rounded(jax.nn.silu(conv_out))
    signal_wide = wide(signal)
    selection = sum_columns(
        lax.dot_general(
            weight_x, signal, (((0,), (1,)), ((), ())), preferred_element_type=jnp.float32
        )
    )
    down_sent = tied(halves_out(ffn_down, 1, 0), selection)
    down_got = [exchange(piece, "shard", k + 1) for k, piece in enumerate(down_sent)]
    rank_part = rounded(selection[:R])
    rows = jnp.swapaxes(selection[R:].reshape(2 * N, sequences, length), 0, 1).reshape(
        sequences, 1, 2 * N * length
    )
    pre_rate = dot_first(rank_part, weight_dt) + bias_dt
    rates = by_sequence(jax.nn.softplus(pre_rate))
    signals = by_sequence(signal)
    sizes = (sequences, length, channels)
    end_state, total_rate = scan_call(
        end_kernel,
        "scan_end",
        *sizes,
        [("rows", rows), ("tokens", rates), ("tokens", signals), ("fixed", a_scaled)],
        ["states", "total"],
        ["tokens", "tokens"],
        [near] + far,
    )
    incoming, first_round = chained(total_rate, end_state, a_scaled, 1)
    down_other = [exchange(piece, "seq", 1) for piece in tied(down_got[1:], first_round)]
    ffn_width = ffn_in.shape[1] // (2 * shards)
    (scan_out,) = scan_call(
        scan_kernel,
        "scan_out",
        *sizes,
        [
            ("rows", rows),
            ("tokens", rates),
            ("tokens", signals),
            ("fixed", a_scaled),
            ("states", incoming),
        ],
        ["tokens"],
        ["fixed", "tokens", "tokens", "tokens"],
        down_got,
    )
    weight_down = halves_in(ffn_down, 1, 0, down_got, tied(down_other, scan_out))
    ffn_offset = 2 * channels // ffn_width
    weight_gate, weight_up = recut_end(own, near, ffn_far, 2, ffn_width, ffn_offset)
    scanned = scan_out.reshape(row_count, channels) + weight_skip * signal_wide
    gate_act = jax.nn.silu(gate_mix)
    gated = rounded(scanned * gate_act)
    inputs = wide(tokens_own)

    def mixed_rows(first, last):
        return dot_last(gated[first * own_rows : last * own_rows], weight_out)

    middle = inputs + scatter_rows(mixed_rows, True, [weight_gate, weight_up])

    scale_two = lax.rsqrt(jnp.mean(middle * middle, axis=1, keepdims=True) + epsilon)
    arrived = []
    normed_two = gather_rows(rounded(middle * scale_two * gain_second), arrived)
    up_all = gather_rows(tied(up_own, arrived))
    gate_part = dot_plain(normed_two, weight_gate)
    up_part = dot_plain(normed_two, weight_up)
    gate_silu = jax.nn.silu(gate_part)
    activated = rounded(gate_silu * up_part)
    columns = activated.shape[1] // 2
    up_halves = split_columns(up_all, 0)
    down_first = WeightGrad(up_halves, activated[:, :columns])
    down_second = WeightGrad(up_halves, activated[:, columns:])
    up_late = tied(up_all, down_first.ready())
    act_grad = dot_plain(up_late, weight_down)
    gate_grad = rounded(act_grad * up_part * silu_slope(gate_part))
    up_grad = rounded(act_grad * gate_silu)
    gate_late, up_grad_late = tied((gate_grad, up_grad), down_second.ready(gate_grad))

    def normed_two_rows(first, last):
        at = slice(first * own_rows, last * own_rows)
        return dot_last(gate_late[at], weight_gate) + dot_last(up_grad_late[at], weight_up)

    normed_two_grad = scatter_rows(normed_two_rows)
    two_halves = split_columns(normed_two, 0)
    gate_first = WeightGrad(two_halves, gate_grad[:, :columns])
    gate_second = WeightGrad(two_halves, gate_grad[:, columns:])
    up_first = WeightGrad(two_halves, up_grad[:, :columns])
    up_second = WeightGrad(two_halves, up_grad[:, columns:])
    gain_two_grad = jnp.sum(normed_two_grad * middle * scale_two, axis=0)
    scaled_two = normed_two_grad * gain_second
    middle_grad = (
        wide(up_own)
        + scale_two * scaled_two
        - middle
        * (scale_two * scale_two * scale_two)
        * jnp.mean(scaled_two * middle, axis=1, keepdims=True)
    )
    mixed_grad = gather_rows(rounded(middle_grad))
    steps = [down_first.step(middle_grad), gate_first.ready(middle_grad)]
    mixed_late = tied(mixed_grad, steps)

    gated_grad = dot_plain(mixed_late, weight_out)
    scan_grad = gated_grad * gate_act
    gate_mix_grad = rounded(gated_grad * scanned * silu_slope(gate_mix))
    skip_grad = jnp.sum(scan_grad * signal_wide, axis=0)
    ups = by_sequence(scan_grad)
    steps = [down_second.step(ups)]
    (seed,) = scan_call(
        seed_kernel,
        "scan_seed",
        *sizes,
        [("rows", rows), ("tokens", rates), ("tokens", ups), ("fixed", a_scaled)],
        ["states"],
        ["tokens", "tokens"],
        steps,
    )
    returning, first_round = chained(total_rate, seed, a_scaled, -1)
    activated_late = tied(activated, seed)

    def result_rows(first, last):
        return dot_last(activated_late[first * own_rows : last * own_rows], weight_down)

    result = middle + scatter_rows(result_rows)
    output = rounded(result).reshape(tokens.shape)
    steps = [gate_second.ready(first_round)]
    steps += [down_first.step(returning), gate_first.step(returning), up_first.ready(returning)]
    mixed_halves = split_columns(mixed_grad, 0)
    normed_halves = split_columns(normed, 0)
    out_sum = WeightGrad(mixed_halves, gated)
    in_gate_sum = WeightGrad(normed_halves, gate_mix_grad)
    grads = None
    for part in range(2):
        grads = scan_call(
            grad_kernel,
            "scan_grad",
            *sizes,
            [
                ("rows", rows),
                ("tokens", rates),
                ("tokens", signals),
                ("tokens", ups),
                ("fixed", a_scaled),
                ("states", incoming),
                ("states", returning),
                ("fixed", jnp.zeros_like(a_scaled) if grads is None else grads[3]),
            ],
            ["tokens", "tokens", "rows_grad", "fixed"],
            ["history", "fixed", "tokens", "tokens", "tokens", "tokens", "tokens"],
            steps,
            part=(part, 2),
            before=None if grads is None else grads[:3],
        )
        if part == 0:
            token = grads[3]
            steps = [down_second.step(token), gate_second.step(token), up_second.ready(token)]
            steps += [down_first.end(token)]
    rate_grad, scan_signal_grad, rows_grad, a_grad = grads
    steps = [gate_first.step(a_grad), up_first.step(a_grad), out_sum.ready(a_grad)]
    steps += [down_second.end(a_grad)]
    rate_grad = tied(rate_grad, steps)
    rate_grad = rate_grad.reshape(row_count, channels)
    pre_grad = rate_grad * jax.nn.sigmoid(pre_rate)
    pre_grad_low = rounded(pre_grad)
    rank_grad = dot_last(weight_dt, pre_grad_low)
    rows_grad = jnp.swapaxes(jnp.sum(rows_grad, axis=3), 0, 1).reshape(2 * N, row_count)
    selection_grad = rounded(sum_columns(jnp.concatenate([rank_grad, rows_grad], axis=0)))
    steps = [gate_second.step(selection_grad), up_second.step(selection_grad)]
    steps += [in_gate_sum.ready(selection_grad), gate_first.end(selection_grad)]
    selection_grad = tied(selection_grad, steps)
    signal_grad = (
        scan_grad * weight_skip
        + scan_signal_grad.reshape(row_count, channels)
        + lax.dot_general(
            selection_grad, weight_x, (((0,), (1,)), ((), ())), preferred_element_type=jnp.float32
        )
    )
    conv_grad = (signal_grad * silu_slope(conv_out)).reshape(sequences, length, channels)
    padded_grad = jnp.zeros((sequences, length + K - 1, channels), jnp.float32)
    for offset in range(K):
        padded_grad = padded_grad + jnp.pad(
            conv_taps[offset] * conv_grad, ((0, 0), (offset, K - 1 - offset), (0, 0))
        )
    returned = wide(passed_along(low(padded_grad[:, : K - 1]), "seq", -1))
    conv_in_grad = rounded(
        padded_grad[:, K - 1 :] + jnp.pad(returned, ((0, 0), (length - (K - 1), 0), (0, 0)))
    ).reshape(row_count, channels)
    in_conv_sum = WeightGrad(normed_halves, conv_in_grad)
    steps = [in_conv_sum.ready(), up_first.step(conv_in_grad), out_sum.step(conv_in_grad)]
    steps += [gate_second.end(conv_in_grad)]
    conv_in_grad = tied(conv_in_grad, steps)
    normed_grad_parts = {}
    conv_in_late = tied(conv_in_grad, [up_second.step(conv_in_grad), in_gate_sum.step(conv_in_grad)])

    def normed_rows(first, last):
        at = slice(first * own_rows, last * own_rows)
        part = dot_last(conv_in_late[at], weight_conv_in) + dot_last(
            gate_mix_grad[at], weight_gate_in
        )
        normed_grad_parts[first] = jnp.sum(part * inputs_all[at] * scale_all[at], axis=0)
        return part

    normed_grad = scatter_rows(normed_rows)
    gain_one_grad = sum(normed_grad_parts.values())
    steps = [in_conv_sum.step(gain_one_grad), out_sum.step(gain_one_grad)]
    gain_one_grad = tied(gain_one_grad, steps)
    scale_one = scale_all[:own_rows]
    scaled_one = normed_grad * gain_norm
    input_grad = (
        middle_grad
        + scale_one * scaled_one
        - inputs
        * (scale_one * scale_one * scale_one)
        * jnp.mean(scaled_one * inputs, axis=1, keepdims=True)
    )


    conv_weight_grad = jnp.stack(
        [
            jnp.sum(conv_grad * padded[:, offset : offset + length], axis=(0, 1))
            for offset in range(K)
        ],
        axis=1,
    )
    column_sums = jnp.stack(
        [jnp.sum(conv_grad, axis=(0, 1)), jnp.sum(pre_grad, axis=0), skip_grad], axis=1
    )
    a_log_grad = a_grad.reshape(N, channels).T * a_matrix
    dt_weight_grad = lax.dot_general(
        pre_grad_low, rank_part, (((0,), (1,)), ((), ())), preferred_element_type=jnp.float32
    )
    x_weight_grad = lax.dot_general(
        signal, selection_grad, (((0,), (1,)), ((), ())), preferred_element_type=jnp.float32
    )
    small, gain_grads = small_grads(
        jnp.concatenate(
            [dt_weight_grad, x_weight_grad, a_log_grad, conv_weight_grad, column_sums], axis=1
        ),
        jnp.stack([gain_one_grad, gain_two_grad]),
    )
    at = R + R + 2 * N

    ffn_down_result = rows_of_columns([down_first.done, down_second.done], 1)
    ffn_in_result = rows_of_columns(
        [
            gate_first.done,
            gate_second.done,
            up_first.end(gain_one_grad),
            up_second.end(gain_one_grad),
        ],
        2,
    )
    out_result = rows_of_columns([out_sum.end()], 1)
    in_result = rows_of_columns([in_conv_sum.end(), in_gate_sum.end()], 2)
    return (
        output,
        rounded(input_grad).reshape(tokens.shape),
        gain_grads[0],
        in_result,
        small[:, at + N : at + N + K].T,
        small[:, at + N + K],
        small[:, R:at],
        small[:, :R].T,
        small[:, at + N + K + 1],
        small[:, at : at + N],
        small[:, at + N + K + 2],
        out_result,
        gain_grads[1],
        ffn_in_result,
        ffn_down_result,
    )


def solution(mesh):
    in_specs = (
        P("shard", "seq", None),
        P("shard"),
        P("shard", None),
        P(None, "shard"),
        P("shard"),
        P("shard", None),
        P(None, "shard"),
        P("shard"),
        P("shard", None),
        P("shard"),
        P("shard", None),
        P("shard"),
        P("shard", None),
        P("shard", None),
        P("shard", "seq", None),
    )
    out_specs = (
        P("shard", "seq", None),
        P("shard", "seq", None),
        P(("seq", "shard")),
        P(("seq", "shard"), None),
        P(None, ("seq", "shard")),
        P(("seq", "shard")),
        P(("seq", "shard"), None),
        P(None, ("seq", "shard")),
        P(("seq", "shard")),
        P(("seq", "shard"), None),
        P(("seq", "shard")),
        P(("seq", "shard"), None),
        P(("seq", "shard")),
        P(("seq", "shard"), None),
        P(("seq", "shard"), None),
    )
    return jax.shard_map(local, mesh=mesh, in_specs=in_specs, out_specs=out_specs, check_vma=False)
```

```python
import functools
import math

import jax
import jax.numpy as jnp
from jax import lax
from jax.experimental import pallas as pl
from jax.experimental.pallas import tpu as pltpu
from jax.sharding import PartitionSpec as P

D = 2048
E = 4096
N = 16
K = 4
R = 128
FF = 8192

LANES = 128
GROUP = 8

epsilon = 1e-05
log2_e = math.log2(math.e)
ln_2 = math.log(2.0)


def silu_slope(value):
    sigma = jax.nn.sigmoid(value)
    return sigma * (1.0 + value * (1.0 - sigma))


def dot_last(left, right):
    return lax.dot_general(
        left, right, (((1,), (1,)), ((), ())), preferred_element_type=jnp.float32
    )


def dot_first(left, right):
    return lax.dot_general(
        left, right, (((0,), (0,)), ((), ())), preferred_element_type=jnp.float32
    )


def dot_plain(left, right):
    return jnp.dot(left, right, preferred_element_type=jnp.float32)


def wide(value):
    return value.astype(jnp.float32)


def low(value):
    return value.astype(jnp.bfloat16)


def rounded(value):
    return lax.reduce_precision(value, 8, 7).astype(jnp.bfloat16)


def exchange(value, axis, mask):
    return lax.ppermute(value, axis, [(i, i ^ mask) for i in range(lax.axis_size(axis))])


def passed_along(value, axis, by):
    peers = lax.axis_size(axis)
    pairs = [(i, i + by) for i in range(peers) if 0 <= i + by < peers]
    return lax.ppermute(value, axis, pairs)


def masks_of(axis):
    size = lax.axis_size(axis)
    return [1 << bit for bit in range(size.bit_length() - 1)]


def gather_rows(value, arrived=None):
    parts = {0: value}
    for mask in reversed(masks_of("shard")):
        held = sorted(parts)
        got = exchange(jnp.concatenate([parts[k] for k in held], axis=0), "shard", mask)
        if arrived is not None and mask > 1:
            arrived.append(got)
        for place, k in enumerate(held):
            parts[k ^ mask] = got[place * value.shape[0] : (place + 1) * value.shape[0]]
    return jnp.concatenate([parts[k] for k in sorted(parts)], axis=0)


def exchange_scaled(value, axis, mask):
    largest = jnp.maximum(jnp.max(jnp.abs(value)), 1e-30)
    scale = jnp.broadcast_to(largest, (8, LANES))
    got_scale = exchange(scale, axis, mask)
    got = exchange((value * (1.0 / largest)).astype(jnp.float16), axis, mask)
    return got.astype(jnp.float32) * got_scale[0, 0]


def scatter_rows(make, scaled=False, after=None):
    shards = lax.axis_size("shard")
    parts = {}
    for pair in reversed(range(0, shards, 2)):
        value = make(pair, pair + 2)
        rows = value.shape[0] // 2
        parts[pair] = value[:rows] + exchange(value[rows:], "shard", 1)
    return scatter_far(parts, rows, scaled, after)


def scatter_near(value):
    shards = lax.axis_size("shard")
    rows = value.shape[0] // shards
    blocks = [value[k * rows : (k + 1) * rows] for k in range(shards)]
    got = exchange(jnp.concatenate(blocks[1::2], axis=0), "shard", 1)
    return {
        2 * k: blocks[2 * k] + got[k * rows : (k + 1) * rows] for k in range(shards // 2)
    }


def scatter_far(parts, rows, scaled=False, after=None):
    parts = dict(parts)
    for mask in masks_of("shard")[1:]:
        sent = [k for k in sorted(parts) if k & mask]
        block = jnp.concatenate([parts[k] for k in sent], axis=0)
        if scaled:
            got = exchange_scaled(block, "shard", mask)
        else:
            got = wide(exchange(low(block), "shard", mask))
        if after is not None:
            got = tied(got, after)
        for place, k in enumerate(sent):
            parts[k ^ mask] = parts[k ^ mask] + got[place * rows : (place + 1) * rows]
            del parts[k]
    return parts[0]


def sum_columns(value):
    shards = lax.axis_size("shard")
    count = value.shape[1] // shards
    for mask in masks_of("shard"):
        got = exchange(value, "shard", mask)
        order = [k ^ mask for k in range(shards)]
        value = value + jnp.concatenate(
            [got[:, k * count : (k + 1) * count] for k in order], axis=1
        )
    return value


def tied(values, after):
    return lax.optimization_barrier((values, after))[0]


def assemble_kernel(plan, count, at_ref, *refs):
    pieces, outs = refs[:count], refs[count : -1 - len(plan)]
    held, sems = refs[-1 - len(plan) : -1], refs[-1]
    fetches, stores = [], []
    for place, (piece, part, target, row, col, shape) in enumerate(plan):
        first = pl.multiple_of(at_ref[row], 16) if row is not None else 0
        left = pl.multiple_of(at_ref[col], LANES) if col is not None else 0
        fetch = pltpu.make_async_copy(
            pieces[piece].at[:, pl.ds(part * shape[1], shape[1])], held[place], sems.at[0, place]
        )
        fetch.start()
        fetches.append(fetch)
        stores.append(
            pltpu.make_async_copy(
                held[place],
                outs[target].at[pl.ds(first, shape[0]), pl.ds(left, shape[1])],
                sems.at[1, place],
            )
        )
    for fetch, store in zip(fetches, stores):
        fetch.wait()
        store.start()
    for store in stores:
        store.wait()


def assemble(pieces, plan, offsets, shapes):
    kind = pieces[0].dtype
    moved = sum(shape[0] * shape[1] * kind.itemsize for shape in shapes)
    any_space = pl.BlockSpec(memory_space=pl.ANY)
    return pl.pallas_call(
        functools.partial(assemble_kernel, plan, len(pieces)),
        name="assemble",
        in_specs=[pl.BlockSpec(memory_space=pltpu.SMEM)] + [any_space] * len(pieces),
        out_specs=[any_space] * len(shapes),
        out_shape=[jax.ShapeDtypeStruct(shape, kind) for shape in shapes],
        scratch_shapes=[pltpu.VMEM(entry[5], kind) for entry in plan]
        + [pltpu.SemaphoreType.DMA((2, len(plan)))],
        compiler_params=pltpu.CompilerParams(vmem_limit_bytes=48 * 1024 * 1024),
        cost_estimate=pl.CostEstimate(flops=0, bytes_accessed=2 * moved, transcendentals=0),
    )(jnp.stack(offsets).astype(jnp.int32), *pieces)


def column_part(weight, groups, group, target, first, count):
    columns = weight.shape[1] // (groups * lax.axis_size("shard"))
    at = (first, (group * lax.axis_size("shard") + target) * columns)
    return low(lax.dynamic_slice(weight, at, (count, columns)))


def halves_out(weight, groups, group):
    shards, mine = lax.axis_size("shard"), lax.axis_index("shard")
    rows = weight.shape[0]
    side = (lax.axis_index("seq") & 1) * (rows // 2)
    sent = [column_part(weight, groups, group, mine ^ 1, 0, rows)]
    return sent + [
        column_part(weight, groups, group, mine ^ k, side, rows // 2) for k in range(2, shards)
    ]


def halves_in(weight, groups, group, got, other):
    shards, mine = lax.axis_size("shard"), lax.axis_index("shard")
    rows = weight.shape[0]
    half = rows // 2
    side = (lax.axis_index("seq") & 1) * half
    own = column_part(weight, groups, group, mine, 0, rows)
    pieces = [own] + got + other
    offsets = [mine * rows, (mine ^ 1) * rows]
    offsets += [(mine ^ k) * rows + side for k in range(2, shards)]
    offsets += [(mine ^ k) * rows + half - side for k in range(2, shards)]
    plan = [(place, 0, 0, place, None, piece.shape) for place, piece in enumerate(pieces)]
    return assemble(pieces, plan, offsets, [(shards * rows, own.shape[1])])[0]


def recut(groups, after):
    shards, mine = lax.axis_size("shard"), lax.axis_index("shard")
    peers, range_at = lax.axis_size("seq"), lax.axis_index("seq")
    rows = groups[0][0].shape[0]
    fetched = rows // peers

    def part(target, first, count):
        pieces = [column_part(*group, target, first, count) for group in groups]
        return jnp.concatenate(pieces, axis=1)

    far = [part(mine ^ k, range_at * fetched, fetched) for k in range(2, shards)]
    far = [exchange(piece, "shard", k + 2) for k, piece in enumerate(tied(far, after))]
    near = exchange(part(mine ^ 1, 0, rows), "shard", 1)
    return part(mine, 0, rows), near, far


def gathered(pieces):
    return lax.all_gather(jnp.concatenate(pieces, axis=1), "seq", axis=0, tiled=True)


def recut_end(own, near, far, count, width, first=0):
    shards, mine = lax.axis_size("shard"), lax.axis_index("shard")
    rows = own.shape[0]
    plan, offsets = [], []
    for k in range(shards):
        offsets.append((mine ^ k) * rows)
        for group in range(count):
            part = first + group if k < 2 else (k - 2) * count + group
            plan.append((min(k, 2), part, group, k, None, (rows, width)))
    return assemble([own, near, far], plan, offsets, [(shards * rows, width)] * count)


def with_bit(blocks, bit):
    return [b for b in range(blocks) if not b >> bit & 1]


def halve(value, left, bit, sent_type):
    mine = (lax.axis_index("seq") >> bit) & 1
    inner = 1 << sorted(left).index(bit)
    blocks, rows, columns = value.shape
    shaped = value.reshape(blocks // (2 * inner), 2, inner * rows, columns)
    sent = lax.dynamic_index_in_dim(shaped, 1 - mine, 1, keepdims=False).astype(sent_type)
    kept = lax.dynamic_index_in_dim(shaped, mine, 1, keepdims=False)
    left.remove(bit)
    return sent, kept


def split_columns(left, bit):
    peers = lax.axis_size("seq")
    mine = (lax.axis_index("seq") >> bit) & 1
    rows = left.shape[1] // peers

    def half(which):
        pieces = [
            lax.dynamic_slice_in_dim(left, (b + (which << bit)) * rows, rows, axis=1)
            for b in with_bit(peers, bit)
        ]
        return jnp.concatenate(pieces, axis=1)

    return half(1 - mine), half(mine)


class WeightGrad:
    def __init__(self, halves, right):
        self.halves, self.right = halves, right
        self.remaining = [mask.bit_length() - 1 for mask in masks_of("seq")]
        self.rows = 2 * halves[0].shape[1] // lax.axis_size("seq")
        self.total = None

    def ready(self, after=None):
        bit = self.remaining[0]
        if self.total is None:
            if after is not None:
                self.right = tied(self.right, after)
            self.sent = low(dot_first(self.halves[0], self.right))
            self.remaining.remove(bit)
        else:
            self.sent, self.kept = halve(self.total, self.remaining, bit, jnp.bfloat16)
        self.got = exchange(self.sent, "seq", 1 << bit)
        return self.sent

    def add(self, after=None):
        got = self.got if after is None else tied(self.got, after)
        if self.total is None:
            total = dot_first(self.halves[1], self.right) + wide(got)
        else:
            total = self.kept + wide(got).reshape(self.kept.shape)
        self.total = total.reshape(-1, self.rows, self.right.shape[1])

    def step(self, after=None):
        self.add(after)
        return self.ready()

    def end(self, after=None):
        self.add(after)
        while self.remaining:
            self.ready()
            self.add()
        self.done = self.total.reshape(self.total.shape[1:])
        return self.done


def rows_of_columns(blocks, groups):
    shards, mine = lax.axis_size("shard"), lax.axis_index("shard")
    parts = len(blocks) // groups
    rows = blocks[0].shape[0] // shards
    columns = blocks[0].shape[1]

    def part(target):
        return jnp.concatenate(
            [lax.dynamic_slice_in_dim(block, target * rows, rows, axis=0) for block in blocks],
            axis=1,
        )

    pieces = [part(mine)] + [exchange(part(mine ^ k), "shard", k) for k in range(1, shards)]
    offsets = [
        (group * shards + (mine ^ k)) * columns * parts
        for k in range(shards)
        for group in range(groups)
    ]
    shape = (rows, columns * parts)
    plan = [
        (k, group, 0, None, k * groups + group, shape)
        for k in range(shards)
        for group in range(groups)
    ]
    return assemble(pieces, plan, offsets, [(rows, groups * shards * columns * parts)])[0]


def small_grads(value, gains):
    peers, shards = lax.axis_size("seq"), lax.axis_size("shard")
    rows = value.shape[0] // peers
    width = value.shape[1]
    packed = jnp.transpose(gains.reshape(2, peers, shards, -1), (1, 0, 3, 2))
    value = jnp.concatenate([value, packed.reshape(value.shape[0], shards)], axis=1)
    total = value.reshape(peers, rows, width + shards)
    left = [mask.bit_length() - 1 for mask in masks_of("seq")]
    for bit in list(left):
        sent, kept = halve(total, left, bit, jnp.float32)
        total = (kept + exchange(sent, "seq", 1 << bit)).reshape(-1, rows, width + shards)
    total = total.reshape(rows, width + shards)
    gain_sum = total[:, width:]
    for mask in masks_of("shard"):
        gain_sum = gain_sum + exchange(gain_sum, "shard", mask)
    gain_sum = lax.dynamic_index_in_dim(gain_sum, lax.axis_index("shard"), 1, keepdims=False)
    pairs = [(s * shards + h, h * peers + s) for s in range(peers) for h in range(shards)]
    return lax.ppermute(total[:, :width], ("seq", "shard"), pairs), gain_sum.reshape(2, -1)


def spread(source, target, length):
    for c in range(source.shape[-1] // LANES):
        target[pl.ds(c * length, length), :] = wide(source[0, :, c * LANES : (c + 1) * LANES])


def collect(source, target, length):
    for c in range(target.shape[-1] // LANES):
        target[0, :, c * LANES : (c + 1) * LANES] = source[pl.ds(c * length, length), :]


def token_rows(ref, token, blocks, length):
    return ref[pl.ds(token, blocks, stride=length), :]


def sum_blocks(values):
    blocks = values[0].shape[0]
    if blocks != GROUP:
        return jnp.concatenate([jnp.sum(v, axis=0, keepdims=True) for v in values], axis=0)
    row = lax.broadcasted_iota(jnp.int32, (GROUP, LANES), 0)
    upper = row < 4
    level = [
        jnp.where(upper, values[j], values[j + 4])
        + pltpu.roll(jnp.where(upper, values[j + 4], values[j]), 4, 0)
        for j in range(4)
    ]
    for step in (2, 1):
        first = (row & step) == 0
        level = [
            jnp.where(
                first,
                level[j] + pltpu.roll(level[j], GROUP - step, 0),
                level[j + step] + pltpu.roll(level[j + step], step, 0),
            )
            for j in range(step)
        ]
    return level[0]


def end_kernel(length, blocks, rows_ref, rate_ref, signal_ref, a_ref, state_ref, total_ref, rate, signal):
    spread(rate_ref, rate, length)
    spread(signal_ref, signal, length)
    state_ref[...] = jnp.zeros_like(state_ref)

    def group(i, total):
        start = i * GROUP
        rates = [token_rows(rate, start + j, blocks, length) for j in range(GROUP)]
        drives = [
            rates[j] * token_rows(signal, start + j, blocks, length) for j in range(GROUP)
        ]
        for n in range(N):
            state, a = state_ref[0, n], a_ref[n]
            for j in range(GROUP):
                state = jnp.exp2(rates[j] * a) * state + drives[j] * rows_ref[0, 0, n * length + start + j]
            state_ref[0, n] = state
        for j in range(GROUP):
            total = total + rates[j]
        return total

    total_ref[0, 0] = lax.fori_loop(
        0, length // GROUP, group, jnp.zeros((blocks, LANES), jnp.float32)
    )


def scan_kernel(
    length, blocks, rows_ref, rate_ref, signal_ref, a_ref, in_ref, out_ref, state_ref, rate, signal, out
):
    spread(rate_ref, rate, length)
    spread(signal_ref, signal, length)
    state_ref[...] = in_ref[0]

    def group(i, carry):
        start = i * GROUP
        rates = [token_rows(rate, start + j, blocks, length) for j in range(GROUP)]
        drives = [
            rates[j] * token_rows(signal, start + j, blocks, length) for j in range(GROUP)
        ]
        outs = [None] * GROUP
        for n in range(N):
            state, a = state_ref[n], a_ref[n]
            for j in range(GROUP):
                state = jnp.exp2(rates[j] * a) * state + drives[j] * rows_ref[0, 0, n * length + start + j]
                term = state * rows_ref[0, 0, (N + n) * length + start + j]
                outs[j] = term if outs[j] is None else outs[j] + term
            state_ref[n] = state
        for j in range(GROUP):
            out[pl.ds(start + j, blocks, stride=length), :] = outs[j]
        return carry

    lax.fori_loop(0, length // GROUP, group, 0)
    collect(out, out_ref, length)


def seed_kernel(length, blocks, rows_ref, rate_ref, up_ref, a_ref, seed_ref, rate, up):
    spread(rate_ref, rate, length)
    spread(up_ref, up, length)
    seed_ref[...] = jnp.zeros_like(seed_ref)

    def group(i, carry):
        start = length - GROUP - i * GROUP
        rates = [token_rows(rate, start + j, blocks, length) for j in range(GROUP)]
        ups = [token_rows(up, start + j, blocks, length) for j in range(GROUP)]
        for n in range(N):
            back, a = seed_ref[0, n], a_ref[n]
            for j in reversed(range(GROUP)):
                back = jnp.exp2(rates[j] * a) * (
                    back + ups[j] * rows_ref[0, 0, (N + n) * length + start + j]
                )
            seed_ref[0, n] = back
        return carry

    lax.fori_loop(0, length // GROUP, group, 0)


def grad_kernel(
    length,
    blocks,
    rows_ref,
    rate_ref,
    signal_ref,
    up_ref,
    a_ref,
    in_ref,
    back_ref,
    a_before_ref,
    rate_grad_ref,
    signal_grad_ref,
    rows_grad_ref,
    a_grad_ref,
    states,
    back_state,
    rate,
    signal,
    up,
    rate_grad,
    signal_grad,
):
    spread(rate_ref, rate, length)
    spread(signal_ref, signal, length)
    spread(up_ref, up, length)
    for n in range(N):
        states[n, 0] = in_ref[0, n]
    back_state[...] = back_ref[0]

    @pl.when(pl.program_id(0) == 0)
    def _():
        a_grad_ref[...] = a_before_ref[...]

    def forward(i, carry):
        start = i * GROUP
        rates = [token_rows(rate, start + j, blocks, length) for j in range(GROUP)]
        drives = [
            rates[j] * token_rows(signal, start + j, blocks, length) for j in range(GROUP)
        ]
        for n in range(N):
            state, a = states[n, start], a_ref[n]
            for j in range(GROUP):
                state = jnp.exp2(rates[j] * a) * state + drives[j] * rows_ref[0, 0, n * length + start + j]
                states[n, start + j + 1] = state
        return carry

    lax.fori_loop(0, length // GROUP, forward, 0)

    def backward(i, carry):
        start = length - GROUP - i * GROUP
        rates = [token_rows(rate, start + j, blocks, length) for j in range(GROUP)]
        signals = [token_rows(signal, start + j, blocks, length) for j in range(GROUP)]
        ups = [token_rows(up, start + j, blocks, length) for j in range(GROUP)]
        through = [None] * GROUP
        slope = [None] * GROUP
        for n in range(N):
            back, a = back_state[n], a_ref[n]
            a_sum = None
            to_b = [None] * GROUP
            to_c = [None] * GROUP
            for j in reversed(range(GROUP)):
                b = rows_ref[0, 0, n * length + start + j]
                c = rows_ref[0, 0, (N + n) * length + start + j]
                here = back + ups[j] * c
                back = jnp.exp2(rates[j] * a) * here
                moved = back * states[n, start + j]
                a_term = moved * rates[j]
                a_sum = a_term if a_sum is None else a_sum + a_term
                b_term, a_slope = here * b, moved * a
                through[j] = b_term if through[j] is None else through[j] + b_term
                slope[j] = a_slope if slope[j] is None else slope[j] + a_slope
                to_b[j] = here * (rates[j] * signals[j])
                to_c[j] = ups[j] * states[n, start + j + 1]
            back_state[n] = back
            a_grad_ref[n] = a_grad_ref[n] + a_sum
            at = pl.ds(pl.multiple_of(start, GROUP), GROUP)
            rows_grad_ref[0, n, at, :] = sum_blocks(to_b)
            rows_grad_ref[0, N + n, at, :] = sum_blocks(to_c)
        for j in range(GROUP):
            rows = pl.ds(start + j, blocks, stride=length)
            rate_grad[rows, :] = through[j] * signals[j] + slope[j] * ln_2
            signal_grad[rows, :] = through[j] * rates[j]
        return carry

    lax.fori_loop(0, length // GROUP, backward, 0)
    collect(rate_grad, rate_grad_ref, length)
    collect(signal_grad, signal_grad_ref, length)


def scan_call(kernel, name, sequences, length, channels, inputs, outputs, scratch, after=(), part=(0, 1), before=None):
    blocks = channels // LANES
    count = sequences // part[1]
    at = part[0] * count
    before = [] if before is None else list(before)
    kinds = {
        "rows": ((1, 1, 2 * N * length), lambda s: (at + s, 0, 0)),
        "tokens": ((1, length, channels), lambda s: (at + s, 0, 0)),
        "states": ((1, N, blocks, LANES), lambda s: (at + s, 0, 0, 0)),
        "total": ((1, 1, blocks, LANES), lambda s: (at + s, 0, 0, 0)),
        "fixed": ((N, blocks, LANES), lambda s: (0, 0, 0)),
        "rows_grad": ((1, 2 * N, length, LANES), lambda s: (at + s, 0, 0, 0)),
    }

    def spec(kind):
        shape, index = kinds[kind]
        if kind == "rows":
            return pl.BlockSpec(shape, index, memory_space=pltpu.SMEM)
        return pl.BlockSpec(shape, index)

    def whole(kind):
        shape = kinds[kind][0]
        if kind != "fixed":
            shape = (sequences,) + shape[1:]
        return jax.ShapeDtypeStruct(shape, jnp.float32)

    def space(kind):
        if kind == "tokens":
            return pltpu.VMEM((blocks * length, LANES), jnp.float32)
        if kind == "history":
            return pltpu.VMEM((N, length + 1, blocks, LANES), jnp.float32)
        return pltpu.VMEM((N, blocks, LANES), jnp.float32)

    values = [value for _, value in inputs]
    values = tied(values, list(after))
    def body(*refs):
        kernel(length, blocks, *refs[: len(inputs)], *refs[len(inputs) + len(before) :])

    return pl.pallas_call(
        body,
        name=name,
        grid=(count,),
        in_specs=[spec(kind) for kind, _ in inputs]
        + [pl.BlockSpec(memory_space=pl.ANY)] * len(before),
        input_output_aliases={len(inputs) + i: i for i in range(len(before))},
        out_specs=[spec(kind) for kind in outputs],
        out_shape=[whole(kind) for kind in outputs],
        scratch_shapes=[space(kind) for kind in scratch],
        compiler_params=pltpu.CompilerParams(vmem_limit_bytes=56 * 1024 * 1024),
        cost_estimate=pl.CostEstimate(
            flops=0,
            bytes_accessed=0,
            transcendentals=0,
        ),
    )(*values, *before)


def chained(total, state, a_scaled, direction):
    peers = lax.axis_size("seq")
    second_of_pair = (lax.axis_index("seq") & 1) == (1 if direction == 1 else 0)

    def join(first, second):
        return (
            first[0] + second[0],
            jnp.exp2(second[0] * a_scaled) * first[1] + second[1],
        )

    def split(packed):
        return (packed[:, :1], packed[:, 1:])

    def chosen(flag, yes, no):
        return tuple(jnp.where(flag, a, b) for a, b in zip(yes, no))

    own = (total, state)
    mate = split(exchange(jnp.concatenate(own, axis=1), "seq", 1))
    first = chosen(second_of_pair, mate, own)
    pair = join(first, chosen(second_of_pair, own, mate))
    packed = jnp.concatenate(pair, axis=1)
    before = None
    for by in reversed(range(2, peers, 2)):
        got = split(passed_along(packed, "seq", direction * by))
        before = got if before is None else join(before, got)
    return jnp.where(second_of_pair, join(before, first)[1], before[1]), packed


def local(
    tokens,
    gain_one,
    in_weight,
    conv_weight,
    conv_bias,
    x_weight,
    dt_weight,
    dt_bias,
    a_log,
    skip_gain,
    out_weight,
    gain_two,
    ffn_in,
    ffn_down,
    cotangent,
):
    shards = lax.axis_size("shard")
    held, length, _ = tokens.shape
    sequences = held * shards
    own_rows = held * length
    row_count = sequences * length
    channels = conv_bias.shape[0]
    blocks = channels // LANES

    def by_sequence(value):
        return value.reshape(sequences, length, value.shape[-1])

    tokens_own = tokens.reshape(own_rows, D)
    up_own = cotangent.reshape(own_rows, D)
    gains_own = rounded(jnp.concatenate([gain_one, gain_two])).reshape(1, -1)
    gain_rows = jnp.pad(gains_own, ((0, 15), (0, D - gains_own.shape[1])))
    conv_sent = halves_out(in_weight, 2, 0)
    conv_got = [exchange(piece, "shard", k + 1) for k, piece in enumerate(conv_sent)]
    arrived = []
    packed = jnp.concatenate([tokens_own, gain_rows], axis=0)
    packed = gather_rows(tied(packed, conv_sent), arrived).reshape(shards, own_rows + 16, D)
    tokens_all = packed[:, :own_rows].reshape(row_count, D)
    gains = packed[:, own_rows, : gains_own.shape[1]].reshape(shards, 2, -1)
    in_turn = [
        lax.dynamic_index_in_dim(gains, lax.axis_index("shard") ^ k, 0, keepdims=False)
        for k in range(shards)
    ]
    gains = wide(jnp.concatenate(in_turn, axis=1))
    gain_norm, gain_second = gains[0], gains[1]

    conv_other = [exchange(piece, "seq", 1) for piece in conv_got[1:]]
    groups = [(in_weight, 2, 1), (out_weight, 1, 0)]
    weight_conv_in = halves_in(in_weight, 2, 0, conv_got, conv_other)
    groups += [(ffn_in, 2, 0), (ffn_in, 2, 1)]
    own, near, far = recut(groups, [arrived, weight_conv_in])
    mixer_far = gathered([piece[:, : 2 * channels] for piece in far])
    ffn_far = gathered([piece[:, 2 * channels :] for piece in far])
    weight_gate_in, weight_out = recut_end(own, near, mixer_far, 2, channels)

    conv_taps = wide(rounded(conv_weight))
    bias_conv = wide(rounded(conv_bias))
    weight_x = rounded(x_weight)
    weight_dt = rounded(dt_weight)
    bias_dt = wide(rounded(dt_bias))
    weight_skip = wide(rounded(skip_gain))
    a_matrix = -jnp.exp(wide(rounded(a_log)))
    a_scaled = (a_matrix * log2_e).T.reshape(N, blocks, LANES)

    inputs_all = wide(tokens_all)
    scale_all = lax.rsqrt(jnp.mean(inputs_all * inputs_all, axis=1, keepdims=True) + epsilon)
    normed = rounded(inputs_all * scale_all * gain_norm)
    conv_in = by_sequence(rounded(dot_plain(normed, weight_conv_in)))
    gate_mix = dot_plain(normed, weight_gate_in)
    borrowed = passed_along(conv_in[:, length - (K - 1) :], "seq", 1)
    padded = wide(jnp.concatenate([borrowed, conv_in], axis=1))
    conv_out = bias_conv + jnp.zeros((sequences, length, channels), jnp.float32)
    for offset in range(K):
        conv_out = conv_out + conv_taps[offset] * padded[:, offset : offset + length]
    conv_out = conv_out.reshape(row_count, channels)
    signal = rounded(jax.nn.silu(conv_out))
    signal_wide = wide(signal)
    selection = sum_columns(
        lax.dot_general(
            weight_x, signal, (((0,), (1,)), ((), ())), preferred_element_type=jnp.float32
        )
    )
    down_own, down_near, down_parts = recut([(ffn_down, 1, 0)], [selection])
    down_far = gathered(down_parts)
    rank_part = rounded(selection[:R])
    rows = jnp.swapaxes(selection[R:].reshape(2 * N, sequences, length), 0, 1).reshape(
        sequences, 1, 2 * N * length
    )
    pre_rate = dot_first(rank_part, weight_dt) + bias_dt
    rates = by_sequence(jax.nn.softplus(pre_rate))
    signals = by_sequence(signal)
    sizes = (sequences, length, channels)
    end_state, total_rate = scan_call(
        end_kernel,
        "scan_end",
        *sizes,
        [("rows", rows), ("tokens", rates), ("tokens", signals), ("fixed", a_scaled)],
        ["states", "total"],
        ["tokens", "tokens"],
        [near] + far,
    )
    incoming, _ = chained(total_rate, end_state, a_scaled, 1)
    ffn_width = ffn_in.shape[1] // (2 * shards)
    (scan_out,) = scan_call(
        scan_kernel,
        "scan_out",
        *sizes,
        [
            ("rows", rows),
            ("tokens", rates),
            ("tokens", signals),
            ("fixed", a_scaled),
            ("states", incoming),
        ],
        ["tokens"],
        ["fixed", "tokens", "tokens", "tokens"],
        [down_near] + down_parts,
    )
    (weight_down,) = recut_end(down_own, down_near, down_far, 1, down_own.shape[1])
    ffn_offset = 2 * channels // ffn_width
    weight_gate, weight_up = recut_end(own, near, ffn_far, 2, ffn_width, ffn_offset)
    scanned = scan_out.reshape(row_count, channels) + weight_skip * signal_wide
    gate_act = jax.nn.silu(gate_mix)
    gated = rounded(scanned * gate_act)
    inputs = wide(tokens_own)

    def mixed_rows(first, last):
        return dot_last(gated[first * own_rows : last * own_rows], weight_out)

    middle = inputs + scatter_rows(mixed_rows, True, [weight_gate, weight_up])

    scale_two = lax.rsqrt(jnp.mean(middle * middle, axis=1, keepdims=True) + epsilon)
    arrived = []
    normed_two = gather_rows(rounded(middle * scale_two * gain_second), arrived)
    up_all = gather_rows(tied(up_own, arrived))
    gate_part = dot_plain(normed_two, weight_gate)
    up_part = dot_plain(normed_two, weight_up)
    gate_silu = jax.nn.silu(gate_part)
    activated = rounded(gate_silu * up_part)
    columns = activated.shape[1] // 2
    up_halves = split_columns(up_all, 0)
    down_first = WeightGrad(up_halves, activated[:, :columns])
    down_second = WeightGrad(up_halves, activated[:, columns:])
    up_late = tied(up_all, down_first.ready())
    act_grad = dot_plain(up_late, weight_down)
    gate_grad = rounded(act_grad * up_part * silu_slope(gate_part))
    up_grad = rounded(act_grad * gate_silu)
    gate_late, up_grad_late = tied((gate_grad, up_grad), down_second.ready(gate_grad))

    def normed_two_rows(first, last):
        at = slice(first * own_rows, last * own_rows)
        return dot_last(gate_late[at], weight_gate) + dot_last(up_grad_late[at], weight_up)

    normed_two_grad = scatter_rows(normed_two_rows)
    two_halves = split_columns(normed_two, 0)
    gate_first = WeightGrad(two_halves, gate_grad[:, :columns])
    gate_second = WeightGrad(two_halves, gate_grad[:, columns:])
    up_first = WeightGrad(two_halves, up_grad[:, :columns])
    up_second = WeightGrad(two_halves, up_grad[:, columns:])
    gain_two_grad = jnp.sum(normed_two_grad * middle * scale_two, axis=0)
    scaled_two = normed_two_grad * gain_second
    middle_grad = (
        wide(up_own)
        + scale_two * scaled_two
        - middle
        * (scale_two * scale_two * scale_two)
        * jnp.mean(scaled_two * middle, axis=1, keepdims=True)
    )
    mixed_grad = gather_rows(rounded(middle_grad))
    steps = [down_first.step(middle_grad), gate_first.ready(middle_grad)]
    mixed_late = tied(mixed_grad, steps)

    gated_grad = dot_plain(mixed_late, weight_out)
    scan_grad = gated_grad * gate_act
    gate_mix_grad = rounded(gated_grad * scanned * silu_slope(gate_mix))
    skip_grad = jnp.sum(scan_grad * signal_wide, axis=0)
    ups = by_sequence(scan_grad)
    steps = [down_second.step(ups)]
    (seed,) = scan_call(
        seed_kernel,
        "scan_seed",
        *sizes,
        [("rows", rows), ("tokens", rates), ("tokens", ups), ("fixed", a_scaled)],
        ["states"],
        ["tokens", "tokens"],
        steps,
    )
    returning, first_round = chained(total_rate, seed, a_scaled, -1)
    steps = [gate_second.ready(first_round)]
    steps += [up_first.ready(returning), down_first.step(returning)]
    steps += [gate_first.step(returning), down_second.step(returning)]
    mixed_halves = split_columns(mixed_grad, 0)
    normed_halves = split_columns(normed, 0)
    out_sum = WeightGrad(mixed_halves, gated)
    in_gate_sum = WeightGrad(normed_halves, gate_mix_grad)
    grads = None
    for part in range(2):
        grads = scan_call(
            grad_kernel,
            "scan_grad",
            *sizes,
            [
                ("rows", rows),
                ("tokens", rates),
                ("tokens", signals),
                ("tokens", ups),
                ("fixed", a_scaled),
                ("states", incoming),
                ("states", returning),
                ("fixed", jnp.zeros_like(a_scaled) if grads is None else grads[3]),
            ],
            ["tokens", "tokens", "rows_grad", "fixed"],
            ["history", "fixed", "tokens", "tokens", "tokens", "tokens", "tokens"],
            steps,
            part=(part, 2),
            before=None if grads is None else grads[:3],
        )
        if part == 0:
            token = grads[3]
            steps = [up_second.ready(token), gate_second.step(token), gate_first.step(token)]
            steps += [down_first.end(token), down_second.end(token)]
            result_parts = scatter_near(dot_last(tied(activated, token), weight_down))
            steps += list(result_parts.values())
    rate_grad, scan_signal_grad, rows_grad, a_grad = grads
    steps = [out_sum.ready(a_grad), up_first.step(a_grad), gate_second.step(a_grad)]
    steps += [gate_first.end(a_grad)]
    rate_grad = tied(rate_grad, steps)
    result = middle + scatter_far(tied(result_parts, a_grad), own_rows)
    output = rounded(result).reshape(tokens.shape)
    rate_grad = rate_grad.reshape(row_count, channels)
    pre_grad = rate_grad * jax.nn.sigmoid(pre_rate)
    pre_grad_low = rounded(pre_grad)
    rank_grad = dot_last(weight_dt, pre_grad_low)
    rows_grad = jnp.swapaxes(jnp.sum(rows_grad, axis=3), 0, 1).reshape(2 * N, row_count)
    selection_grad = rounded(sum_columns(jnp.concatenate([rank_grad, rows_grad], axis=0)))
    steps = [up_second.step(selection_grad), up_first.step(selection_grad), output]
    steps += [gate_second.end(selection_grad)]
    selection_grad = tied(selection_grad, steps)
    signal_grad = (
        scan_grad * weight_skip
        + scan_signal_grad.reshape(row_count, channels)
        + lax.dot_general(
            selection_grad, weight_x, (((0,), (1,)), ((), ())), preferred_element_type=jnp.float32
        )
    )
    conv_grad = (signal_grad * silu_slope(conv_out)).reshape(sequences, length, channels)
    padded_grad = jnp.zeros((sequences, length + K - 1, channels), jnp.float32)
    for offset in range(K):
        padded_grad = padded_grad + jnp.pad(
            conv_taps[offset] * conv_grad, ((0, 0), (offset, K - 1 - offset), (0, 0))
        )
    returned = wide(passed_along(low(padded_grad[:, : K - 1]), "seq", -1))
    in_gate_sum.ready(returned)
    conv_in_grad = rounded(
        padded_grad[:, K - 1 :] + jnp.pad(returned, ((0, 0), (length - (K - 1), 0), (0, 0)))
    ).reshape(row_count, channels)
    in_conv_sum = WeightGrad(normed_halves, conv_in_grad)
    steps = [in_conv_sum.ready(), out_sum.step(conv_in_grad), up_second.step(conv_in_grad)]
    steps += [up_first.end(conv_in_grad)]
    conv_in_grad = tied(conv_in_grad, steps)
    normed_grad_parts = {}
    conv_in_late = tied(conv_in_grad, [in_gate_sum.step(conv_in_grad)])

    def normed_rows(first, last):
        at = slice(first * own_rows, last * own_rows)
        part = dot_last(conv_in_late[at], weight_conv_in) + dot_last(
            gate_mix_grad[at], weight_gate_in
        )
        normed_grad_parts[first] = jnp.sum(part * inputs_all[at] * scale_all[at], axis=0)
        return part

    normed_grad = scatter_rows(normed_rows)
    gain_one_grad = sum(normed_grad_parts.values())
    steps = [in_conv_sum.step(gain_one_grad), out_sum.step(gain_one_grad)]
    gain_one_grad = tied(gain_one_grad, steps)
    scale_one = scale_all[:own_rows]
    scaled_one = normed_grad * gain_norm
    input_grad = (
        middle_grad
        + scale_one * scaled_one
        - inputs
        * (scale_one * scale_one * scale_one)
        * jnp.mean(scaled_one * inputs, axis=1, keepdims=True)
    )


    conv_weight_grad = jnp.stack(
        [
            jnp.sum(conv_grad * padded[:, offset : offset + length], axis=(0, 1))
            for offset in range(K)
        ],
        axis=1,
    )
    column_sums = jnp.stack(
        [jnp.sum(conv_grad, axis=(0, 1)), jnp.sum(pre_grad, axis=0), skip_grad], axis=1
    )
    a_log_grad = a_grad.reshape(N, channels).T * a_matrix
    dt_weight_grad = lax.dot_general(
        pre_grad_low, rank_part, (((0,), (1,)), ((), ())), preferred_element_type=jnp.float32
    )
    x_weight_grad = lax.dot_general(
        signal, selection_grad, (((0,), (1,)), ((), ())), preferred_element_type=jnp.float32
    )
    small, gain_grads = small_grads(
        jnp.concatenate(
            [dt_weight_grad, x_weight_grad, a_log_grad, conv_weight_grad, column_sums], axis=1
        ),
        jnp.stack([gain_one_grad, gain_two_grad]),
    )
    at = R + R + 2 * N

    ffn_down_result = rows_of_columns([down_first.done, down_second.done], 1)
    ffn_in_result = rows_of_columns(
        [
            gate_first.done,
            gate_second.done,
            up_first.done,
            up_second.end(gain_one_grad),
        ],
        2,
    )
    out_result = rows_of_columns([out_sum.end()], 1)
    in_result = rows_of_columns([in_conv_sum.end(), in_gate_sum.end()], 2)
    return (
        output,
        rounded(input_grad).reshape(tokens.shape),
        gain_grads[0],
        in_result,
        small[:, at + N : at + N + K].T,
        small[:, at + N + K],
        small[:, R:at],
        small[:, :R].T,
        small[:, at + N + K + 1],
        small[:, at : at + N],
        small[:, at + N + K + 2],
        out_result,
        gain_grads[1],
        ffn_in_result,
        ffn_down_result,
    )


def solution(mesh):
    in_specs = (
        P("shard", "seq", None),
        P("shard"),
        P("shard", None),
        P(None, "shard"),
        P("shard"),
        P("shard", None),
        P(None, "shard"),
        P("shard"),
        P("shard", None),
        P("shard"),
        P("shard", None),
        P("shard"),
        P("shard", None),
        P("shard", None),
        P("shard", "seq", None),
    )
    out_specs = (
        P("shard", "seq", None),
        P("shard", "seq", None),
        P(("seq", "shard")),
        P(("seq", "shard"), None),
        P(None, ("seq", "shard")),
        P(("seq", "shard")),
        P(("seq", "shard"), None),
        P(None, ("seq", "shard")),
        P(("seq", "shard")),
        P(("seq", "shard"), None),
        P(("seq", "shard")),
        P(("seq", "shard"), None),
        P(("seq", "shard")),
        P(("seq", "shard"), None),
        P(("seq", "shard"), None),
    )
    return jax.shard_map(local, mesh=mesh, in_specs=in_specs, out_specs=out_specs, check_vma=False)
```

```python
import functools
import math

import jax
import jax.numpy as jnp
from jax import lax
from jax.experimental import pallas as pl
from jax.experimental.pallas import tpu as pltpu
from jax.sharding import PartitionSpec as P

D = 2048
E = 4096
N = 16
K = 4
R = 128
FF = 8192

LANES = 128
GROUP = 8

epsilon = 1e-05
log2_e = math.log2(math.e)
ln_2 = math.log(2.0)


def silu_slope(value):
    sigma = jax.nn.sigmoid(value)
    return sigma * (1.0 + value * (1.0 - sigma))


def dot_last(left, right):
    return lax.dot_general(
        left, right, (((1,), (1,)), ((), ())), preferred_element_type=jnp.float32
    )


def dot_first(left, right):
    return lax.dot_general(
        left, right, (((0,), (0,)), ((), ())), preferred_element_type=jnp.float32
    )


def dot_plain(left, right):
    return jnp.dot(left, right, preferred_element_type=jnp.float32)


def wide(value):
    return value.astype(jnp.float32)


def low(value):
    return value.astype(jnp.bfloat16)


def rounded(value):
    return lax.reduce_precision(value, 8, 7).astype(jnp.bfloat16)


def exchange(value, axis, mask):
    return lax.ppermute(value, axis, [(i, i ^ mask) for i in range(lax.axis_size(axis))])


def passed_along(value, axis, by):
    peers = lax.axis_size(axis)
    pairs = [(i, i + by) for i in range(peers) if 0 <= i + by < peers]
    return lax.ppermute(value, axis, pairs)


def masks_of(axis):
    size = lax.axis_size(axis)
    return [1 << bit for bit in range(size.bit_length() - 1)]


def gather_rows(value, arrived=None):
    parts = {0: value}
    for mask in reversed(masks_of("shard")):
        held = sorted(parts)
        got = exchange(jnp.concatenate([parts[k] for k in held], axis=0), "shard", mask)
        if arrived is not None and mask > 1:
            arrived.append(got)
        for place, k in enumerate(held):
            parts[k ^ mask] = got[place * value.shape[0] : (place + 1) * value.shape[0]]
    return jnp.concatenate([parts[k] for k in sorted(parts)], axis=0)


def exchange_scaled(value, axis, mask):
    largest = jnp.maximum(jnp.max(jnp.abs(value)), 1e-30)
    scale = jnp.broadcast_to(largest, (8, LANES))
    got_scale = exchange(scale, axis, mask)
    got = exchange((value * (1.0 / largest)).astype(jnp.float16), axis, mask)
    return got.astype(jnp.float32) * got_scale[0, 0]


def scatter_rows(make, scaled=False, after=None):
    shards = lax.axis_size("shard")
    parts = {}
    for pair in reversed(range(0, shards, 2)):
        value = make(pair, pair + 2)
        rows = value.shape[0] // 2
        parts[pair] = value[:rows] + exchange(value[rows:], "shard", 1)
    return scatter_far(parts, rows, scaled, after)


def scatter_near(value):
    shards = lax.axis_size("shard")
    rows = value.shape[0] // shards
    blocks = [value[k * rows : (k + 1) * rows] for k in range(shards)]
    got = exchange(jnp.concatenate(blocks[1::2], axis=0), "shard", 1)
    return {
        2 * k: blocks[2 * k] + got[k * rows : (k + 1) * rows] for k in range(shards // 2)
    }


def scatter_far(parts, rows, scaled=False, after=None):
    parts = dict(parts)
    for mask in masks_of("shard")[1:]:
        sent = [k for k in sorted(parts) if k & mask]
        block = jnp.concatenate([parts[k] for k in sent], axis=0)
        if scaled:
            got = exchange_scaled(block, "shard", mask)
        else:
            got = wide(exchange(low(block), "shard", mask))
        if after is not None:
            got = tied(got, after)
        for place, k in enumerate(sent):
            parts[k ^ mask] = parts[k ^ mask] + got[place * rows : (place + 1) * rows]
            del parts[k]
    return parts[0]


def sum_columns(value):
    shards = lax.axis_size("shard")
    count = value.shape[1] // shards
    for mask in masks_of("shard"):
        got = exchange(value, "shard", mask)
        order = [k ^ mask for k in range(shards)]
        value = value + jnp.concatenate(
            [got[:, k * count : (k + 1) * count] for k in order], axis=1
        )
    return value


def tied(values, after):
    return lax.optimization_barrier((values, after))[0]


def assemble_kernel(plan, count, at_ref, *refs):
    pieces, outs = refs[:count], refs[count : -1 - len(plan)]
    held, sems = refs[-1 - len(plan) : -1], refs[-1]
    fetches, stores = [], []
    for place, (piece, part, target, row, col, shape) in enumerate(plan):
        first = pl.multiple_of(at_ref[row], 16) if row is not None else 0
        left = pl.multiple_of(at_ref[col], LANES) if col is not None else 0
        fetch = pltpu.make_async_copy(
            pieces[piece].at[:, pl.ds(part * shape[1], shape[1])], held[place], sems.at[0, place]
        )
        fetch.start()
        fetches.append(fetch)
        stores.append(
            pltpu.make_async_copy(
                held[place],
                outs[target].at[pl.ds(first, shape[0]), pl.ds(left, shape[1])],
                sems.at[1, place],
            )
        )
    for fetch, store in zip(fetches, stores):
        fetch.wait()
        store.start()
    for store in stores:
        store.wait()


def assemble(pieces, plan, offsets, shapes):
    kind = pieces[0].dtype
    moved = sum(shape[0] * shape[1] * kind.itemsize for shape in shapes)
    any_space = pl.BlockSpec(memory_space=pl.ANY)
    return pl.pallas_call(
        functools.partial(assemble_kernel, plan, len(pieces)),
        name="assemble",
        in_specs=[pl.BlockSpec(memory_space=pltpu.SMEM)] + [any_space] * len(pieces),
        out_specs=[any_space] * len(shapes),
        out_shape=[jax.ShapeDtypeStruct(shape, kind) for shape in shapes],
        scratch_shapes=[pltpu.VMEM(entry[5], kind) for entry in plan]
        + [pltpu.SemaphoreType.DMA((2, len(plan)))],
        compiler_params=pltpu.CompilerParams(vmem_limit_bytes=48 * 1024 * 1024),
        cost_estimate=pl.CostEstimate(flops=0, bytes_accessed=2 * moved, transcendentals=0),
    )(jnp.stack(offsets).astype(jnp.int32), *pieces)


def column_part(weight, groups, group, target, first, count):
    columns = weight.shape[1] // (groups * lax.axis_size("shard"))
    at = (first, (group * lax.axis_size("shard") + target) * columns)
    return low(lax.dynamic_slice(weight, at, (count, columns)))


def halves_out(weight, groups, group):
    shards, mine = lax.axis_size("shard"), lax.axis_index("shard")
    rows = weight.shape[0]
    side = (lax.axis_index("seq") & 1) * (rows // 2)
    sent = [column_part(weight, groups, group, mine ^ 1, 0, rows)]
    return sent + [
        column_part(weight, groups, group, mine ^ k, side, rows // 2) for k in range(2, shards)
    ]


def halves_in(weight, groups, group, got, other):
    shards, mine = lax.axis_size("shard"), lax.axis_index("shard")
    rows = weight.shape[0]
    half = rows // 2
    side = (lax.axis_index("seq") & 1) * half
    own = column_part(weight, groups, group, mine, 0, rows)
    pieces = [own] + got + other
    offsets = [mine * rows, (mine ^ 1) * rows]
    offsets += [(mine ^ k) * rows + side for k in range(2, shards)]
    offsets += [(mine ^ k) * rows + half - side for k in range(2, shards)]
    plan = [(place, 0, 0, place, None, piece.shape) for place, piece in enumerate(pieces)]
    return assemble(pieces, plan, offsets, [(shards * rows, own.shape[1])])[0]


def recut(groups, after):
    shards, mine = lax.axis_size("shard"), lax.axis_index("shard")
    peers, range_at = lax.axis_size("seq"), lax.axis_index("seq")
    rows = groups[0][0].shape[0]
    fetched = rows // peers

    def part(target, first, count):
        pieces = [column_part(*group, target, first, count) for group in groups]
        return jnp.concatenate(pieces, axis=1)

    far = [part(mine ^ k, range_at * fetched, fetched) for k in range(2, shards)]
    far = [exchange(piece, "shard", k + 2) for k, piece in enumerate(tied(far, after))]
    near = exchange(part(mine ^ 1, 0, rows), "shard", 1)
    return part(mine, 0, rows), near, far


def gathered(pieces):
    return lax.all_gather(jnp.concatenate(pieces, axis=1), "seq", axis=0, tiled=True)


def recut_end(own, near, far, count, width, first=0):
    shards, mine = lax.axis_size("shard"), lax.axis_index("shard")
    rows = own.shape[0]
    plan, offsets = [], []
    for k in range(shards):
        offsets.append((mine ^ k) * rows)
        for group in range(count):
            part = first + group if k < 2 else (k - 2) * count + group
            plan.append((min(k, 2), part, group, k, None, (rows, width)))
    return assemble([own, near, far], plan, offsets, [(shards * rows, width)] * count)


def with_bit(blocks, bit):
    return [b for b in range(blocks) if not b >> bit & 1]


def halve(value, left, bit, sent_type):
    mine = (lax.axis_index("seq") >> bit) & 1
    inner = 1 << sorted(left).index(bit)
    blocks, rows, columns = value.shape
    shaped = value.reshape(blocks // (2 * inner), 2, inner * rows, columns)
    sent = lax.dynamic_index_in_dim(shaped, 1 - mine, 1, keepdims=False).astype(sent_type)
    kept = lax.dynamic_index_in_dim(shaped, mine, 1, keepdims=False)
    left.remove(bit)
    return sent, kept


def split_columns(left, bit):
    peers = lax.axis_size("seq")
    mine = (lax.axis_index("seq") >> bit) & 1
    rows = left.shape[1] // peers

    def half(which):
        pieces = [
            lax.dynamic_slice_in_dim(left, (b + (which << bit)) * rows, rows, axis=1)
            for b in with_bit(peers, bit)
        ]
        return jnp.concatenate(pieces, axis=1)

    return half(1 - mine), half(mine)


class WeightGrad:
    def __init__(self, halves, right):
        self.halves, self.right = halves, right
        self.remaining = [mask.bit_length() - 1 for mask in masks_of("seq")]
        self.rows = 2 * halves[0].shape[1] // lax.axis_size("seq")
        self.total = None

    def ready(self, after=None):
        bit = self.remaining[0]
        if self.total is None:
            if after is not None:
                self.right = tied(self.right, after)
            self.sent = low(dot_first(self.halves[0], self.right))
            self.remaining.remove(bit)
        else:
            self.sent, self.kept = halve(self.total, self.remaining, bit, jnp.bfloat16)
        self.got = exchange(self.sent, "seq", 1 << bit)
        return self.sent

    def add(self, after=None):
        got = self.got if after is None else tied(self.got, after)
        if self.total is None:
            total = dot_first(self.halves[1], self.right) + wide(got)
        else:
            total = self.kept + wide(got).reshape(self.kept.shape)
        self.total = total.reshape(-1, self.rows, self.right.shape[1])

    def step(self, after=None):
        self.add(after)
        return self.ready()

    def end(self, after=None):
        self.add(after)
        while self.remaining:
            self.ready()
            self.add()
        self.done = self.total.reshape(self.total.shape[1:])
        return self.done


def rows_of_columns(blocks, groups):
    shards, mine = lax.axis_size("shard"), lax.axis_index("shard")
    parts = len(blocks) // groups
    rows = blocks[0].shape[0] // shards
    columns = blocks[0].shape[1]

    def part(target):
        return jnp.concatenate(
            [lax.dynamic_slice_in_dim(block, target * rows, rows, axis=0) for block in blocks],
            axis=1,
        )

    pieces = [part(mine)] + [exchange(part(mine ^ k), "shard", k) for k in range(1, shards)]
    offsets = [
        (group * shards + (mine ^ k)) * columns * parts
        for k in range(shards)
        for group in range(groups)
    ]
    shape = (rows, columns * parts)
    plan = [
        (k, group, 0, None, k * groups + group, shape)
        for k in range(shards)
        for group in range(groups)
    ]
    return assemble(pieces, plan, offsets, [(rows, groups * shards * columns * parts)])[0]


def small_grads(value, gains, between):
    peers, shards = lax.axis_size("seq"), lax.axis_size("shard")
    rows = value.shape[0] // peers
    width = value.shape[1]
    packed = jnp.transpose(gains.reshape(2, peers, shards, -1), (1, 0, 3, 2))
    value = jnp.concatenate([value, packed.reshape(value.shape[0], shards)], axis=1)
    total = value.reshape(peers, rows, width + shards)
    left = [mask.bit_length() - 1 for mask in masks_of("seq")]
    for bit in list(left):
        sent, kept = halve(total, left, bit, jnp.float32)
        total = (kept + exchange(sent, "seq", 1 << bit)).reshape(-1, rows, width + shards)
        if between:
            total = tied(total, between.pop(0)(total))
    total = total.reshape(rows, width + shards)
    gain_sum = total[:, width:]
    for mask in masks_of("shard"):
        gain_sum = gain_sum + exchange(gain_sum, "shard", mask)
    gain_sum = lax.dynamic_index_in_dim(gain_sum, lax.axis_index("shard"), 1, keepdims=False)
    pairs = [(s * shards + h, h * peers + s) for s in range(peers) for h in range(shards)]
    return lax.ppermute(total[:, :width], ("seq", "shard"), pairs), gain_sum.reshape(2, -1)


def spread(source, target, length):
    for c in range(source.shape[-1] // LANES):
        target[pl.ds(c * length, length), :] = wide(source[0, :, c * LANES : (c + 1) * LANES])


def collect(source, target, length):
    for c in range(target.shape[-1] // LANES):
        target[0, :, c * LANES : (c + 1) * LANES] = source[pl.ds(c * length, length), :]


def token_rows(ref, token, blocks, length):
    return ref[pl.ds(token, blocks, stride=length), :]


def sum_blocks(values):
    blocks = values[0].shape[0]
    if blocks != GROUP:
        return jnp.concatenate([jnp.sum(v, axis=0, keepdims=True) for v in values], axis=0)
    row = lax.broadcasted_iota(jnp.int32, (GROUP, LANES), 0)
    upper = row < 4
    level = [
        jnp.where(upper, values[j], values[j + 4])
        + pltpu.roll(jnp.where(upper, values[j + 4], values[j]), 4, 0)
        for j in range(4)
    ]
    for step in (2, 1):
        first = (row & step) == 0
        level = [
            jnp.where(
                first,
                level[j] + pltpu.roll(level[j], GROUP - step, 0),
                level[j + step] + pltpu.roll(level[j + step], step, 0),
            )
            for j in range(step)
        ]
    return level[0]


def end_kernel(length, blocks, rows_ref, rate_ref, signal_ref, a_ref, state_ref, total_ref, rate, signal):
    spread(rate_ref, rate, length)
    spread(signal_ref, signal, length)
    state_ref[...] = jnp.zeros_like(state_ref)

    def group(i, total):
        start = i * GROUP
        rates = [token_rows(rate, start + j, blocks, length) for j in range(GROUP)]
        drives = [
            rates[j] * token_rows(signal, start + j, blocks, length) for j in range(GROUP)
        ]
        for n in range(N):
            state, a = state_ref[0, n], a_ref[n]
            for j in range(GROUP):
                state = jnp.exp2(rates[j] * a) * state + drives[j] * rows_ref[0, 0, n * length + start + j]
            state_ref[0, n] = state
        for j in range(GROUP):
            total = total + rates[j]
        return total

    total_ref[0, 0] = lax.fori_loop(
        0, length // GROUP, group, jnp.zeros((blocks, LANES), jnp.float32)
    )


def scan_kernel(
    length, blocks, rows_ref, rate_ref, signal_ref, a_ref, in_ref, out_ref, state_ref, rate, signal, out
):
    spread(rate_ref, rate, length)
    spread(signal_ref, signal, length)
    state_ref[...] = in_ref[0]

    def group(i, carry):
        start = i * GROUP
        rates = [token_rows(rate, start + j, blocks, length) for j in range(GROUP)]
        drives = [
            rates[j] * token_rows(signal, start + j, blocks, length) for j in range(GROUP)
        ]
        outs = [None] * GROUP
        for n in range(N):
            state, a = state_ref[n], a_ref[n]
            for j in range(GROUP):
                state = jnp.exp2(rates[j] * a) * state + drives[j] * rows_ref[0, 0, n * length + start + j]
                term = state * rows_ref[0, 0, (N + n) * length + start + j]
                outs[j] = term if outs[j] is None else outs[j] + term
            state_ref[n] = state
        for j in range(GROUP):
            out[pl.ds(start + j, blocks, stride=length), :] = outs[j]
        return carry

    lax.fori_loop(0, length // GROUP, group, 0)
    collect(out, out_ref, length)


def seed_kernel(length, blocks, rows_ref, rate_ref, up_ref, a_ref, seed_ref, rate, up):
    spread(rate_ref, rate, length)
    spread(up_ref, up, length)
    seed_ref[...] = jnp.zeros_like(seed_ref)

    def group(i, carry):
        start = length - GROUP - i * GROUP
        rates = [token_rows(rate, start + j, blocks, length) for j in range(GROUP)]
        ups = [token_rows(up, start + j, blocks, length) for j in range(GROUP)]
        for n in range(N):
            back, a = seed_ref[0, n], a_ref[n]
            for j in reversed(range(GROUP)):
                back = jnp.exp2(rates[j] * a) * (
                    back + ups[j] * rows_ref[0, 0, (N + n) * length + start + j]
                )
            seed_ref[0, n] = back
        return carry

    lax.fori_loop(0, length // GROUP, group, 0)


def grad_kernel(
    length,
    blocks,
    rows_ref,
    rate_ref,
    signal_ref,
    up_ref,
    a_ref,
    in_ref,
    back_ref,
    a_before_ref,
    rate_grad_ref,
    signal_grad_ref,
    rows_grad_ref,
    a_grad_ref,
    states,
    back_state,
    rate,
    signal,
    up,
    rate_grad,
    signal_grad,
):
    spread(rate_ref, rate, length)
    spread(signal_ref, signal, length)
    spread(up_ref, up, length)
    for n in range(N):
        states[n, 0] = in_ref[0, n]
    back_state[...] = back_ref[0]

    @pl.when(pl.program_id(0) == 0)
    def _():
        a_grad_ref[...] = a_before_ref[...]

    def forward(i, carry):
        start = i * GROUP
        rates = [token_rows(rate, start + j, blocks, length) for j in range(GROUP)]
        drives = [
            rates[j] * token_rows(signal, start + j, blocks, length) for j in range(GROUP)
        ]
        for n in range(N):
            state, a = states[n, start], a_ref[n]
            for j in range(GROUP):
                state = jnp.exp2(rates[j] * a) * state + drives[j] * rows_ref[0, 0, n * length + start + j]
                states[n, start + j + 1] = state
        return carry

    lax.fori_loop(0, length // GROUP, forward, 0)

    def backward(i, carry):
        start = length - GROUP - i * GROUP
        rates = [token_rows(rate, start + j, blocks, length) for j in range(GROUP)]
        signals = [token_rows(signal, start + j, blocks, length) for j in range(GROUP)]
        ups = [token_rows(up, start + j, blocks, length) for j in range(GROUP)]
        through = [None] * GROUP
        slope = [None] * GROUP
        for n in range(N):
            back, a = back_state[n], a_ref[n]
            a_sum = None
            to_b = [None] * GROUP
            to_c = [None] * GROUP
            for j in reversed(range(GROUP)):
                b = rows_ref[0, 0, n * length + start + j]
                c = rows_ref[0, 0, (N + n) * length + start + j]
                here = back + ups[j] * c
                back = jnp.exp2(rates[j] * a) * here
                moved = back * states[n, start + j]
                a_term = moved * rates[j]
                a_sum = a_term if a_sum is None else a_sum + a_term
                b_term, a_slope = here * b, moved * a
                through[j] = b_term if through[j] is None else through[j] + b_term
                slope[j] = a_slope if slope[j] is None else slope[j] + a_slope
                to_b[j] = here * (rates[j] * signals[j])
                to_c[j] = ups[j] * states[n, start + j + 1]
            back_state[n] = back
            a_grad_ref[n] = a_grad_ref[n] + a_sum
            at = pl.ds(pl.multiple_of(start, GROUP), GROUP)
            rows_grad_ref[0, n, at, :] = sum_blocks(to_b)
            rows_grad_ref[0, N + n, at, :] = sum_blocks(to_c)
        for j in range(GROUP):
            rows = pl.ds(start + j, blocks, stride=length)
            rate_grad[rows, :] = through[j] * signals[j] + slope[j] * ln_2
            signal_grad[rows, :] = through[j] * rates[j]
        return carry

    lax.fori_loop(0, length // GROUP, backward, 0)
    collect(rate_grad, rate_grad_ref, length)
    collect(signal_grad, signal_grad_ref, length)


def scan_call(kernel, name, sequences, length, channels, inputs, outputs, scratch, after=(), part=(0, 1), before=None):
    blocks = channels // LANES
    count = sequences // part[1]
    at = part[0] * count
    before = [] if before is None else list(before)
    kinds = {
        "rows": ((1, 1, 2 * N * length), lambda s: (at + s, 0, 0)),
        "tokens": ((1, length, channels), lambda s: (at + s, 0, 0)),
        "states": ((1, N, blocks, LANES), lambda s: (at + s, 0, 0, 0)),
        "total": ((1, 1, blocks, LANES), lambda s: (at + s, 0, 0, 0)),
        "fixed": ((N, blocks, LANES), lambda s: (0, 0, 0)),
        "rows_grad": ((1, 2 * N, length, LANES), lambda s: (at + s, 0, 0, 0)),
    }

    def spec(kind):
        shape, index = kinds[kind]
        if kind == "rows":
            return pl.BlockSpec(shape, index, memory_space=pltpu.SMEM)
        return pl.BlockSpec(shape, index)

    def whole(kind):
        shape = kinds[kind][0]
        if kind != "fixed":
            shape = (sequences,) + shape[1:]
        return jax.ShapeDtypeStruct(shape, jnp.float32)

    def space(kind):
        if kind == "tokens":
            return pltpu.VMEM((blocks * length, LANES), jnp.float32)
        if kind == "history":
            return pltpu.VMEM((N, length + 1, blocks, LANES), jnp.float32)
        return pltpu.VMEM((N, blocks, LANES), jnp.float32)

    values = [value for _, value in inputs]
    values = tied(values, list(after))
    def body(*refs):
        kernel(length, blocks, *refs[: len(inputs)], *refs[len(inputs) + len(before) :])

    return pl.pallas_call(
        body,
        name=name,
        grid=(count,),
        in_specs=[spec(kind) for kind, _ in inputs]
        + [pl.BlockSpec(memory_space=pl.ANY)] * len(before),
        input_output_aliases={len(inputs) + i: i for i in range(len(before))},
        out_specs=[spec(kind) for kind in outputs],
        out_shape=[whole(kind) for kind in outputs],
        scratch_shapes=[space(kind) for kind in scratch],
        compiler_params=pltpu.CompilerParams(vmem_limit_bytes=56 * 1024 * 1024),
        cost_estimate=pl.CostEstimate(
            flops=0,
            bytes_accessed=0,
            transcendentals=0,
        ),
    )(*values, *before)


def chained(total, state, a_scaled, direction):
    peers = lax.axis_size("seq")
    second_of_pair = (lax.axis_index("seq") & 1) == (1 if direction == 1 else 0)

    def join(first, second):
        return (
            first[0] + second[0],
            jnp.exp2(second[0] * a_scaled) * first[1] + second[1],
        )

    def split(packed):
        return (packed[:, :1], packed[:, 1:])

    def chosen(flag, yes, no):
        return tuple(jnp.where(flag, a, b) for a, b in zip(yes, no))

    own = (total, state)
    mate = split(exchange(jnp.concatenate(own, axis=1), "seq", 1))
    first = chosen(second_of_pair, mate, own)
    pair = join(first, chosen(second_of_pair, own, mate))
    packed = jnp.concatenate(pair, axis=1)
    before = None
    for by in reversed(range(2, peers, 2)):
        got = split(passed_along(packed, "seq", direction * by))
        before = got if before is None else join(before, got)
    return jnp.where(second_of_pair, join(before, first)[1], before[1]), packed


def local(
    tokens,
    gain_one,
    in_weight,
    conv_weight,
    conv_bias,
    x_weight,
    dt_weight,
    dt_bias,
    a_log,
    skip_gain,
    out_weight,
    gain_two,
    ffn_in,
    ffn_down,
    cotangent,
):
    shards = lax.axis_size("shard")
    held, length, _ = tokens.shape
    sequences = held * shards
    own_rows = held * length
    row_count = sequences * length
    channels = conv_bias.shape[0]
    blocks = channels // LANES

    def by_sequence(value):
        return value.reshape(sequences, length, value.shape[-1])

    tokens_own = tokens.reshape(own_rows, D)
    up_own = cotangent.reshape(own_rows, D)
    gains_own = rounded(jnp.concatenate([gain_one, gain_two])).reshape(1, -1)
    gain_rows = jnp.pad(gains_own, ((0, 15), (0, D - gains_own.shape[1])))
    conv_sent = halves_out(in_weight, 2, 0)
    conv_got = [exchange(piece, "shard", k + 1) for k, piece in enumerate(conv_sent)]
    arrived = []
    packed = jnp.concatenate([tokens_own, gain_rows], axis=0)
    packed = gather_rows(tied(packed, conv_sent), arrived).reshape(shards, own_rows + 16, D)
    tokens_all = packed[:, :own_rows].reshape(row_count, D)
    gains = packed[:, own_rows, : gains_own.shape[1]].reshape(shards, 2, -1)
    in_turn = [
        lax.dynamic_index_in_dim(gains, lax.axis_index("shard") ^ k, 0, keepdims=False)
        for k in range(shards)
    ]
    gains = wide(jnp.concatenate(in_turn, axis=1))
    gain_norm, gain_second = gains[0], gains[1]

    conv_other = [exchange(piece, "seq", 1) for piece in conv_got[1:]]
    groups = [(in_weight, 2, 1), (out_weight, 1, 0)]
    weight_conv_in = halves_in(in_weight, 2, 0, conv_got, conv_other)
    groups += [(ffn_in, 2, 0), (ffn_in, 2, 1)]
    own, near, far = recut(groups, [arrived, weight_conv_in])
    mixer_far = gathered([piece[:, : 2 * channels] for piece in far])
    ffn_far = gathered([piece[:, 2 * channels :] for piece in far])
    weight_gate_in, weight_out = recut_end(own, near, mixer_far, 2, channels)

    conv_taps = wide(rounded(conv_weight))
    bias_conv = wide(rounded(conv_bias))
    weight_x = rounded(x_weight)
    weight_dt = rounded(dt_weight)
    bias_dt = wide(rounded(dt_bias))
    weight_skip = wide(rounded(skip_gain))
    a_matrix = -jnp.exp(wide(rounded(a_log)))
    a_scaled = (a_matrix * log2_e).T.reshape(N, blocks, LANES)

    inputs_all = wide(tokens_all)
    scale_all = lax.rsqrt(jnp.mean(inputs_all * inputs_all, axis=1, keepdims=True) + epsilon)
    normed = rounded(inputs_all * scale_all * gain_norm)
    conv_in = by_sequence(rounded(dot_plain(normed, weight_conv_in)))
    gate_mix = dot_plain(normed, weight_gate_in)
    borrowed = passed_along(conv_in[:, length - (K - 1) :], "seq", 1)
    padded = wide(jnp.concatenate([borrowed, conv_in], axis=1))
    conv_out = bias_conv + jnp.zeros((sequences, length, channels), jnp.float32)
    for offset in range(K):
        conv_out = conv_out + conv_taps[offset] * padded[:, offset : offset + length]
    conv_out = conv_out.reshape(row_count, channels)
    signal = rounded(jax.nn.silu(conv_out))
    signal_wide = wide(signal)
    selection = sum_columns(
        lax.dot_general(
            weight_x, signal, (((0,), (1,)), ((), ())), preferred_element_type=jnp.float32
        )
    )
    down_own, down_near, down_parts = recut([(ffn_down, 1, 0)], [selection])
    down_far = gathered(down_parts)
    rank_part = rounded(selection[:R])
    rows = jnp.swapaxes(selection[R:].reshape(2 * N, sequences, length), 0, 1).reshape(
        sequences, 1, 2 * N * length
    )
    pre_rate = dot_first(rank_part, weight_dt) + bias_dt
    rates = by_sequence(jax.nn.softplus(pre_rate))
    signals = by_sequence(signal)
    sizes = (sequences, length, channels)
    end_state, total_rate = scan_call(
        end_kernel,
        "scan_end",
        *sizes,
        [("rows", rows), ("tokens", rates), ("tokens", signals), ("fixed", a_scaled)],
        ["states", "total"],
        ["tokens", "tokens"],
        [near] + far,
    )
    incoming, _ = chained(total_rate, end_state, a_scaled, 1)
    ffn_width = ffn_in.shape[1] // (2 * shards)
    (scan_out,) = scan_call(
        scan_kernel,
        "scan_out",
        *sizes,
        [
            ("rows", rows),
            ("tokens", rates),
            ("tokens", signals),
            ("fixed", a_scaled),
            ("states", incoming),
        ],
        ["tokens"],
        ["fixed", "tokens", "tokens", "tokens"],
        [down_near] + down_parts,
    )
    (weight_down,) = recut_end(down_own, down_near, down_far, 1, down_own.shape[1])
    ffn_offset = 2 * channels // ffn_width
    weight_gate, weight_up = recut_end(own, near, ffn_far, 2, ffn_width, ffn_offset)
    scanned = scan_out.reshape(row_count, channels) + weight_skip * signal_wide
    gate_act = jax.nn.silu(gate_mix)
    gated = rounded(scanned * gate_act)
    inputs = wide(tokens_own)

    def mixed_rows(first, last):
        return dot_last(gated[first * own_rows : last * own_rows], weight_out)

    middle = inputs + scatter_rows(mixed_rows, True, [weight_gate, weight_up])

    scale_two = lax.rsqrt(jnp.mean(middle * middle, axis=1, keepdims=True) + epsilon)
    arrived = []
    normed_two = gather_rows(rounded(middle * scale_two * gain_second), arrived)
    up_all = gather_rows(tied(up_own, arrived))
    gate_part = dot_plain(normed_two, weight_gate)
    up_part = dot_plain(normed_two, weight_up)
    gate_silu = jax.nn.silu(gate_part)
    activated = rounded(gate_silu * up_part)
    columns = activated.shape[1] // 2
    up_halves = split_columns(up_all, 0)
    down_first = WeightGrad(up_halves, activated[:, :columns])
    down_second = WeightGrad(up_halves, activated[:, columns:])
    up_late = tied(up_all, down_first.ready())
    act_grad = dot_plain(up_late, weight_down)
    gate_grad = rounded(act_grad * up_part * silu_slope(gate_part))
    up_grad = rounded(act_grad * gate_silu)
    gate_late, up_grad_late = tied((gate_grad, up_grad), down_second.ready(gate_grad))

    def normed_two_rows(first, last):
        at = slice(first * own_rows, last * own_rows)
        gate_rows, up_rows = gate_late[at], up_grad_late[at]
        if first == 0:
            gate_rows, up_rows = tied((gate_rows, up_rows), down_first.step())
        return dot_last(gate_rows, weight_gate) + dot_last(up_rows, weight_up)

    normed_two_grad = scatter_rows(normed_two_rows)
    two_halves = split_columns(normed_two, 0)
    gate_first = WeightGrad(two_halves, gate_grad[:, :columns])
    gate_second = WeightGrad(two_halves, gate_grad[:, columns:])
    up_first = WeightGrad(two_halves, up_grad[:, :columns])
    up_second = WeightGrad(two_halves, up_grad[:, columns:])
    gain_two_grad = jnp.sum(normed_two_grad * middle * scale_two, axis=0)
    scaled_two = normed_two_grad * gain_second
    middle_grad = (
        wide(up_own)
        + scale_two * scaled_two
        - middle
        * (scale_two * scale_two * scale_two)
        * jnp.mean(scaled_two * middle, axis=1, keepdims=True)
    )
    mixed_grad = gather_rows(rounded(middle_grad))
    token = tied(middle_grad, [down_first.got, down_second.got])
    steps = [down_second.step(token), down_first.step(token), gate_first.ready(token)]
    mixed_late = tied(mixed_grad, steps)

    gated_grad = dot_plain(mixed_late, weight_out)
    scan_grad = gated_grad * gate_act
    gate_mix_grad = rounded(gated_grad * scanned * silu_slope(gate_mix))
    skip_grad = jnp.sum(scan_grad * signal_wide, axis=0)
    ups = by_sequence(scan_grad)
    token = tied(ups, [gate_first.got, down_second.got, down_first.got])
    steps = [gate_second.ready(token), gate_first.step(token), down_second.step(token)]
    down_first.end(token)
    (seed,) = scan_call(
        seed_kernel,
        "scan_seed",
        *sizes,
        [("rows", rows), ("tokens", rates), ("tokens", ups), ("fixed", a_scaled)],
        ["states"],
        ["tokens", "tokens"],
        steps,
    )
    returning, first_round = chained(total_rate, seed, a_scaled, -1)
    token = tied(first_round, [gate_second.got, gate_first.got, down_second.got])
    steps = [up_first.ready(token), gate_second.step(token)]
    down_second.end(token)
    token = tied(returning, steps)
    steps = [up_second.ready(token), gate_first.step(token)]
    mixed_halves = split_columns(mixed_grad, 0)
    normed_halves = split_columns(normed, 0)
    out_sum = WeightGrad(mixed_halves, gated)
    in_gate_sum = WeightGrad(normed_halves, gate_mix_grad)
    grads = None
    for part in range(2):
        grads = scan_call(
            grad_kernel,
            "scan_grad",
            *sizes,
            [
                ("rows", rows),
                ("tokens", rates),
                ("tokens", signals),
                ("tokens", ups),
                ("fixed", a_scaled),
                ("states", incoming),
                ("states", returning),
                ("fixed", jnp.zeros_like(a_scaled) if grads is None else grads[3]),
            ],
            ["tokens", "tokens", "rows_grad", "fixed"],
            ["history", "fixed", "tokens", "tokens", "tokens", "tokens", "tokens"],
            steps,
            part=(part, 2),
            before=None if grads is None else grads[:3],
        )
        if part == 0:
            token = tied(
                grads[3], [up_first.got, up_second.got, gate_second.got, gate_first.got]
            )
            steps = [out_sum.ready(token), in_gate_sum.ready(token), up_first.step(token)]
            steps += [up_second.step(token), gate_second.step(token), gate_first.end(token)]
    rate_grad, scan_signal_grad, rows_grad, a_grad = grads
    token = tied(a_grad, [up_first.got, up_second.got, out_sum.got])
    steps = [out_sum.step(token), up_first.step(token)]
    rate_grad = tied(rate_grad, steps)
    rate_grad = rate_grad.reshape(row_count, channels)
    pre_grad = rate_grad * jax.nn.sigmoid(pre_rate)
    pre_grad_low = rounded(pre_grad)
    rank_grad = dot_last(weight_dt, pre_grad_low)
    rows_grad = jnp.swapaxes(jnp.sum(rows_grad, axis=3), 0, 1).reshape(2 * N, row_count)
    selection_grad = rounded(sum_columns(jnp.concatenate([rank_grad, rows_grad], axis=0)))
    token = tied(selection_grad, [gate_second.got, up_first.got])
    steps = [up_second.step(token), gate_second.end(token)]
    selection_grad = tied(selection_grad, steps)
    signal_grad = (
        scan_grad * weight_skip
        + scan_signal_grad.reshape(row_count, channels)
        + lax.dot_general(
            selection_grad, weight_x, (((0,), (1,)), ((), ())), preferred_element_type=jnp.float32
        )
    )
    conv_grad = (signal_grad * silu_slope(conv_out)).reshape(sequences, length, channels)
    padded_grad = jnp.zeros((sequences, length + K - 1, channels), jnp.float32)
    for offset in range(K):
        padded_grad = padded_grad + jnp.pad(
            conv_taps[offset] * conv_grad, ((0, 0), (offset, K - 1 - offset), (0, 0))
        )
    returned = wide(passed_along(low(padded_grad[:, : K - 1]), "seq", -1))
    conv_in_grad = rounded(
        padded_grad[:, K - 1 :] + jnp.pad(returned, ((0, 0), (length - (K - 1), 0), (0, 0)))
    ).reshape(row_count, channels)
    in_conv_sum = WeightGrad(normed_halves, conv_in_grad)
    token = tied(conv_in_grad, [in_conv_sum.ready(), in_gate_sum.got, out_sum.got])
    steps = [in_gate_sum.step(token), out_sum.step(token), up_first.end(token)]
    conv_in_grad = tied(conv_in_grad, steps)
    normed_grad_parts = {}
    activated_late = tied(activated, conv_in_grad)

    def normed_rows(first, last):
        at = slice(first * own_rows, last * own_rows)
        part = dot_last(conv_in_grad[at], weight_conv_in) + dot_last(
            gate_mix_grad[at], weight_gate_in
        )
        normed_grad_parts[first] = jnp.sum(part * inputs_all[at] * scale_all[at], axis=0)
        return part

    normed_grad = scatter_rows(normed_rows)
    gain_one_grad = sum(normed_grad_parts.values())
    token = tied(gain_one_grad, [in_conv_sum.got, in_gate_sum.got])
    steps = [in_conv_sum.step(token), in_gate_sum.step(token), up_second.end(token)]
    gain_one_grad = tied(gain_one_grad, steps)
    result = middle + scatter_far(scatter_near(dot_last(activated_late, weight_down)), own_rows)
    output = rounded(result).reshape(tokens.shape)
    scale_one = scale_all[:own_rows]
    scaled_one = normed_grad * gain_norm
    input_grad = (
        middle_grad
        + scale_one * scaled_one
        - inputs
        * (scale_one * scale_one * scale_one)
        * jnp.mean(scaled_one * inputs, axis=1, keepdims=True)
    )


    conv_weight_grad = jnp.stack(
        [
            jnp.sum(conv_grad * padded[:, offset : offset + length], axis=(0, 1))
            for offset in range(K)
        ],
        axis=1,
    )
    column_sums = jnp.stack(
        [jnp.sum(conv_grad, axis=(0, 1)), jnp.sum(pre_grad, axis=0), skip_grad], axis=1
    )
    a_log_grad = a_grad.reshape(N, channels).T * a_matrix
    dt_weight_grad = lax.dot_general(
        pre_grad_low, rank_part, (((0,), (1,)), ((), ())), preferred_element_type=jnp.float32
    )
    x_weight_grad = lax.dot_general(
        signal, selection_grad, (((0,), (1,)), ((), ())), preferred_element_type=jnp.float32
    )
    small, gain_grads = small_grads(
        jnp.concatenate(
            [dt_weight_grad, x_weight_grad, a_log_grad, conv_weight_grad, column_sums], axis=1
        ),
        jnp.stack([gain_one_grad, gain_two_grad]),
        [in_conv_sum.step, in_conv_sum.end],
    )
    at = R + R + 2 * N

    ffn_down_result = rows_of_columns([down_first.done, down_second.done], 1)
    ffn_in_result = rows_of_columns(
        [
            gate_first.done,
            gate_second.done,
            up_first.done,
            up_second.done,
        ],
        2,
    )
    out_result = rows_of_columns([out_sum.end()], 1)
    in_result = rows_of_columns([in_conv_sum.done, in_gate_sum.end()], 2)
    return (
        output,
        rounded(input_grad).reshape(tokens.shape),
        gain_grads[0],
        in_result,
        small[:, at + N : at + N + K].T,
        small[:, at + N + K],
        small[:, R:at],
        small[:, :R].T,
        small[:, at + N + K + 1],
        small[:, at : at + N],
        small[:, at + N + K + 2],
        out_result,
        gain_grads[1],
        ffn_in_result,
        ffn_down_result,
    )


def solution(mesh):
    in_specs = (
        P("shard", "seq", None),
        P("shard"),
        P("shard", None),
        P(None, "shard"),
        P("shard"),
        P("shard", None),
        P(None, "shard"),
        P("shard"),
        P("shard", None),
        P("shard"),
        P("shard", None),
        P("shard"),
        P("shard", None),
        P("shard", None),
        P("shard", "seq", None),
    )
    out_specs = (
        P("shard", "seq", None),
        P("shard", "seq", None),
        P(("seq", "shard")),
        P(("seq", "shard"), None),
        P(None, ("seq", "shard")),
        P(("seq", "shard")),
        P(("seq", "shard"), None),
        P(None, ("seq", "shard")),
        P(("seq", "shard")),
        P(("seq", "shard"), None),
        P(("seq", "shard")),
        P(("seq", "shard"), None),
        P(("seq", "shard")),
        P(("seq", "shard"), None),
        P(("seq", "shard"), None),
    )
    return jax.shard_map(local, mesh=mesh, in_specs=in_specs, out_specs=out_specs, check_vma=False)
```

```python
import functools
import math

import jax
import jax.numpy as jnp
from jax import lax
from jax.experimental import pallas as pl
from jax.experimental.pallas import tpu as pltpu
from jax.sharding import PartitionSpec as P

D = 2048
E = 4096
N = 16
K = 4
R = 128
FF = 8192

LANES = 128
GROUP = 8

epsilon = 1e-05
log2_e = math.log2(math.e)
ln_2 = math.log(2.0)


def silu_slope(value):
    sigma = jax.nn.sigmoid(value)
    return sigma * (1.0 + value * (1.0 - sigma))


def dot_last(left, right):
    return lax.dot_general(
        left, right, (((1,), (1,)), ((), ())), preferred_element_type=jnp.float32
    )


def dot_first(left, right):
    return lax.dot_general(
        left, right, (((0,), (0,)), ((), ())), preferred_element_type=jnp.float32
    )


def dot_plain(left, right):
    return jnp.dot(left, right, preferred_element_type=jnp.float32)


def wide(value):
    return value.astype(jnp.float32)


def low(value):
    return value.astype(jnp.bfloat16)


def rounded(value):
    return lax.reduce_precision(value, 8, 7).astype(jnp.bfloat16)


def exchange(value, axis, mask):
    return lax.ppermute(value, axis, [(i, i ^ mask) for i in range(lax.axis_size(axis))])


def passed_along(value, axis, by):
    peers = lax.axis_size(axis)
    pairs = [(i, i + by) for i in range(peers) if 0 <= i + by < peers]
    return lax.ppermute(value, axis, pairs)


def masks_of(axis):
    size = lax.axis_size(axis)
    return [1 << bit for bit in range(size.bit_length() - 1)]


def gather_rows(value, arrived=None, after=None):
    parts = {0: value}
    for mask in reversed(masks_of("shard")):
        held = sorted(parts)
        got = exchange(jnp.concatenate([parts[k] for k in held], axis=0), "shard", mask)
        if arrived is not None and mask > 1:
            arrived.append(got)
        if after is not None and mask > 1:
            got = tied(got, after)
        for place, k in enumerate(held):
            parts[k ^ mask] = got[place * value.shape[0] : (place + 1) * value.shape[0]]
    return jnp.concatenate([parts[k] for k in sorted(parts)], axis=0)


def exchange_scaled(value, axis, mask):
    largest = jnp.maximum(jnp.max(jnp.abs(value)), 1e-30)
    scale = jnp.broadcast_to(largest, (8, LANES))
    got_scale = exchange(scale, axis, mask)
    scaled = (value * (1.0 / largest)).astype(jnp.float16)
    got = exchange(tied(scaled, got_scale), axis, mask)
    return got.astype(jnp.float32) * got_scale[0, 0]


def scatter_rows(make, scaled=False, after=None):
    shards = lax.axis_size("shard")
    parts = {}
    for pair in reversed(range(0, shards, 2)):
        value = make(pair, pair + 2)
        rows = value.shape[0] // 2
        parts[pair] = value[:rows] + exchange(value[rows:], "shard", 1)
    return scatter_far(parts, rows, scaled, after)


def scatter_near(value):
    shards = lax.axis_size("shard")
    rows = value.shape[0] // shards
    blocks = [value[k * rows : (k + 1) * rows] for k in range(shards)]
    got = exchange(jnp.concatenate(blocks[1::2], axis=0), "shard", 1)
    return {
        2 * k: blocks[2 * k] + got[k * rows : (k + 1) * rows] for k in range(shards // 2)
    }


def scatter_far(parts, rows, scaled=False, after=None):
    parts = dict(parts)
    for mask in masks_of("shard")[1:]:
        sent = [k for k in sorted(parts) if k & mask]
        block = jnp.concatenate([parts[k] for k in sent], axis=0)
        if scaled:
            got = exchange_scaled(block, "shard", mask)
        else:
            got = wide(exchange(low(block), "shard", mask))
        if after is not None:
            got = tied(got, after)
        for place, k in enumerate(sent):
            parts[k ^ mask] = parts[k ^ mask] + got[place * rows : (place + 1) * rows]
            del parts[k]
    return parts[0]


def sum_columns(value):
    shards = lax.axis_size("shard")
    count = value.shape[1] // shards
    for mask in masks_of("shard"):
        got = exchange(value, "shard", mask)
        order = [k ^ mask for k in range(shards)]
        value = value + jnp.concatenate(
            [got[:, k * count : (k + 1) * count] for k in order], axis=1
        )
    return value


def tied(values, after):
    return lax.optimization_barrier((values, after))[0]


def assemble_kernel(plan, count, at_ref, *refs):
    pieces, outs = refs[:count], refs[count : -1 - len(plan)]
    held, sems = refs[-1 - len(plan) : -1], refs[-1]
    fetches, stores = [], []
    for place, (piece, part, target, row, col, shape) in enumerate(plan):
        first = pl.multiple_of(at_ref[row], 16) if row is not None else 0
        left = pl.multiple_of(at_ref[col], LANES) if col is not None else 0
        fetch = pltpu.make_async_copy(
            pieces[piece].at[:, pl.ds(part * shape[1], shape[1])], held[place], sems.at[0, place]
        )
        fetch.start()
        fetches.append(fetch)
        stores.append(
            pltpu.make_async_copy(
                held[place],
                outs[target].at[pl.ds(first, shape[0]), pl.ds(left, shape[1])],
                sems.at[1, place],
            )
        )
    for fetch, store in zip(fetches, stores):
        fetch.wait()
        store.start()
    for store in stores:
        store.wait()


def assemble(pieces, plan, offsets, shapes):
    kind = pieces[0].dtype
    moved = sum(shape[0] * shape[1] * kind.itemsize for shape in shapes)
    any_space = pl.BlockSpec(memory_space=pl.ANY)
    return pl.pallas_call(
        functools.partial(assemble_kernel, plan, len(pieces)),
        name="assemble",
        in_specs=[pl.BlockSpec(memory_space=pltpu.SMEM)] + [any_space] * len(pieces),
        out_specs=[any_space] * len(shapes),
        out_shape=[jax.ShapeDtypeStruct(shape, kind) for shape in shapes],
        scratch_shapes=[pltpu.VMEM(entry[5], kind) for entry in plan]
        + [pltpu.SemaphoreType.DMA((2, len(plan)))],
        compiler_params=pltpu.CompilerParams(vmem_limit_bytes=48 * 1024 * 1024),
        cost_estimate=pl.CostEstimate(flops=0, bytes_accessed=2 * moved, transcendentals=0),
    )(jnp.stack(offsets).astype(jnp.int32), *pieces)


def column_part(weight, groups, group, target, first, count):
    columns = weight.shape[1] // (groups * lax.axis_size("shard"))
    at = (first, (group * lax.axis_size("shard") + target) * columns)
    return low(lax.dynamic_slice(weight, at, (count, columns)))


def halves_out(weight, groups, group):
    shards, mine = lax.axis_size("shard"), lax.axis_index("shard")
    rows = weight.shape[0]
    side = (lax.axis_index("seq") & 1) * (rows // 2)
    sent = [column_part(weight, groups, group, mine ^ 1, 0, rows)]
    return sent + [
        column_part(weight, groups, group, mine ^ k, side, rows // 2) for k in range(2, shards)
    ]


def halves_in(weight, groups, group, got, other):
    shards, mine = lax.axis_size("shard"), lax.axis_index("shard")
    rows = weight.shape[0]
    half = rows // 2
    side = (lax.axis_index("seq") & 1) * half
    own = column_part(weight, groups, group, mine, 0, rows)
    pieces = [own] + got + other
    offsets = [mine * rows, (mine ^ 1) * rows]
    offsets += [(mine ^ k) * rows + side for k in range(2, shards)]
    offsets += [(mine ^ k) * rows + half - side for k in range(2, shards)]
    plan = [(place, 0, 0, place, None, piece.shape) for place, piece in enumerate(pieces)]
    return assemble(pieces, plan, offsets, [(shards * rows, own.shape[1])])[0]


def recut(groups, after, late):
    shards, mine = lax.axis_size("shard"), lax.axis_index("shard")
    peers, range_at = lax.axis_size("seq"), lax.axis_index("seq")
    rows = groups[0][0].shape[0]
    fetched = rows // peers

    def part(target, first, count):
        pieces = [column_part(*group, target, first, count) for group in groups]
        return jnp.concatenate(pieces, axis=1)

    far = [part(mine ^ k, range_at * fetched, fetched) for k in range(2, shards)]
    far = [exchange(piece, "shard", k + 2) for k, piece in enumerate(tied(far, after))]
    far = tied(far, late)
    mine = tied(mine, late)
    near = exchange(part(mine ^ 1, 0, rows), "shard", 1)
    return part(mine, 0, rows), near, far


def gathered(pieces):
    return lax.all_gather(jnp.concatenate(pieces, axis=1), "seq", axis=0, tiled=True)


def recut_end(own, near, far, count, width, first=0):
    shards, mine = lax.axis_size("shard"), lax.axis_index("shard")
    rows = own.shape[0]
    plan, offsets = [], []
    for k in range(shards):
        offsets.append((mine ^ k) * rows)
        for group in range(count):
            part = first + group if k < 2 else (k - 2) * count + group
            plan.append((min(k, 2), part, group, k, None, (rows, width)))
    return assemble([own, near, far], plan, offsets, [(shards * rows, width)] * count)


def with_bit(blocks, bit):
    return [b for b in range(blocks) if not b >> bit & 1]


def halve(value, left, bit, sent_type):
    mine = (lax.axis_index("seq") >> bit) & 1
    inner = 1 << sorted(left).index(bit)
    blocks, rows, columns = value.shape
    shaped = value.reshape(blocks // (2 * inner), 2, inner * rows, columns)
    sent = lax.dynamic_index_in_dim(shaped, 1 - mine, 1, keepdims=False).astype(sent_type)
    kept = lax.dynamic_index_in_dim(shaped, mine, 1, keepdims=False)
    left.remove(bit)
    return sent, kept


def split_columns(left, bit):
    peers = lax.axis_size("seq")
    mine = (lax.axis_index("seq") >> bit) & 1
    rows = left.shape[1] // peers

    def half(which):
        pieces = [
            lax.dynamic_slice_in_dim(left, (b + (which << bit)) * rows, rows, axis=1)
            for b in with_bit(peers, bit)
        ]
        return jnp.concatenate(pieces, axis=1)

    return half(1 - mine), half(mine)


class WeightGrad:
    def __init__(self, halves, right):
        self.halves, self.right = halves, right
        self.remaining = [mask.bit_length() - 1 for mask in masks_of("seq")]
        self.rows = 2 * halves[0].shape[1] // lax.axis_size("seq")
        self.total = None

    def ready(self, after=None):
        bit = self.remaining[0]
        if self.total is None:
            if after is not None:
                self.right = tied(self.right, after)
            self.sent = low(dot_first(self.halves[0], self.right))
            self.remaining.remove(bit)
        else:
            self.sent, self.kept = halve(self.total, self.remaining, bit, jnp.bfloat16)
        self.got = exchange(self.sent, "seq", 1 << bit)
        return self.sent

    def add(self, after=None):
        got = self.got if after is None else tied(self.got, after)
        if self.total is None:
            total = dot_first(self.halves[1], self.right) + wide(got)
        else:
            total = self.kept + wide(got).reshape(self.kept.shape)
        self.total = total.reshape(-1, self.rows, self.right.shape[1])

    def step(self, after=None):
        self.add(after)
        return self.ready()

    def end(self, after=None):
        self.add(after)
        while self.remaining:
            self.ready()
            self.add()
        self.done = self.total.reshape(self.total.shape[1:])
        return self.done


def rows_of_columns(blocks, groups):
    shards, mine = lax.axis_size("shard"), lax.axis_index("shard")
    parts = len(blocks) // groups
    rows = blocks[0].shape[0] // shards
    columns = blocks[0].shape[1]

    def part(target):
        return jnp.concatenate(
            [lax.dynamic_slice_in_dim(block, target * rows, rows, axis=0) for block in blocks],
            axis=1,
        )

    pieces = [part(mine)]
    pieces += [wide(exchange(low(part(mine ^ k)), "shard", k)) for k in range(1, shards)]
    offsets = [
        (group * shards + (mine ^ k)) * columns * parts
        for k in range(shards)
        for group in range(groups)
    ]
    shape = (rows, columns * parts)
    plan = [
        (k, group, 0, None, k * groups + group, shape)
        for k in range(shards)
        for group in range(groups)
    ]
    return assemble(pieces, plan, offsets, [(rows, groups * shards * columns * parts)])[0]


def small_grads(value, gains, between):
    peers, shards = lax.axis_size("seq"), lax.axis_size("shard")
    rows = value.shape[0] // peers
    width = value.shape[1]
    packed = jnp.transpose(gains.reshape(2, peers, shards, -1), (1, 0, 3, 2))
    value = jnp.concatenate([value, packed.reshape(value.shape[0], shards)], axis=1)
    total = value.reshape(peers, rows, width + shards)
    left = [mask.bit_length() - 1 for mask in masks_of("seq")]
    for bit in list(left):
        sent, kept = halve(total, left, bit, jnp.float32)
        total = (kept + exchange(sent, "seq", 1 << bit)).reshape(-1, rows, width + shards)
        if between:
            total = tied(total, between.pop(0))
    total = total.reshape(rows, width + shards)
    gain_sum = total[:, width:]
    for mask in masks_of("shard"):
        gain_sum = gain_sum + exchange(gain_sum, "shard", mask)
    gain_sum = lax.dynamic_index_in_dim(gain_sum, lax.axis_index("shard"), 1, keepdims=False)
    pairs = [(s * shards + h, h * peers + s) for s in range(peers) for h in range(shards)]
    return lax.ppermute(total[:, :width], ("seq", "shard"), pairs), gain_sum.reshape(2, -1)


def spread(source, target, length):
    for c in range(source.shape[-1] // LANES):
        target[pl.ds(c * length, length), :] = wide(source[0, :, c * LANES : (c + 1) * LANES])


def collect(source, target, length):
    for c in range(target.shape[-1] // LANES):
        target[0, :, c * LANES : (c + 1) * LANES] = source[pl.ds(c * length, length), :]


def token_rows(ref, token, blocks, length):
    return ref[pl.ds(token, blocks, stride=length), :]


def sum_blocks(values):
    blocks = values[0].shape[0]
    if blocks != GROUP:
        return jnp.concatenate([jnp.sum(v, axis=0, keepdims=True) for v in values], axis=0)
    row = lax.broadcasted_iota(jnp.int32, (GROUP, LANES), 0)
    upper = row < 4
    level = [
        jnp.where(upper, values[j], values[j + 4])
        + pltpu.roll(jnp.where(upper, values[j + 4], values[j]), 4, 0)
        for j in range(4)
    ]
    for step in (2, 1):
        first = (row & step) == 0
        level = [
            jnp.where(
                first,
                level[j] + pltpu.roll(level[j], GROUP - step, 0),
                level[j + step] + pltpu.roll(level[j + step], step, 0),
            )
            for j in range(step)
        ]
    return level[0]


def end_kernel(length, blocks, rows_ref, rate_ref, signal_ref, a_ref, state_ref, total_ref, rate, signal):
    spread(rate_ref, rate, length)
    spread(signal_ref, signal, length)
    state_ref[...] = jnp.zeros_like(state_ref)

    def group(i, total):
        start = i * GROUP
        rates = [token_rows(rate, start + j, blocks, length) for j in range(GROUP)]
        drives = [
            rates[j] * token_rows(signal, start + j, blocks, length) for j in range(GROUP)
        ]
        for n in range(N):
            state, a = state_ref[0, n], a_ref[n]
            for j in range(GROUP):
                state = jnp.exp2(rates[j] * a) * state + drives[j] * rows_ref[0, 0, n * length + start + j]
            state_ref[0, n] = state
        for j in range(GROUP):
            total = total + rates[j]
        return total

    total_ref[0, 0] = lax.fori_loop(
        0, length // GROUP, group, jnp.zeros((blocks, LANES), jnp.float32)
    )


def scan_kernel(
    length, blocks, rows_ref, rate_ref, signal_ref, a_ref, in_ref, out_ref, state_ref, rate, signal, out
):
    spread(rate_ref, rate, length)
    spread(signal_ref, signal, length)
    state_ref[...] = in_ref[0]

    def group(i, carry):
        start = i * GROUP
        rates = [token_rows(rate, start + j, blocks, length) for j in range(GROUP)]
        drives = [
            rates[j] * token_rows(signal, start + j, blocks, length) for j in range(GROUP)
        ]
        outs = [None] * GROUP
        for n in range(N):
            state, a = state_ref[n], a_ref[n]
            for j in range(GROUP):
                state = jnp.exp2(rates[j] * a) * state + drives[j] * rows_ref[0, 0, n * length + start + j]
                term = state * rows_ref[0, 0, (N + n) * length + start + j]
                outs[j] = term if outs[j] is None else outs[j] + term
            state_ref[n] = state
        for j in range(GROUP):
            out[pl.ds(start + j, blocks, stride=length), :] = outs[j]
        return carry

    lax.fori_loop(0, length // GROUP, group, 0)
    collect(out, out_ref, length)


def seed_kernel(length, blocks, rows_ref, rate_ref, up_ref, a_ref, seed_ref, rate, up):
    spread(rate_ref, rate, length)
    spread(up_ref, up, length)
    seed_ref[...] = jnp.zeros_like(seed_ref)

    def group(i, carry):
        start = length - GROUP - i * GROUP
        rates = [token_rows(rate, start + j, blocks, length) for j in range(GROUP)]
        ups = [token_rows(up, start + j, blocks, length) for j in range(GROUP)]
        for n in range(N):
            back, a = seed_ref[0, n], a_ref[n]
            for j in reversed(range(GROUP)):
                back = jnp.exp2(rates[j] * a) * (
                    back + ups[j] * rows_ref[0, 0, (N + n) * length + start + j]
                )
            seed_ref[0, n] = back
        return carry

    lax.fori_loop(0, length // GROUP, group, 0)


def grad_kernel(
    length,
    blocks,
    rows_ref,
    rate_ref,
    signal_ref,
    up_ref,
    a_ref,
    in_ref,
    back_ref,
    a_before_ref,
    rate_grad_ref,
    signal_grad_ref,
    rows_grad_ref,
    a_grad_ref,
    states,
    back_state,
    rate,
    signal,
    up,
    rate_grad,
    signal_grad,
):
    spread(rate_ref, rate, length)
    spread(signal_ref, signal, length)
    spread(up_ref, up, length)
    for n in range(N):
        states[n, 0] = in_ref[0, n]
    back_state[...] = back_ref[0]

    @pl.when(pl.program_id(0) == 0)
    def _():
        a_grad_ref[...] = a_before_ref[...]

    def forward(i, carry):
        start = i * GROUP
        rates = [token_rows(rate, start + j, blocks, length) for j in range(GROUP)]
        drives = [
            rates[j] * token_rows(signal, start + j, blocks, length) for j in range(GROUP)
        ]
        for n in range(N):
            state, a = states[n, start], a_ref[n]
            for j in range(GROUP):
                state = jnp.exp2(rates[j] * a) * state + drives[j] * rows_ref[0, 0, n * length + start + j]
                states[n, start + j + 1] = state
        return carry

    lax.fori_loop(0, length // GROUP, forward, 0)

    def backward(i, carry):
        start = length - GROUP - i * GROUP
        rates = [token_rows(rate, start + j, blocks, length) for j in range(GROUP)]
        signals = [token_rows(signal, start + j, blocks, length) for j in range(GROUP)]
        ups = [token_rows(up, start + j, blocks, length) for j in range(GROUP)]
        through = [None] * GROUP
        slope = [None] * GROUP
        for n in range(N):
            back, a = back_state[n], a_ref[n]
            a_sum = None
            to_b = [None] * GROUP
            to_c = [None] * GROUP
            for j in reversed(range(GROUP)):
                b = rows_ref[0, 0, n * length + start + j]
                c = rows_ref[0, 0, (N + n) * length + start + j]
                here = back + ups[j] * c
                back = jnp.exp2(rates[j] * a) * here
                moved = back * states[n, start + j]
                a_term = moved * rates[j]
                a_sum = a_term if a_sum is None else a_sum + a_term
                b_term, a_slope = here * b, moved * a
                through[j] = b_term if through[j] is None else through[j] + b_term
                slope[j] = a_slope if slope[j] is None else slope[j] + a_slope
                to_b[j] = here * (rates[j] * signals[j])
                to_c[j] = ups[j] * states[n, start + j + 1]
            back_state[n] = back
            a_grad_ref[n] = a_grad_ref[n] + a_sum
            at = pl.ds(pl.multiple_of(start, GROUP), GROUP)
            rows_grad_ref[0, n, at, :] = sum_blocks(to_b)
            rows_grad_ref[0, N + n, at, :] = sum_blocks(to_c)
        for j in range(GROUP):
            rows = pl.ds(start + j, blocks, stride=length)
            rate_grad[rows, :] = through[j] * signals[j] + slope[j] * ln_2
            signal_grad[rows, :] = through[j] * rates[j]
        return carry

    lax.fori_loop(0, length // GROUP, backward, 0)
    collect(rate_grad, rate_grad_ref, length)
    collect(signal_grad, signal_grad_ref, length)


def scan_call(kernel, name, sequences, length, channels, inputs, outputs, scratch, after=(), part=(0, 1), before=None):
    blocks = channels // LANES
    count = sequences // part[1]
    at = part[0] * count
    before = [] if before is None else list(before)
    kinds = {
        "rows": ((1, 1, 2 * N * length), lambda s: (at + s, 0, 0)),
        "tokens": ((1, length, channels), lambda s: (at + s, 0, 0)),
        "states": ((1, N, blocks, LANES), lambda s: (at + s, 0, 0, 0)),
        "total": ((1, 1, blocks, LANES), lambda s: (at + s, 0, 0, 0)),
        "fixed": ((N, blocks, LANES), lambda s: (0, 0, 0)),
        "rows_grad": ((1, 2 * N, length, LANES), lambda s: (at + s, 0, 0, 0)),
    }

    def spec(kind):
        shape, index = kinds[kind]
        if kind == "rows":
            return pl.BlockSpec(shape, index, memory_space=pltpu.SMEM)
        return pl.BlockSpec(shape, index)

    def whole(kind):
        shape = kinds[kind][0]
        if kind != "fixed":
            shape = (sequences,) + shape[1:]
        return jax.ShapeDtypeStruct(shape, jnp.float32)

    def space(kind):
        if kind == "tokens":
            return pltpu.VMEM((blocks * length, LANES), jnp.float32)
        if kind == "history":
            return pltpu.VMEM((N, length + 1, blocks, LANES), jnp.float32)
        return pltpu.VMEM((N, blocks, LANES), jnp.float32)

    values = [value for _, value in inputs]
    values = tied(values, list(after))
    def body(*refs):
        kernel(length, blocks, *refs[: len(inputs)], *refs[len(inputs) + len(before) :])

    return pl.pallas_call(
        body,
        name=name,
        grid=(count,),
        in_specs=[spec(kind) for kind, _ in inputs]
        + [pl.BlockSpec(memory_space=pl.ANY)] * len(before),
        input_output_aliases={len(inputs) + i: i for i in range(len(before))},
        out_specs=[spec(kind) for kind in outputs],
        out_shape=[whole(kind) for kind in outputs],
        scratch_shapes=[space(kind) for kind in scratch],
        compiler_params=pltpu.CompilerParams(vmem_limit_bytes=56 * 1024 * 1024),
        cost_estimate=pl.CostEstimate(
            flops=0,
            bytes_accessed=0,
            transcendentals=0,
        ),
    )(*values, *before)


def chained(total, state, a_scaled, direction):
    peers = lax.axis_size("seq")
    second_of_pair = (lax.axis_index("seq") & 1) == (1 if direction == 1 else 0)

    def join(first, second):
        return (
            first[0] + second[0],
            jnp.exp2(second[0] * a_scaled) * first[1] + second[1],
        )

    def split(packed):
        return (packed[:, :1], packed[:, 1:])

    def chosen(flag, yes, no):
        return tuple(jnp.where(flag, a, b) for a, b in zip(yes, no))

    own = (total, state)
    mate = split(exchange(jnp.concatenate(own, axis=1), "seq", 1))
    first = chosen(second_of_pair, mate, own)
    pair = join(first, chosen(second_of_pair, own, mate))
    packed = jnp.concatenate(pair, axis=1)
    before = None
    for by in reversed(range(2, peers, 2)):
        got = split(passed_along(packed, "seq", direction * by))
        before = got if before is None else join(before, got)
    return jnp.where(second_of_pair, join(before, first)[1], before[1]), packed


def local(
    tokens,
    gain_one,
    in_weight,
    conv_weight,
    conv_bias,
    x_weight,
    dt_weight,
    dt_bias,
    a_log,
    skip_gain,
    out_weight,
    gain_two,
    ffn_in,
    ffn_down,
    cotangent,
):
    shards = lax.axis_size("shard")
    held, length, _ = tokens.shape
    sequences = held * shards
    own_rows = held * length
    row_count = sequences * length
    channels = conv_bias.shape[0]
    blocks = channels // LANES

    def by_sequence(value):
        return value.reshape(sequences, length, value.shape[-1])

    tokens_own = tokens.reshape(own_rows, D)
    up_own = cotangent.reshape(own_rows, D)
    gains_own = rounded(jnp.concatenate([gain_one, gain_two])).reshape(1, -1)
    gain_rows = jnp.pad(gains_own, ((0, 15), (0, D - gains_own.shape[1])))
    conv_sent = halves_out(in_weight, 2, 0)
    conv_got = [exchange(piece, "shard", k + 1) for k, piece in enumerate(conv_sent)]
    arrived = []
    packed = jnp.concatenate([tokens_own, gain_rows], axis=0)
    packed = gather_rows(tied(packed, conv_sent), arrived).reshape(shards, own_rows + 16, D)
    tokens_all = packed[:, :own_rows].reshape(row_count, D)
    gains = packed[:, own_rows, : gains_own.shape[1]].reshape(shards, 2, -1)
    in_turn = [
        lax.dynamic_index_in_dim(gains, lax.axis_index("shard") ^ k, 0, keepdims=False)
        for k in range(shards)
    ]
    gains = wide(jnp.concatenate(in_turn, axis=1))
    gain_norm, gain_second = gains[0], gains[1]

    conv_other = [exchange(piece, "seq", 1) for piece in conv_got[1:]]
    groups = [(in_weight, 2, 1), (out_weight, 1, 0)]
    weight_conv_in = halves_in(in_weight, 2, 0, conv_got, conv_other)

    conv_taps = wide(rounded(conv_weight))
    bias_conv = wide(rounded(conv_bias))
    weight_x = rounded(x_weight)
    weight_dt = rounded(dt_weight)
    bias_dt = wide(rounded(dt_bias))
    weight_skip = wide(rounded(skip_gain))
    a_matrix = -jnp.exp(wide(rounded(a_log)))
    a_scaled = (a_matrix * log2_e).T.reshape(N, blocks, LANES)

    inputs_all = wide(tokens_all)
    scale_all = lax.rsqrt(jnp.mean(inputs_all * inputs_all, axis=1, keepdims=True) + epsilon)
    normed = rounded(inputs_all * scale_all * gain_norm)
    groups = [(in_weight, 2, 1), (out_weight, 1, 0), (ffn_in, 2, 0), (ffn_in, 2, 1)]
    own, near, far = recut(groups, [arrived, weight_conv_in], normed)
    mixer_far = gathered([piece[:, : 2 * channels] for piece in far])
    ffn_far = gathered([piece[:, 2 * channels :] for piece in far])
    weight_gate_in, weight_out = recut_end(own, near, mixer_far, 2, channels)
    conv_in = by_sequence(rounded(dot_plain(normed, weight_conv_in)))
    gate_mix = dot_plain(normed, weight_gate_in)
    borrowed = passed_along(conv_in[:, length - (K - 1) :], "seq", 1)
    padded = wide(jnp.concatenate([borrowed, conv_in], axis=1))
    conv_out = bias_conv + jnp.zeros((sequences, length, channels), jnp.float32)
    for offset in range(K):
        conv_out = conv_out + conv_taps[offset] * padded[:, offset : offset + length]
    conv_out = conv_out.reshape(row_count, channels)
    signal = rounded(jax.nn.silu(conv_out))
    signal_wide = wide(signal)
    selection = sum_columns(
        lax.dot_general(
            weight_x, signal, (((0,), (1,)), ((), ())), preferred_element_type=jnp.float32
        )
    )
    down_own, down_near, down_parts = recut([(ffn_down, 1, 0)], [selection], selection)
    down_far = gathered(down_parts)
    rank_part = rounded(selection[:R])
    rows = jnp.swapaxes(selection[R:].reshape(2 * N, sequences, length), 0, 1).reshape(
        sequences, 1, 2 * N * length
    )
    pre_rate = dot_first(rank_part, weight_dt) + bias_dt
    rates = by_sequence(jax.nn.softplus(pre_rate))
    signals = by_sequence(signal)
    sizes = (sequences, length, channels)
    end_state, total_rate = scan_call(
        end_kernel,
        "scan_end",
        *sizes,
        [("rows", rows), ("tokens", rates), ("tokens", signals), ("fixed", a_scaled)],
        ["states", "total"],
        ["tokens", "tokens"],
        [near] + far,
    )
    incoming, _ = chained(total_rate, end_state, a_scaled, 1)
    ffn_width = ffn_in.shape[1] // (2 * shards)
    (scan_out,) = scan_call(
        scan_kernel,
        "scan_out",
        *sizes,
        [
            ("rows", rows),
            ("tokens", rates),
            ("tokens", signals),
            ("fixed", a_scaled),
            ("states", incoming),
        ],
        ["tokens"],
        ["fixed", "tokens", "tokens", "tokens"],
        [down_near] + down_parts,
    )
    ffn_offset = 2 * channels // ffn_width
    weight_gate, weight_up = recut_end(own, near, ffn_far, 2, ffn_width, ffn_offset)
    scanned = scan_out.reshape(row_count, channels) + weight_skip * signal_wide
    gate_act = jax.nn.silu(gate_mix)
    gated = rounded(scanned * gate_act)
    inputs = wide(tokens_own)

    def mixed_rows(first, last):
        return dot_last(gated[first * own_rows : last * own_rows], weight_out)

    middle = inputs + scatter_rows(mixed_rows, True, [weight_gate, weight_up])

    scale_two = lax.rsqrt(jnp.mean(middle * middle, axis=1, keepdims=True) + epsilon)
    arrived = []
    normed_two = gather_rows(rounded(middle * scale_two * gain_second), arrived)
    gate_part = dot_plain(normed_two, weight_gate)
    up_all = gather_rows(tied(up_own, arrived), None, gate_part)
    down_far = tied(down_far, gate_part)
    (weight_down,) = recut_end(down_own, down_near, down_far, 1, down_own.shape[1])
    up_part = dot_plain(normed_two, weight_up)
    gate_silu = jax.nn.silu(gate_part)
    activated = rounded(gate_silu * up_part)
    columns = activated.shape[1] // 2
    up_halves = split_columns(up_all, 0)
    down_first = WeightGrad(up_halves, activated[:, :columns])
    down_second = WeightGrad(up_halves, activated[:, columns:])
    up_late = tied(up_all, down_first.ready())
    act_grad = dot_plain(up_late, weight_down)
    gate_grad = rounded(act_grad * up_part * silu_slope(gate_part))
    up_grad = rounded(act_grad * gate_silu)
    gate_late, up_grad_late = tied((gate_grad, up_grad), down_second.ready(gate_grad))

    def normed_two_rows(first, last):
        at = slice(first * own_rows, last * own_rows)
        gate_rows, up_rows = gate_late[at], up_grad_late[at]
        if first == 0:
            gate_rows, up_rows = tied((gate_rows, up_rows), down_first.step())
        return dot_last(gate_rows, weight_gate) + dot_last(up_rows, weight_up)

    normed_two_grad = scatter_rows(normed_two_rows)
    two_halves = split_columns(normed_two, 0)
    gate_first = WeightGrad(two_halves, gate_grad[:, :columns])
    gate_second = WeightGrad(two_halves, gate_grad[:, columns:])
    up_first = WeightGrad(two_halves, up_grad[:, :columns])
    up_second = WeightGrad(two_halves, up_grad[:, columns:])
    gain_two_grad = jnp.sum(normed_two_grad * middle * scale_two, axis=0)
    scaled_two = normed_two_grad * gain_second
    middle_grad = (
        wide(up_own)
        + scale_two * scaled_two
        - middle
        * (scale_two * scale_two * scale_two)
        * jnp.mean(scaled_two * middle, axis=1, keepdims=True)
    )
    mixed_grad = gather_rows(rounded(middle_grad))
    token = tied(middle_grad, [down_first.got, down_second.got])
    steps = [down_second.step(token), down_first.step(token), gate_first.ready(token)]
    mixed_late = tied(mixed_grad, steps)

    gated_grad = dot_plain(mixed_late, weight_out)
    scan_grad = gated_grad * gate_act
    gate_mix_grad = rounded(gated_grad * scanned * silu_slope(gate_mix))
    skip_grad = jnp.sum(scan_grad * signal_wide, axis=0)
    ups = by_sequence(scan_grad)
    token = tied(ups, [gate_first.got, down_first.got])
    steps = [gate_second.ready(token), gate_first.step(token)]
    down_first.end(token)
    (seed,) = scan_call(
        seed_kernel,
        "scan_seed",
        *sizes,
        [("rows", rows), ("tokens", rates), ("tokens", ups), ("fixed", a_scaled)],
        ["states"],
        ["tokens", "tokens"],
        steps,
    )
    returning, first_round = chained(total_rate, seed, a_scaled, -1)
    token = tied(first_round, [gate_second.got, gate_first.got, down_second.got])
    steps = [up_first.ready(token), gate_second.step(token)]
    result_part = dot_last(tied(activated, seed), weight_down)
    token = tied(returning, steps)
    steps = [up_second.ready(token), down_second.step(token)]
    result_parts = scatter_near(tied(result_part, token))
    mixed_halves = split_columns(mixed_grad, 0)
    normed_halves = split_columns(normed, 0)
    out_sum = WeightGrad(mixed_halves, gated)
    in_gate_sum = WeightGrad(normed_halves, gate_mix_grad)
    grads = None
    for part in range(2):
        grads = scan_call(
            grad_kernel,
            "scan_grad",
            *sizes,
            [
                ("rows", rows),
                ("tokens", rates),
                ("tokens", signals),
                ("tokens", ups),
                ("fixed", a_scaled),
                ("states", incoming),
                ("states", returning),
                ("fixed", jnp.zeros_like(a_scaled) if grads is None else grads[3]),
            ],
            ["tokens", "tokens", "rows_grad", "fixed"],
            ["history", "fixed", "tokens", "tokens", "tokens", "tokens", "tokens"],
            steps,
            part=(part, 2),
            before=None if grads is None else grads[:3],
        )
        if part == 0:
            late = [up_first.got, up_second.got, gate_second.got, down_second.got]
            token = tied(grads[3], late + list(result_parts.values()))
            steps = [out_sum.ready(token), in_gate_sum.ready(token), up_first.step(token)]
            steps += [gate_first.step(token), gate_second.step(token), down_second.end(token)]
            result = middle + scatter_far(tied(result_parts, token), own_rows)
    rate_grad, scan_signal_grad, rows_grad, a_grad = grads
    token = tied(a_grad, [up_first.got, gate_first.got, out_sum.got, result])
    steps = [up_second.step(token), out_sum.step(token), up_first.step(token)]
    gate_first.end(token)
    output = rounded(result).reshape(tokens.shape)
    rate_grad = tied(rate_grad, steps)
    rate_grad = rate_grad.reshape(row_count, channels)
    pre_grad = rate_grad * jax.nn.sigmoid(pre_rate)
    pre_grad_low = rounded(pre_grad)
    rank_grad = dot_last(weight_dt, pre_grad_low)
    rows_grad = jnp.swapaxes(jnp.sum(rows_grad, axis=3), 0, 1).reshape(2 * N, row_count)
    selection_grad = rounded(sum_columns(jnp.concatenate([rank_grad, rows_grad], axis=0)))
    token = tied(selection_grad, [gate_second.got, up_first.got])
    steps = [up_second.step(token), gate_second.end(token)]
    selection_grad = tied(selection_grad, steps)
    signal_grad = (
        scan_grad * weight_skip
        + scan_signal_grad.reshape(row_count, channels)
        + lax.dot_general(
            selection_grad, weight_x, (((0,), (1,)), ((), ())), preferred_element_type=jnp.float32
        )
    )
    conv_grad = (signal_grad * silu_slope(conv_out)).reshape(sequences, length, channels)
    padded_grad = jnp.zeros((sequences, length + K - 1, channels), jnp.float32)
    for offset in range(K):
        padded_grad = padded_grad + jnp.pad(
            conv_taps[offset] * conv_grad, ((0, 0), (offset, K - 1 - offset), (0, 0))
        )
    returned = wide(passed_along(low(padded_grad[:, : K - 1]), "seq", -1))
    conv_in_grad = rounded(
        padded_grad[:, K - 1 :] + jnp.pad(returned, ((0, 0), (length - (K - 1), 0), (0, 0)))
    ).reshape(row_count, channels)
    in_conv_sum = WeightGrad(normed_halves, conv_in_grad)
    token = tied(conv_in_grad, [in_conv_sum.ready(), in_gate_sum.got, out_sum.got])
    steps = [in_gate_sum.step(token), out_sum.step(token), up_first.end(token)]
    conv_in_grad = tied(conv_in_grad, steps)
    normed_grad_parts = {}

    def normed_rows(first, last):
        at = slice(first * own_rows, last * own_rows)
        part = dot_last(conv_in_grad[at], weight_conv_in) + dot_last(
            gate_mix_grad[at], weight_gate_in
        )
        normed_grad_parts[first] = jnp.sum(part * inputs_all[at] * scale_all[at], axis=0)
        return part

    normed_grad = scatter_rows(normed_rows)
    gain_one_grad = sum(normed_grad_parts.values())
    token = tied(gain_one_grad, [in_conv_sum.got, in_gate_sum.got])
    steps = [in_conv_sum.step(token), in_gate_sum.step(token), up_second.end(token)]
    gain_one_grad = tied(gain_one_grad, steps)
    last_step = in_conv_sum.step()
    in_conv_sum.end()
    scale_one = scale_all[:own_rows]
    scaled_one = normed_grad * gain_norm
    input_grad = (
        middle_grad
        + scale_one * scaled_one
        - inputs
        * (scale_one * scale_one * scale_one)
        * jnp.mean(scaled_one * inputs, axis=1, keepdims=True)
    )


    conv_weight_grad = jnp.stack(
        [
            jnp.sum(conv_grad * padded[:, offset : offset + length], axis=(0, 1))
            for offset in range(K)
        ],
        axis=1,
    )
    column_sums = jnp.stack(
        [jnp.sum(conv_grad, axis=(0, 1)), jnp.sum(pre_grad, axis=0), skip_grad], axis=1
    )
    a_log_grad = a_grad.reshape(N, channels).T * a_matrix
    dt_weight_grad = lax.dot_general(
        pre_grad_low, rank_part, (((0,), (1,)), ((), ())), preferred_element_type=jnp.float32
    )
    x_weight_grad = lax.dot_general(
        signal, selection_grad, (((0,), (1,)), ((), ())), preferred_element_type=jnp.float32
    )
    small, gain_grads = small_grads(
        jnp.concatenate(
            [dt_weight_grad, x_weight_grad, a_log_grad, conv_weight_grad, column_sums], axis=1
        ),
        jnp.stack([gain_one_grad, gain_two_grad]),
        [last_step],
    )
    at = R + R + 2 * N

    ffn_down_result = rows_of_columns([down_first.done, down_second.done], 1)
    ffn_in_result = rows_of_columns(
        [
            gate_first.done,
            gate_second.done,
            up_first.done,
            up_second.done,
        ],
        2,
    )
    out_result = rows_of_columns([out_sum.end()], 1)
    in_result = rows_of_columns([in_conv_sum.done, in_gate_sum.end()], 2)
    return (
        output,
        rounded(input_grad).reshape(tokens.shape),
        gain_grads[0],
        in_result,
        small[:, at + N : at + N + K].T,
        small[:, at + N + K],
        small[:, R:at],
        small[:, :R].T,
        small[:, at + N + K + 1],
        small[:, at : at + N],
        small[:, at + N + K + 2],
        out_result,
        gain_grads[1],
        ffn_in_result,
        ffn_down_result,
    )


def solution(mesh):
    in_specs = (
        P("shard", "seq", None),
        P("shard"),
        P("shard", None),
        P(None, "shard"),
        P("shard"),
        P("shard", None),
        P(None, "shard"),
        P("shard"),
        P("shard", None),
        P("shard"),
        P("shard", None),
        P("shard"),
        P("shard", None),
        P("shard", None),
        P("shard", "seq", None),
    )
    out_specs = (
        P("shard", "seq", None),
        P("shard", "seq", None),
        P(("seq", "shard")),
        P(("seq", "shard"), None),
        P(None, ("seq", "shard")),
        P(("seq", "shard")),
        P(("seq", "shard"), None),
        P(None, ("seq", "shard")),
        P(("seq", "shard")),
        P(("seq", "shard"), None),
        P(("seq", "shard")),
        P(("seq", "shard"), None),
        P(("seq", "shard")),
        P(("seq", "shard"), None),
        P(("seq", "shard"), None),
    )
    return jax.shard_map(local, mesh=mesh, in_specs=in_specs, out_specs=out_specs, check_vma=False)
```

```python
import functools
import math

import jax
import jax.numpy as jnp
from jax import lax
from jax.experimental import pallas as pl
from jax.experimental.pallas import tpu as pltpu
from jax.sharding import PartitionSpec as P

D = 2048
E = 4096
N = 16
K = 4
R = 128
FF = 8192

LANES = 128
GROUP = 8

epsilon = 1e-05
log2_e = math.log2(math.e)
ln_2 = math.log(2.0)


def silu_slope(value):
    sigma = jax.nn.sigmoid(value)
    return sigma * (1.0 + value * (1.0 - sigma))


def dot_last(left, right):
    return lax.dot_general(
        left, right, (((1,), (1,)), ((), ())), preferred_element_type=jnp.float32
    )


def dot_first(left, right):
    return lax.dot_general(
        left, right, (((0,), (0,)), ((), ())), preferred_element_type=jnp.float32
    )


def dot_plain(left, right):
    return jnp.dot(left, right, preferred_element_type=jnp.float32)


def wide(value):
    return value.astype(jnp.float32)


def low(value):
    return value.astype(jnp.bfloat16)


def rounded(value):
    return lax.reduce_precision(value, 8, 7).astype(jnp.bfloat16)


def exchange(value, axis, mask):
    return lax.ppermute(value, axis, [(i, i ^ mask) for i in range(lax.axis_size(axis))])


def passed_along(value, axis, by):
    peers = lax.axis_size(axis)
    pairs = [(i, i + by) for i in range(peers) if 0 <= i + by < peers]
    return lax.ppermute(value, axis, pairs)


def masks_of(axis):
    size = lax.axis_size(axis)
    return [1 << bit for bit in range(size.bit_length() - 1)]


def gather_rows(value, arrived=None, after=None):
    parts = {0: value}
    for mask in reversed(masks_of("shard")):
        held = sorted(parts)
        got = exchange(jnp.concatenate([parts[k] for k in held], axis=0), "shard", mask)
        if arrived is not None and mask > 1:
            arrived.append(got)
        if after is not None and mask > 1:
            got = tied(got, after)
        for place, k in enumerate(held):
            parts[k ^ mask] = got[place * value.shape[0] : (place + 1) * value.shape[0]]
    return jnp.concatenate([parts[k] for k in sorted(parts)], axis=0)


def exchange_scaled(value, axis, mask):
    largest = jnp.maximum(jnp.max(jnp.abs(value)), 1e-30)
    scale = jnp.broadcast_to(largest, (8, LANES))
    got_scale = exchange(scale, axis, mask)
    scaled = (value * (1.0 / largest)).astype(jnp.float16)
    got = exchange(tied(scaled, got_scale), axis, mask)
    return got.astype(jnp.float32) * got_scale[0, 0]


def scatter_rows(make, scaled=False, after=None):
    shards = lax.axis_size("shard")
    parts = {}
    for pair in reversed(range(0, shards, 2)):
        value = make(pair, pair + 2)
        rows = value.shape[0] // 2
        parts[pair] = value[:rows] + exchange(value[rows:], "shard", 1)
    return scatter_far(parts, rows, scaled, after)


def scatter_near(value):
    shards = lax.axis_size("shard")
    rows = value.shape[0] // shards
    blocks = [value[k * rows : (k + 1) * rows] for k in range(shards)]
    got = exchange(jnp.concatenate(blocks[1::2], axis=0), "shard", 1)
    return {
        2 * k: blocks[2 * k] + got[k * rows : (k + 1) * rows] for k in range(shards // 2)
    }


def scatter_far(parts, rows, scaled=False, after=None):
    parts = dict(parts)
    for mask in masks_of("shard")[1:]:
        sent = [k for k in sorted(parts) if k & mask]
        block = jnp.concatenate([parts[k] for k in sent], axis=0)
        if scaled:
            got = exchange_scaled(block, "shard", mask)
        else:
            got = wide(exchange(low(block), "shard", mask))
        if after is not None:
            got = tied(got, after)
        for place, k in enumerate(sent):
            parts[k ^ mask] = parts[k ^ mask] + got[place * rows : (place + 1) * rows]
            del parts[k]
    return parts[0]


def sum_columns(value):
    shards = lax.axis_size("shard")
    count = value.shape[1] // shards
    for mask in masks_of("shard"):
        got = exchange(value, "shard", mask)
        order = [k ^ mask for k in range(shards)]
        value = value + jnp.concatenate(
            [got[:, k * count : (k + 1) * count] for k in order], axis=1
        )
    return value


def tied(values, after):
    return lax.optimization_barrier((values, after))[0]


def assemble_kernel(plan, count, at_ref, *refs):
    pieces, outs = refs[:count], refs[count : -1 - len(plan)]
    held, sems = refs[-1 - len(plan) : -1], refs[-1]
    fetches, stores = [], []
    for place, (piece, part, target, row, col, shape) in enumerate(plan):
        first = pl.multiple_of(at_ref[row], 16) if row is not None else 0
        left = pl.multiple_of(at_ref[col], LANES) if col is not None else 0
        fetch = pltpu.make_async_copy(
            pieces[piece].at[:, pl.ds(part * shape[1], shape[1])], held[place], sems.at[0, place]
        )
        fetch.start()
        fetches.append(fetch)
        stores.append(
            pltpu.make_async_copy(
                held[place],
                outs[target].at[pl.ds(first, shape[0]), pl.ds(left, shape[1])],
                sems.at[1, place],
            )
        )
    for fetch, store in zip(fetches, stores):
        fetch.wait()
        store.start()
    for store in stores:
        store.wait()


def assemble(pieces, plan, offsets, shapes):
    kind = pieces[0].dtype
    moved = sum(shape[0] * shape[1] * kind.itemsize for shape in shapes)
    any_space = pl.BlockSpec(memory_space=pl.ANY)
    return pl.pallas_call(
        functools.partial(assemble_kernel, plan, len(pieces)),
        name="assemble",
        in_specs=[pl.BlockSpec(memory_space=pltpu.SMEM)] + [any_space] * len(pieces),
        out_specs=[any_space] * len(shapes),
        out_shape=[jax.ShapeDtypeStruct(shape, kind) for shape in shapes],
        scratch_shapes=[pltpu.VMEM(entry[5], kind) for entry in plan]
        + [pltpu.SemaphoreType.DMA((2, len(plan)))],
        compiler_params=pltpu.CompilerParams(vmem_limit_bytes=48 * 1024 * 1024),
        cost_estimate=pl.CostEstimate(flops=0, bytes_accessed=2 * moved, transcendentals=0),
    )(jnp.stack(offsets).astype(jnp.int32), *pieces)


def column_part(weight, groups, group, target, first, count):
    columns = weight.shape[1] // (groups * lax.axis_size("shard"))
    at = (first, (group * lax.axis_size("shard") + target) * columns)
    return low(lax.dynamic_slice(weight, at, (count, columns)))


def halves_out(weight, groups, group):
    shards, mine = lax.axis_size("shard"), lax.axis_index("shard")
    rows = weight.shape[0]
    side = (lax.axis_index("seq") & 1) * (rows // 2)
    sent = [column_part(weight, groups, group, mine ^ 1, 0, rows)]
    return sent + [
        column_part(weight, groups, group, mine ^ k, side, rows // 2) for k in range(2, shards)
    ]


def halves_in(weight, groups, group, got, other):
    shards, mine = lax.axis_size("shard"), lax.axis_index("shard")
    rows = weight.shape[0]
    half = rows // 2
    side = (lax.axis_index("seq") & 1) * half
    own = column_part(weight, groups, group, mine, 0, rows)
    pieces = [own] + got + other
    offsets = [mine * rows, (mine ^ 1) * rows]
    offsets += [(mine ^ k) * rows + side for k in range(2, shards)]
    offsets += [(mine ^ k) * rows + half - side for k in range(2, shards)]
    plan = [(place, 0, 0, place, None, piece.shape) for place, piece in enumerate(pieces)]
    return assemble(pieces, plan, offsets, [(shards * rows, own.shape[1])])[0]


def recut(groups, after, late):
    shards, mine = lax.axis_size("shard"), lax.axis_index("shard")
    peers, range_at = lax.axis_size("seq"), lax.axis_index("seq")
    rows = groups[0][0].shape[0]
    fetched = rows // peers

    def part(target, first, count):
        pieces = [column_part(*group, target, first, count) for group in groups]
        return jnp.concatenate(pieces, axis=1)

    far = [part(mine ^ k, range_at * fetched, fetched) for k in range(2, shards)]
    far = [exchange(piece, "shard", k + 2) for k, piece in enumerate(tied(far, after))]
    far = [tied(piece, late[min(k, len(late) - 1)]) for k, piece in enumerate(far)]
    mine = tied(mine, late[0])
    near = exchange(part(mine ^ 1, 0, rows), "shard", 1)
    return part(mine, 0, rows), near, far


def gathered(pieces):
    return lax.all_gather(jnp.concatenate(pieces, axis=1), "seq", axis=0, tiled=True)


def recut_end(own, near, far, count, width, first=0):
    shards, mine = lax.axis_size("shard"), lax.axis_index("shard")
    rows = own.shape[0]
    plan, offsets = [], []
    for k in range(shards):
        offsets.append((mine ^ k) * rows)
        for group in range(count):
            part = first + group if k < 2 else (k - 2) * count + group
            plan.append((min(k, 2), part, group, k, None, (rows, width)))
    return assemble([own, near, far], plan, offsets, [(shards * rows, width)] * count)


def with_bit(blocks, bit):
    return [b for b in range(blocks) if not b >> bit & 1]


def halve(value, left, bit, sent_type):
    mine = (lax.axis_index("seq") >> bit) & 1
    inner = 1 << sorted(left).index(bit)
    blocks, rows, columns = value.shape
    shaped = value.reshape(blocks // (2 * inner), 2, inner * rows, columns)
    sent = lax.dynamic_index_in_dim(shaped, 1 - mine, 1, keepdims=False).astype(sent_type)
    kept = lax.dynamic_index_in_dim(shaped, mine, 1, keepdims=False)
    left.remove(bit)
    return sent, kept


def split_columns(left, bit):
    peers = lax.axis_size("seq")
    mine = (lax.axis_index("seq") >> bit) & 1
    rows = left.shape[1] // peers

    def half(which):
        pieces = [
            lax.dynamic_slice_in_dim(left, (b + (which << bit)) * rows, rows, axis=1)
            for b in with_bit(peers, bit)
        ]
        return jnp.concatenate(pieces, axis=1)

    return half(1 - mine), half(mine)


class WeightGrad:
    def __init__(self, halves, right):
        self.halves, self.right = halves, right
        self.remaining = [mask.bit_length() - 1 for mask in masks_of("seq")]
        self.rows = 2 * halves[0].shape[1] // lax.axis_size("seq")
        self.total = None

    def ready(self, after=None):
        bit = self.remaining[0]
        if self.total is None:
            if after is not None:
                self.right = tied(self.right, after)
            self.sent = low(dot_first(self.halves[0], self.right))
            self.remaining.remove(bit)
        else:
            self.sent, self.kept = halve(self.total, self.remaining, bit, jnp.bfloat16)
        self.got = exchange(self.sent, "seq", 1 << bit)
        return self.sent

    def add(self, after=None):
        got = self.got if after is None else tied(self.got, after)
        if self.total is None:
            total = dot_first(self.halves[1], self.right) + wide(got)
        else:
            total = self.kept + wide(got).reshape(self.kept.shape)
        self.total = total.reshape(-1, self.rows, self.right.shape[1])

    def step(self, after=None):
        self.add(after)
        return self.ready()

    def end(self, after=None):
        self.add(after)
        while self.remaining:
            self.ready()
            self.add()
        self.done = self.total.reshape(self.total.shape[1:])
        return self.done


def rows_of_columns(blocks, groups):
    shards, mine = lax.axis_size("shard"), lax.axis_index("shard")
    parts = len(blocks) // groups
    rows = blocks[0].shape[0] // shards
    columns = blocks[0].shape[1]

    def part(target):
        return jnp.concatenate(
            [lax.dynamic_slice_in_dim(block, target * rows, rows, axis=0) for block in blocks],
            axis=1,
        )

    pieces = [part(mine)]
    pieces += [wide(exchange(low(part(mine ^ k)), "shard", k)) for k in range(1, shards)]
    offsets = [
        (group * shards + (mine ^ k)) * columns * parts
        for k in range(shards)
        for group in range(groups)
    ]
    shape = (rows, columns * parts)
    plan = [
        (k, group, 0, None, k * groups + group, shape)
        for k in range(shards)
        for group in range(groups)
    ]
    return assemble(pieces, plan, offsets, [(rows, groups * shards * columns * parts)])[0]


def small_grads(value, gains, between):
    peers, shards = lax.axis_size("seq"), lax.axis_size("shard")
    rows = value.shape[0] // peers
    width = value.shape[1]
    packed = jnp.transpose(gains.reshape(2, peers, shards, -1), (1, 0, 3, 2))
    value = jnp.concatenate([value, packed.reshape(value.shape[0], shards)], axis=1)
    total = value.reshape(peers, rows, width + shards)
    left = [mask.bit_length() - 1 for mask in masks_of("seq")]
    for bit in list(left):
        sent, kept = halve(total, left, bit, jnp.float32)
        total = (kept + exchange(sent, "seq", 1 << bit)).reshape(-1, rows, width + shards)
        if between:
            total = tied(total, between.pop(0))
    total = total.reshape(rows, width + shards)
    gain_sum = total[:, width:]
    for mask in masks_of("shard"):
        gain_sum = gain_sum + exchange(gain_sum, "shard", mask)
    gain_sum = lax.dynamic_index_in_dim(gain_sum, lax.axis_index("shard"), 1, keepdims=False)
    pairs = [(s * shards + h, h * peers + s) for s in range(peers) for h in range(shards)]
    return lax.ppermute(total[:, :width], ("seq", "shard"), pairs), gain_sum.reshape(2, -1)


def spread(source, target, length):
    for c in range(source.shape[-1] // LANES):
        target[pl.ds(c * length, length), :] = wide(source[0, :, c * LANES : (c + 1) * LANES])


def collect(source, target, length):
    for c in range(target.shape[-1] // LANES):
        target[0, :, c * LANES : (c + 1) * LANES] = source[pl.ds(c * length, length), :]


def token_rows(ref, token, blocks, length):
    return ref[pl.ds(token, blocks, stride=length), :]


def sum_blocks(values):
    blocks = values[0].shape[0]
    if blocks != GROUP:
        return jnp.concatenate([jnp.sum(v, axis=0, keepdims=True) for v in values], axis=0)
    row = lax.broadcasted_iota(jnp.int32, (GROUP, LANES), 0)
    upper = row < 4
    level = [
        jnp.where(upper, values[j], values[j + 4])
        + pltpu.roll(jnp.where(upper, values[j + 4], values[j]), 4, 0)
        for j in range(4)
    ]
    for step in (2, 1):
        first = (row & step) == 0
        level = [
            jnp.where(
                first,
                level[j] + pltpu.roll(level[j], GROUP - step, 0),
                level[j + step] + pltpu.roll(level[j + step], step, 0),
            )
            for j in range(step)
        ]
    return level[0]


def end_kernel(length, blocks, rows_ref, rate_ref, signal_ref, a_ref, state_ref, total_ref, rate, signal):
    spread(rate_ref, rate, length)
    spread(signal_ref, signal, length)
    state_ref[...] = jnp.zeros_like(state_ref)

    def group(i, total):
        start = i * GROUP
        rates = [token_rows(rate, start + j, blocks, length) for j in range(GROUP)]
        drives = [
            rates[j] * token_rows(signal, start + j, blocks, length) for j in range(GROUP)
        ]
        for n in range(N):
            state, a = state_ref[0, n], a_ref[n]
            for j in range(GROUP):
                state = jnp.exp2(rates[j] * a) * state + drives[j] * rows_ref[0, 0, n * length + start + j]
            state_ref[0, n] = state
        for j in range(GROUP):
            total = total + rates[j]
        return total

    total_ref[0, 0] = lax.fori_loop(
        0, length // GROUP, group, jnp.zeros((blocks, LANES), jnp.float32)
    )


def scan_kernel(
    length, blocks, rows_ref, rate_ref, signal_ref, a_ref, in_ref, out_ref, state_ref, rate, signal, out
):
    spread(rate_ref, rate, length)
    spread(signal_ref, signal, length)
    state_ref[...] = in_ref[0]

    def group(i, carry):
        start = i * GROUP
        rates = [token_rows(rate, start + j, blocks, length) for j in range(GROUP)]
        drives = [
            rates[j] * token_rows(signal, start + j, blocks, length) for j in range(GROUP)
        ]
        outs = [None] * GROUP
        for n in range(N):
            state, a = state_ref[n], a_ref[n]
            for j in range(GROUP):
                state = jnp.exp2(rates[j] * a) * state + drives[j] * rows_ref[0, 0, n * length + start + j]
                term = state * rows_ref[0, 0, (N + n) * length + start + j]
                outs[j] = term if outs[j] is None else outs[j] + term
            state_ref[n] = state
        for j in range(GROUP):
            out[pl.ds(start + j, blocks, stride=length), :] = outs[j]
        return carry

    lax.fori_loop(0, length // GROUP, group, 0)
    collect(out, out_ref, length)


def seed_kernel(length, blocks, rows_ref, rate_ref, up_ref, a_ref, seed_ref, rate, up):
    spread(rate_ref, rate, length)
    spread(up_ref, up, length)
    seed_ref[...] = jnp.zeros_like(seed_ref)

    def group(i, carry):
        start = length - GROUP - i * GROUP
        rates = [token_rows(rate, start + j, blocks, length) for j in range(GROUP)]
        ups = [token_rows(up, start + j, blocks, length) for j in range(GROUP)]
        for n in range(N):
            back, a = seed_ref[0, n], a_ref[n]
            for j in reversed(range(GROUP)):
                back = jnp.exp2(rates[j] * a) * (
                    back + ups[j] * rows_ref[0, 0, (N + n) * length + start + j]
                )
            seed_ref[0, n] = back
        return carry

    lax.fori_loop(0, length // GROUP, group, 0)


def grad_kernel(
    length,
    blocks,
    rows_ref,
    rate_ref,
    signal_ref,
    up_ref,
    a_ref,
    in_ref,
    back_ref,
    a_before_ref,
    rate_grad_ref,
    signal_grad_ref,
    rows_grad_ref,
    a_grad_ref,
    states,
    back_state,
    rate,
    signal,
    up,
    rate_grad,
    signal_grad,
):
    spread(rate_ref, rate, length)
    spread(signal_ref, signal, length)
    spread(up_ref, up, length)
    for n in range(N):
        states[n, 0] = in_ref[0, n]
    back_state[...] = back_ref[0]

    @pl.when(pl.program_id(0) == 0)
    def _():
        a_grad_ref[...] = a_before_ref[...]

    def forward(i, carry):
        start = i * GROUP
        rates = [token_rows(rate, start + j, blocks, length) for j in range(GROUP)]
        drives = [
            rates[j] * token_rows(signal, start + j, blocks, length) for j in range(GROUP)
        ]
        for n in range(N):
            state, a = states[n, start], a_ref[n]
            for j in range(GROUP):
                state = jnp.exp2(rates[j] * a) * state + drives[j] * rows_ref[0, 0, n * length + start + j]
                states[n, start + j + 1] = state
        return carry

    lax.fori_loop(0, length // GROUP, forward, 0)

    def backward(i, carry):
        start = length - GROUP - i * GROUP
        rates = [token_rows(rate, start + j, blocks, length) for j in range(GROUP)]
        signals = [token_rows(signal, start + j, blocks, length) for j in range(GROUP)]
        ups = [token_rows(up, start + j, blocks, length) for j in range(GROUP)]
        through = [None] * GROUP
        slope = [None] * GROUP
        for n in range(N):
            back, a = back_state[n], a_ref[n]
            a_sum = None
            to_b = [None] * GROUP
            to_c = [None] * GROUP
            for j in reversed(range(GROUP)):
                b = rows_ref[0, 0, n * length + start + j]
                c = rows_ref[0, 0, (N + n) * length + start + j]
                here = back + ups[j] * c
                back = jnp.exp2(rates[j] * a) * here
                moved = back * states[n, start + j]
                a_term = moved * rates[j]
                a_sum = a_term if a_sum is None else a_sum + a_term
                b_term, a_slope = here * b, moved * a
                through[j] = b_term if through[j] is None else through[j] + b_term
                slope[j] = a_slope if slope[j] is None else slope[j] + a_slope
                to_b[j] = here * (rates[j] * signals[j])
                to_c[j] = ups[j] * states[n, start + j + 1]
            back_state[n] = back
            a_grad_ref[n] = a_grad_ref[n] + a_sum
            at = pl.ds(pl.multiple_of(start, GROUP), GROUP)
            rows_grad_ref[0, n, at, :] = sum_blocks(to_b)
            rows_grad_ref[0, N + n, at, :] = sum_blocks(to_c)
        for j in range(GROUP):
            rows = pl.ds(start + j, blocks, stride=length)
            rate_grad[rows, :] = through[j] * signals[j] + slope[j] * ln_2
            signal_grad[rows, :] = through[j] * rates[j]
        return carry

    lax.fori_loop(0, length // GROUP, backward, 0)
    collect(rate_grad, rate_grad_ref, length)
    collect(signal_grad, signal_grad_ref, length)


def scan_call(kernel, name, sequences, length, channels, inputs, outputs, scratch, after=(), part=(0, 1), before=None):
    blocks = channels // LANES
    count = sequences // part[1]
    at = part[0] * count
    before = [] if before is None else list(before)
    kinds = {
        "rows": ((1, 1, 2 * N * length), lambda s: (at + s, 0, 0)),
        "tokens": ((1, length, channels), lambda s: (at + s, 0, 0)),
        "states": ((1, N, blocks, LANES), lambda s: (at + s, 0, 0, 0)),
        "total": ((1, 1, blocks, LANES), lambda s: (at + s, 0, 0, 0)),
        "fixed": ((N, blocks, LANES), lambda s: (0, 0, 0)),
        "rows_grad": ((1, 2 * N, length, LANES), lambda s: (at + s, 0, 0, 0)),
    }

    def spec(kind):
        shape, index = kinds[kind]
        if kind == "rows":
            return pl.BlockSpec(shape, index, memory_space=pltpu.SMEM)
        return pl.BlockSpec(shape, index)

    def whole(kind):
        shape = kinds[kind][0]
        if kind != "fixed":
            shape = (sequences,) + shape[1:]
        return jax.ShapeDtypeStruct(shape, jnp.float32)

    def space(kind):
        if kind == "tokens":
            return pltpu.VMEM((blocks * length, LANES), jnp.float32)
        if kind == "history":
            return pltpu.VMEM((N, length + 1, blocks, LANES), jnp.float32)
        return pltpu.VMEM((N, blocks, LANES), jnp.float32)

    values = [value for _, value in inputs]
    values = tied(values, list(after))
    def body(*refs):
        kernel(length, blocks, *refs[: len(inputs)], *refs[len(inputs) + len(before) :])

    return pl.pallas_call(
        body,
        name=name,
        grid=(count,),
        in_specs=[spec(kind) for kind, _ in inputs]
        + [pl.BlockSpec(memory_space=pl.ANY)] * len(before),
        input_output_aliases={len(inputs) + i: i for i in range(len(before))},
        out_specs=[spec(kind) for kind in outputs],
        out_shape=[whole(kind) for kind in outputs],
        scratch_shapes=[space(kind) for kind in scratch],
        compiler_params=pltpu.CompilerParams(vmem_limit_bytes=56 * 1024 * 1024),
        cost_estimate=pl.CostEstimate(
            flops=0,
            bytes_accessed=0,
            transcendentals=0,
        ),
    )(*values, *before)


def chained(total, state, a_scaled, direction):
    peers = lax.axis_size("seq")
    second_of_pair = (lax.axis_index("seq") & 1) == (1 if direction == 1 else 0)

    def join(first, second):
        return (
            first[0] + second[0],
            jnp.exp2(second[0] * a_scaled) * first[1] + second[1],
        )

    def split(packed):
        return (packed[:, :1], packed[:, 1:])

    def chosen(flag, yes, no):
        return tuple(jnp.where(flag, a, b) for a, b in zip(yes, no))

    own = (total, state)
    mate = split(exchange(jnp.concatenate(own, axis=1), "seq", 1))
    first = chosen(second_of_pair, mate, own)
    pair = join(first, chosen(second_of_pair, own, mate))
    packed = jnp.concatenate(pair, axis=1)
    before = None
    for by in reversed(range(2, peers, 2)):
        got = split(passed_along(packed, "seq", direction * by))
        before = got if before is None else join(before, got)
    return jnp.where(second_of_pair, join(before, first)[1], before[1]), packed


def local(
    tokens,
    gain_one,
    in_weight,
    conv_weight,
    conv_bias,
    x_weight,
    dt_weight,
    dt_bias,
    a_log,
    skip_gain,
    out_weight,
    gain_two,
    ffn_in,
    ffn_down,
    cotangent,
):
    shards = lax.axis_size("shard")
    held, length, _ = tokens.shape
    sequences = held * shards
    own_rows = held * length
    row_count = sequences * length
    channels = conv_bias.shape[0]
    blocks = channels // LANES

    def by_sequence(value):
        return value.reshape(sequences, length, value.shape[-1])

    tokens_own = tokens.reshape(own_rows, D)
    up_own = cotangent.reshape(own_rows, D)
    gains_own = rounded(jnp.concatenate([gain_one, gain_two])).reshape(1, -1)
    gain_rows = jnp.pad(gains_own, ((0, 15), (0, D - gains_own.shape[1])))
    conv_sent = halves_out(in_weight, 2, 0)
    conv_got = [exchange(piece, "shard", k + 1) for k, piece in enumerate(conv_sent)]
    arrived = []
    packed = jnp.concatenate([tokens_own, gain_rows], axis=0)
    packed = gather_rows(tied(packed, conv_sent), arrived).reshape(shards, own_rows + 16, D)
    tokens_all = packed[:, :own_rows].reshape(row_count, D)
    gains = packed[:, own_rows, : gains_own.shape[1]].reshape(shards, 2, -1)
    in_turn = [
        lax.dynamic_index_in_dim(gains, lax.axis_index("shard") ^ k, 0, keepdims=False)
        for k in range(shards)
    ]
    gains = wide(jnp.concatenate(in_turn, axis=1))
    gain_norm, gain_second = gains[0], gains[1]

    conv_other = [exchange(piece, "seq", 1) for piece in conv_got[1:]]
    groups = [(in_weight, 2, 1), (out_weight, 1, 0)]
    weight_conv_in = halves_in(in_weight, 2, 0, conv_got, conv_other)

    conv_taps = wide(rounded(conv_weight))
    bias_conv = wide(rounded(conv_bias))
    weight_x = rounded(x_weight)
    weight_dt = rounded(dt_weight)
    bias_dt = wide(rounded(dt_bias))
    weight_skip = wide(rounded(skip_gain))
    a_matrix = -jnp.exp(wide(rounded(a_log)))
    a_scaled = (a_matrix * log2_e).T.reshape(N, blocks, LANES)

    inputs_all = wide(tokens_all)
    scale_all = lax.rsqrt(jnp.mean(inputs_all * inputs_all, axis=1, keepdims=True) + epsilon)
    normed = rounded(inputs_all * scale_all * gain_norm)
    conv_in = by_sequence(rounded(dot_plain(normed, weight_conv_in)))
    borrowed = passed_along(conv_in[:, length - (K - 1) :], "seq", 1)
    padded = wide(jnp.concatenate([borrowed, conv_in], axis=1))
    conv_out = bias_conv + jnp.zeros((sequences, length, channels), jnp.float32)
    for offset in range(K):
        conv_out = conv_out + conv_taps[offset] * padded[:, offset : offset + length]
    conv_out = conv_out.reshape(row_count, channels)
    signal = rounded(jax.nn.silu(conv_out))
    signal_wide = wide(signal)
    groups = [(in_weight, 2, 1), (out_weight, 1, 0), (ffn_in, 2, 0), (ffn_in, 2, 1)]
    own, near, far = recut(groups, [arrived, conv_got], [conv_in, signal])
    mixer_far = gathered([piece[:, : 2 * channels] for piece in far])
    ffn_far = gathered([piece[:, 2 * channels :] for piece in far])
    weight_gate_in, weight_out = recut_end(own, near, mixer_far, 2, channels)
    gate_mix = dot_plain(normed, weight_gate_in)
    selection = sum_columns(
        lax.dot_general(
            weight_x, signal, (((0,), (1,)), ((), ())), preferred_element_type=jnp.float32
        )
    )
    down_own, down_near, down_parts = recut([(ffn_down, 1, 0)], [selection], [selection])
    down_far = gathered(down_parts)
    rank_part = rounded(selection[:R])
    rows = jnp.swapaxes(selection[R:].reshape(2 * N, sequences, length), 0, 1).reshape(
        sequences, 1, 2 * N * length
    )
    pre_rate = dot_first(rank_part, weight_dt) + bias_dt
    rates = by_sequence(jax.nn.softplus(pre_rate))
    signals = by_sequence(signal)
    sizes = (sequences, length, channels)
    end_state, total_rate = scan_call(
        end_kernel,
        "scan_end",
        *sizes,
        [("rows", rows), ("tokens", rates), ("tokens", signals), ("fixed", a_scaled)],
        ["states", "total"],
        ["tokens", "tokens"],
        [near] + far,
    )
    incoming, _ = chained(total_rate, end_state, a_scaled, 1)
    ffn_width = ffn_in.shape[1] // (2 * shards)
    (scan_out,) = scan_call(
        scan_kernel,
        "scan_out",
        *sizes,
        [
            ("rows", rows),
            ("tokens", rates),
            ("tokens", signals),
            ("fixed", a_scaled),
            ("states", incoming),
        ],
        ["tokens"],
        ["fixed", "tokens", "tokens", "tokens"],
        [down_near] + down_parts,
    )
    ffn_offset = 2 * channels // ffn_width
    weight_gate, weight_up = recut_end(own, near, ffn_far, 2, ffn_width, ffn_offset)
    scanned = scan_out.reshape(row_count, channels) + weight_skip * signal_wide
    gate_act = jax.nn.silu(gate_mix)
    gated = rounded(scanned * gate_act)
    inputs = wide(tokens_own)

    def mixed_rows(first, last):
        return dot_last(gated[first * own_rows : last * own_rows], weight_out)

    middle = inputs + scatter_rows(mixed_rows, True, [weight_gate, weight_up])

    scale_two = lax.rsqrt(jnp.mean(middle * middle, axis=1, keepdims=True) + epsilon)
    arrived = []
    normed_two = gather_rows(rounded(middle * scale_two * gain_second), arrived)
    gate_part = dot_plain(normed_two, weight_gate)
    up_all = gather_rows(tied(up_own, arrived), None, gate_part)
    down_far = tied(down_far, gate_part)
    (weight_down,) = recut_end(down_own, down_near, down_far, 1, down_own.shape[1])
    up_part = dot_plain(normed_two, weight_up)
    gate_silu = jax.nn.silu(gate_part)
    activated = rounded(gate_silu * up_part)
    columns = activated.shape[1] // 2
    up_halves = split_columns(up_all, 0)
    down_first = WeightGrad(up_halves, activated[:, :columns])
    down_second = WeightGrad(up_halves, activated[:, columns:])
    up_late = tied(up_all, down_first.ready())
    act_grad = dot_plain(up_late, weight_down)
    gate_grad = rounded(act_grad * up_part * silu_slope(gate_part))
    up_grad = rounded(act_grad * gate_silu)
    gate_late, up_grad_late = tied((gate_grad, up_grad), down_second.ready(gate_grad))

    def normed_two_rows(first, last):
        at = slice(first * own_rows, last * own_rows)
        gate_rows, up_rows = gate_late[at], up_grad_late[at]
        if first == 0:
            gate_rows, up_rows = tied((gate_rows, up_rows), down_first.step())
        return dot_last(gate_rows, weight_gate) + dot_last(up_rows, weight_up)

    normed_two_grad = scatter_rows(normed_two_rows)
    two_halves = split_columns(normed_two, 0)
    gate_first = WeightGrad(two_halves, gate_grad[:, :columns])
    gate_second = WeightGrad(two_halves, gate_grad[:, columns:])
    up_first = WeightGrad(two_halves, up_grad[:, :columns])
    up_second = WeightGrad(two_halves, up_grad[:, columns:])
    gain_two_grad = jnp.sum(normed_two_grad * middle * scale_two, axis=0)
    scaled_two = normed_two_grad * gain_second
    middle_grad = (
        wide(up_own)
        + scale_two * scaled_two
        - middle
        * (scale_two * scale_two * scale_two)
        * jnp.mean(scaled_two * middle, axis=1, keepdims=True)
    )
    mixed_grad = gather_rows(rounded(middle_grad))
    token = tied(middle_grad, [down_first.got, down_second.got])
    steps = [down_second.step(token), down_first.step(token), gate_first.ready(token)]
    mixed_late = tied(mixed_grad, steps)

    gated_grad = dot_plain(mixed_late, weight_out)
    scan_grad = gated_grad * gate_act
    gate_mix_grad = rounded(gated_grad * scanned * silu_slope(gate_mix))
    skip_grad = jnp.sum(scan_grad * signal_wide, axis=0)
    ups = by_sequence(scan_grad)
    token = tied(ups, [gate_first.got, down_first.got])
    steps = [gate_first.step(token)]
    down_first.end(token)
    (seed,) = scan_call(
        seed_kernel,
        "scan_seed",
        *sizes,
        [("rows", rows), ("tokens", rates), ("tokens", ups), ("fixed", a_scaled)],
        ["states"],
        ["tokens", "tokens"],
        steps,
    )
    returning, first_round = chained(total_rate, seed, a_scaled, -1)
    token = tied(first_round, [gate_first.got, down_second.got])
    steps = [gate_second.ready(token), gate_first.step(token)]
    result_part = dot_last(tied(activated, seed), weight_down)
    token = tied(returning, steps + [gate_second.got])
    steps = [up_first.ready(token), up_second.ready(token), gate_second.step(token)]
    result_parts = scatter_near(tied(result_part, token))
    mixed_halves = split_columns(mixed_grad, 0)
    normed_halves = split_columns(normed, 0)
    out_sum = WeightGrad(mixed_halves, gated)
    in_gate_sum = WeightGrad(normed_halves, gate_mix_grad)
    grads = None
    for part in range(2):
        grads = scan_call(
            grad_kernel,
            "scan_grad",
            *sizes,
            [
                ("rows", rows),
                ("tokens", rates),
                ("tokens", signals),
                ("tokens", ups),
                ("fixed", a_scaled),
                ("states", incoming),
                ("states", returning),
                ("fixed", jnp.zeros_like(a_scaled) if grads is None else grads[3]),
            ],
            ["tokens", "tokens", "rows_grad", "fixed"],
            ["history", "fixed", "tokens", "tokens", "tokens", "tokens", "tokens"],
            steps,
            part=(part, 2),
            before=None if grads is None else grads[:3],
        )
        if part == 0:
            late = [up_first.got, up_second.got, gate_second.got, gate_first.got]
            token = tied(grads[3], late + list(result_parts.values()))
            steps = [out_sum.ready(token), in_gate_sum.ready(token), up_first.step(token)]
            steps += [down_second.step(token), gate_second.step(token), gate_first.end(token)]
            result = middle + scatter_far(tied(result_parts, token), own_rows)
    rate_grad, scan_signal_grad, rows_grad, a_grad = grads
    token = tied(a_grad, [up_first.got, down_second.got, out_sum.got, result])
    steps = [up_second.step(token), out_sum.step(token), up_first.step(token)]
    down_second.end(token)
    output = rounded(result).reshape(tokens.shape)
    rate_grad = tied(rate_grad, steps)
    rate_grad = rate_grad.reshape(row_count, channels)
    pre_grad = rate_grad * jax.nn.sigmoid(pre_rate)
    pre_grad_low = rounded(pre_grad)
    rank_grad = dot_last(weight_dt, pre_grad_low)
    rows_grad = jnp.swapaxes(jnp.sum(rows_grad, axis=3), 0, 1).reshape(2 * N, row_count)
    selection_grad = rounded(sum_columns(jnp.concatenate([rank_grad, rows_grad], axis=0)))
    token = tied(selection_grad, [gate_second.got, up_first.got])
    steps = [up_second.step(token), gate_second.end(token)]
    selection_grad = tied(selection_grad, steps)
    signal_grad = (
        scan_grad * weight_skip
        + scan_signal_grad.reshape(row_count, channels)
        + lax.dot_general(
            selection_grad, weight_x, (((0,), (1,)), ((), ())), preferred_element_type=jnp.float32
        )
    )
    conv_grad = (signal_grad * silu_slope(conv_out)).reshape(sequences, length, channels)
    padded_grad = jnp.zeros((sequences, length + K - 1, channels), jnp.float32)
    for offset in range(K):
        padded_grad = padded_grad + jnp.pad(
            conv_taps[offset] * conv_grad, ((0, 0), (offset, K - 1 - offset), (0, 0))
        )
    returned = wide(passed_along(low(padded_grad[:, : K - 1]), "seq", -1))
    conv_in_grad = rounded(
        padded_grad[:, K - 1 :] + jnp.pad(returned, ((0, 0), (length - (K - 1), 0), (0, 0)))
    ).reshape(row_count, channels)
    in_conv_sum = WeightGrad(normed_halves, conv_in_grad)
    token = tied(conv_in_grad, [in_conv_sum.ready(), in_gate_sum.got, out_sum.got])
    steps = [in_gate_sum.step(token), out_sum.step(token), up_first.end(token)]
    conv_in_grad = tied(conv_in_grad, steps)
    normed_grad_parts = {}

    def normed_rows(first, last):
        at = slice(first * own_rows, last * own_rows)
        part = dot_last(conv_in_grad[at], weight_conv_in) + dot_last(
            gate_mix_grad[at], weight_gate_in
        )
        normed_grad_parts[first] = jnp.sum(part * inputs_all[at] * scale_all[at], axis=0)
        return part

    normed_grad = scatter_rows(normed_rows)
    gain_one_grad = sum(normed_grad_parts.values())
    token = tied(gain_one_grad, [in_conv_sum.got, in_gate_sum.got])
    steps = [in_conv_sum.step(token), in_gate_sum.step(token), up_second.end(token)]
    gain_one_grad = tied(gain_one_grad, steps)
    last_step = in_conv_sum.step()
    in_conv_sum.end()
    scale_one = scale_all[:own_rows]
    scaled_one = normed_grad * gain_norm
    input_grad = (
        middle_grad
        + scale_one * scaled_one
        - inputs
        * (scale_one * scale_one * scale_one)
        * jnp.mean(scaled_one * inputs, axis=1, keepdims=True)
    )


    conv_weight_grad = jnp.stack(
        [
            jnp.sum(conv_grad * padded[:, offset : offset + length], axis=(0, 1))
            for offset in range(K)
        ],
        axis=1,
    )
    column_sums = jnp.stack(
        [jnp.sum(conv_grad, axis=(0, 1)), jnp.sum(pre_grad, axis=0), skip_grad], axis=1
    )
    a_log_grad = a_grad.reshape(N, channels).T * a_matrix
    dt_weight_grad = lax.dot_general(
        pre_grad_low, rank_part, (((0,), (1,)), ((), ())), preferred_element_type=jnp.float32
    )
    x_weight_grad = lax.dot_general(
        signal, selection_grad, (((0,), (1,)), ((), ())), preferred_element_type=jnp.float32
    )
    small, gain_grads = small_grads(
        jnp.concatenate(
            [dt_weight_grad, x_weight_grad, a_log_grad, conv_weight_grad, column_sums], axis=1
        ),
        jnp.stack([gain_one_grad, gain_two_grad]),
        [last_step],
    )
    at = R + R + 2 * N

    ffn_down_result = rows_of_columns([down_first.done, down_second.done], 1)
    ffn_in_result = rows_of_columns(
        [
            gate_first.done,
            gate_second.done,
            up_first.done,
            up_second.done,
        ],
        2,
    )
    out_result = rows_of_columns([out_sum.end()], 1)
    in_result = rows_of_columns([in_conv_sum.done, in_gate_sum.end()], 2)
    return (
        output,
        rounded(input_grad).reshape(tokens.shape),
        gain_grads[0],
        in_result,
        small[:, at + N : at + N + K].T,
        small[:, at + N + K],
        small[:, R:at],
        small[:, :R].T,
        small[:, at + N + K + 1],
        small[:, at : at + N],
        small[:, at + N + K + 2],
        out_result,
        gain_grads[1],
        ffn_in_result,
        ffn_down_result,
    )


def solution(mesh):
    in_specs = (
        P("shard", "seq", None),
        P("shard"),
        P("shard", None),
        P(None, "shard"),
        P("shard"),
        P("shard", None),
        P(None, "shard"),
        P("shard"),
        P("shard", None),
        P("shard"),
        P("shard", None),
        P("shard"),
        P("shard", None),
        P("shard", None),
        P("shard", "seq", None),
    )
    out_specs = (
        P("shard", "seq", None),
        P("shard", "seq", None),
        P(("seq", "shard")),
        P(("seq", "shard"), None),
        P(None, ("seq", "shard")),
        P(("seq", "shard")),
        P(("seq", "shard"), None),
        P(None, ("seq", "shard")),
        P(("seq", "shard")),
        P(("seq", "shard"), None),
        P(("seq", "shard")),
        P(("seq", "shard"), None),
        P(("seq", "shard")),
        P(("seq", "shard"), None),
        P(("seq", "shard"), None),
    )
    return jax.shard_map(local, mesh=mesh, in_specs=in_specs, out_specs=out_specs, check_vma=False)
```
